512 devices in a mesh: ctx: 8 (over y, core), exp: 16 (over z), tp: 4 (over x).
Axes of the slice: x: 4, y: 4, z: 16, core: 2. Of those that a mesh axis runs over, the one named last changes fastest.
Arguments:
- mixer_input: bfloat16 [1024, 8192], P('ctx', ('exp', 'tp')), may hold values from -6 to 6
- step_sizes: float32 [1024, 8192], P('ctx', ('exp', 'tp')), may hold values from 0.015 to 0.5
- decay_rates: float32 [16, 8192], P(None, ('exp', 'tp')), as said below
- input_proj: float32 [16, 1024], P(None, 'ctx'), may hold values from -3 to 3
- output_proj: float32 [16, 1024], P(None, 'ctx'), may hold values from -1.5 to 1.5
- skip_gain: float32 [8192], P(('exp', 'tp')), may hold values from 0.5 to 1.5
- doc_starts: int32 [1024], P('ctx'), may hold values from 0 to 1, as said below
- ssm_grad: bfloat16 [1024, 8192], P('ctx', ('exp', 'tp')), may hold values from -6 to 6
- mixer_in_weight: bfloat16 [8192, 4096], P(('exp', 'tp'), 'ctx'), may hold values from -0.0078125 to 0.0078125
- residual_grad: bfloat16 [1024, 4096], P(('ctx', 'exp')), may hold values from -0.59765625 to 0.59765625
- expert_index_pairs: int32 [1024, 2], P(('ctx', 'exp')), may hold values from 0 to 15, all different within a row; in each aligned block of 8 rows (0 to 7, 8 to 15, ...) at most 3 rows name the same one
- route_probs: float32 [1024, 2], P(('ctx', 'exp')), may hold values from 0.05 to 0.6
- hidden_saved: bfloat16 [16, 7168, 384], P('exp', ('ctx', 'tp')), may hold values from -3 to 3
- down_weight: bfloat16 [16, 7168, 4096], P('exp', ('ctx', 'tp')), may hold values from -0.0625 to 0.0625
Outputs:
- ssm_input_grad: bfloat16 [1024, 8192], P('ctx', ('exp', 'tp'))
- step_grad: float32 [1024, 8192], P('ctx', ('exp', 'tp'))
- input_proj_grad: float32 [16, 1024], P(None, 'ctx')
- output_proj_grad: float32 [16, 1024], P(None, 'ctx')
- decay_grad: float32 [16, 8192], P(None, ('exp', 'tp'))
- skip_grad: float32 [8192], P(('exp', 'tp'))
- slot_hidden_gradient: bfloat16 [16, 7168, 384], P('exp', ('ctx', 'tp'))
- down_grad: bfloat16 [16, 7168, 4096], P('exp', ('ctx', 'tp'))
- prob_grad: float32 [1024, 2], P(('ctx', 'exp'))
The draws below stay inside these ranges and needn't reach their ends.
Inputs may be any that keep to these rules, and one draw needn't show every extreme that they name: `expert_index_pairs`: in the rows of one device (each aligned block of 8 rows) no expert is named by more than 3 rows; the two experts of a row differ. `doc_starts`: 1 marks the first token of a document: the first token of the window and exactly one more token in each half of the window. `decay_rates`: negative.
All inputs are finite; a program needn't handle non-finite values.
Results may differ from the reference program's by a relative error of at most 0.033.
Values may be sent and summed in bfloat16 or wider, within the bound.
A program may use at most 64 MiB of HBM per device.

```python
import math
import jax
import jax.numpy as jnp
import numpy as np
from jax import lax

D = 4096
FF = 7168
DI = 8192
NS = 16
TOK_DEV = 8
EXPERTS = 16
SPAN_ELEMENTS = 1024
SOURCES = 128
CAP = 3
SLOTS = 384


def draw_step_sizes(key, part):
    key = jax.random.fold_in(key, 11)
    first_key, second_key, third_key = jax.random.split(key, 3)
    starting_shift_amount = jnp.exp(jax.random.uniform(first_key, (1, DI), jnp.float32, jnp.log(0.03), jnp.log(0.08)))
    approximate_guess = jnp.exp(jax.random.uniform(second_key, (SPAN_ELEMENTS, DI), jnp.float32, jnp.log(0.5), jnp.log(1.5)))
    capacity_locations = jax.random.randint(third_key, (3,), 1, SPAN_ELEMENTS)
    transfer_batch = jnp.any(jnp.arange(SPAN_ELEMENTS)[:, None] == capacity_locations[None, :], axis=1)
    return jnp.where(transfer_batch[:, None], 0.5, starting_shift_amount * approximate_guess).astype(jnp.float32)


def draw_decay_rates(key, part):
    key = jax.random.fold_in(key, 12)
    first_key, second_key, third_key = jax.random.split(key, 3)
    share = 0.5
    slow_mask = jax.random.uniform(first_key, (1, DI), jnp.float32) < share
    slow_rates = jnp.exp(jax.random.uniform(second_key, (NS, DI), jnp.float32, jnp.log(4.0 / SPAN_ELEMENTS), jnp.log(20.0 / SPAN_ELEMENTS)))
    fast_rates = jnp.exp(jax.random.uniform(third_key, (NS, DI), jnp.float32, jnp.log(0.25), jnp.log(1.0)))
    return (-jnp.where(slow_mask, slow_rates, fast_rates)).astype(jnp.float32)


def draw_doc_starts(key, part):
    key = jax.random.fold_in(key, 13)
    first_key, second_key = jax.random.split(key, 2)
    first_start = jax.random.randint(first_key, (), 1, SPAN_ELEMENTS // 2)
    second_start = jax.random.randint(second_key, (), SPAN_ELEMENTS // 2, SPAN_ELEMENTS)
    capacity_locations = jnp.arange(SPAN_ELEMENTS)
    return ((capacity_locations == 0) | (capacity_locations == first_start) | (capacity_locations == second_start)).astype(jnp.int32)


def steps_of(key, shape, shards, smallest, high):
    def one(axis_at, shards_of):
        heights = jax.random.uniform(jax.random.fold_in(jax.random.fold_in(key, 6), axis_at), (shards_of,), jnp.float32, smallest / len(shards), high / len(shards))
        return jnp.repeat(jnp.exp(heights), shape[axis_at] // shards_of).reshape((-1,) + (1,) * (len(shape) - axis_at - 1))

    level = one(*shards[0])
    for cut in shards[1:]:
        level = level * one(*cut)
    return level


def shared_out(stream_key, own, number, rows, number_of, top, limit, skew):
    sequence = jax.random.permutation(stream_key, number_of)
    heavy_load, usual = shares(number_of, rows * top, limit, skew, True), shares(number_of, rows * top, limit, skew, False)
    places = jnp.arange(number_of)

    def named(tallies, turn):
        used = int((tallies > 0).sum())
        fixed = max(1, used // 4)
        passed = fixed + (places - fixed + turn * (used - fixed)) % max(1, number_of - fixed)
        return jnp.zeros((number_of,), jnp.int32).at[sequence[jnp.where(places < fixed, places, passed)]].set(jnp.asarray(tallies, jnp.int32))

    tallies = jnp.where(number % 4 == 0, named(heavy_load, number // 4), named(usual, number - number // 4 - 1))
    mixed = jax.random.permutation(jax.random.fold_in(own, 3), number_of)
    source_of, sink = mixed[0:number_of // 2 * 2:2], mixed[1:number_of // 2 * 2:2]
    room = jnp.minimum(tallies[source_of] - 1, limit - tallies[sink]) // 2
    room = jnp.where((source_of == sequence[0]) | (sink == sequence[0]) | (tallies[sink] == 0), 0, jnp.maximum(room, 0))
    passed = jax.random.randint(jax.random.fold_in(own, 4), (number_of // 2,), 0, 1 << 20) % (room + 1)
    tallies = tallies.at[source_of].add(-passed).at[sink].add(passed)
    items = jnp.searchsorted(jnp.cumsum(tallies), jnp.arange(rows * top), side="right").astype(jnp.int32)
    table = items.reshape(top, rows).T
    table = table[jax.random.permutation(jax.random.fold_in(own, 1), rows)]
    turn = jax.random.randint(jax.random.fold_in(own, 2), (rows, 1), 0, top)
    return jnp.take_along_axis(table, (jnp.arange(top)[None, :] + turn) % top, axis=1)


def shares(number_of, total, limit, lean, full):
    weights = [(1 << 20) // math.isqrt(standing ** lean) + 1 for standing in range(1, number_of + 1)]
    largest = limit if full else min(limit, max(-(-total // number_of), total * weights[0] // sum(weights)))
    least = 1 if total - largest >= number_of - 1 else 0
    counts, surplus = [largest] + [least] * (number_of - 1), total - largest - least * (number_of - 1)
    while surplus > 0:
        movable = [i for i in range(1, number_of) if counts[i] < largest] or [i for i in range(1, number_of) if counts[i] < limit]
        whole, budget = sum([weights[i] for i in movable]), surplus
        for i in movable:
            addition = min(limit - counts[i], max(1, budget * weights[i] // whole), surplus)
            counts[i] = counts[i] + addition
            surplus = surplus - addition
    return np.array(counts)


def gaussian(rng, dims, scale, most, cuts=(), kind=jnp.bfloat16):
    result = jax.random.normal(rng, dims, jnp.float32) * scale
    if len(cuts) > 0:
        result = steps_of(rng, dims, cuts, -0.22, 0.18) * result
    return jnp.clip(result, min=-most, max=most).astype(kind)


def setup_inputs(seed: int = 0) -> dict:
    seeds = jax.random.split(jax.random.key(seed), 15)
    mixer_input = gaussian(seeds[0], (SPAN_ELEMENTS, DI), 1.0, 6.0, ((0, 8), (1, 64)))
    step_sizes = draw_step_sizes(jax.random.fold_in(seeds[14], 71), 0)
    decay_rates = draw_decay_rates(jax.random.fold_in(seeds[14], 71), 0)
    input_proj = gaussian(seeds[3], (NS, SPAN_ELEMENTS), 0.5, 3.0, ((1, 8),), jnp.float32)
    output_proj = gaussian(seeds[4], (NS, SPAN_ELEMENTS), 0.25, 1.5, ((1, 8),), jnp.float32)
    skip_gain = jnp.clip(0.5 + 1.0 * jax.random.uniform(seeds[5], (DI,), jnp.float32) ** steps_of(seeds[5], (DI,), ((0, 64),), -0.2, 0.2), 0.5, 1.5)
    doc_starts = draw_doc_starts(jax.random.fold_in(seeds[14], 71), 0)
    ssm_grad = gaussian(seeds[7], (SPAN_ELEMENTS, DI), 1.0, 6.0, ((0, 8), (1, 64)))
    mixer_in_weight = gaussian(seeds[8], (DI, D), (64 * DI) ** -0.5, 0.0078125, ((0, 64), (1, 8)))
    residual_grad = gaussian(seeds[9], (SPAN_ELEMENTS, D), 0.1, 0.59765625, ((0, 128),))
    expert_index_pairs_keys = jax.random.split(jax.random.fold_in(seeds[10], 1), SPAN_ELEMENTS // TOK_DEV)
    expert_index_pairs_turns = jax.random.permutation(jax.random.fold_in(seeds[10], 3), SPAN_ELEMENTS // TOK_DEV)
    expert_index_pairs = jax.vmap(lambda own, number: shared_out(jax.random.fold_in(seeds[10], 2), own, number, TOK_DEV, EXPERTS, 2, CAP, 2))(expert_index_pairs_keys, expert_index_pairs_turns).reshape((SPAN_ELEMENTS, 2))
    route_probs = jnp.clip(0.05 + 0.55 * jax.random.uniform(seeds[11], (SPAN_ELEMENTS, 2), jnp.float32) ** steps_of(seeds[11], (SPAN_ELEMENTS, 2), ((0, 128),), -0.2, 0.2), 0.05, 0.6)
    hidden_saved = gaussian(seeds[12], (EXPERTS, FF, SLOTS), 0.5, 3.0, ((0, 16), (1, 32)))
    down_weight = gaussian(seeds[13], (EXPERTS, FF, D), FF ** -0.5, 0.0625, ((0, 16), (1, 32)))
    return dict(mixer_input=mixer_input, step_sizes=step_sizes, decay_rates=decay_rates, input_proj=input_proj, output_proj=output_proj, skip_gain=skip_gain, doc_starts=doc_starts, ssm_grad=ssm_grad, mixer_in_weight=mixer_in_weight, residual_grad=residual_grad, expert_index_pairs=expert_index_pairs, route_probs=route_probs, hidden_saved=hidden_saved, down_weight=down_weight)


def route_slots(expert_index_pairs):
    chosen = expert_index_pairs.reshape(SOURCES, TOK_DEV * 2).astype(jnp.int32)
    onehot = (chosen[:, :, None] == jnp.arange(EXPERTS, dtype=jnp.int32)[None, None, :]).astype(jnp.int32)
    earlier = jnp.cumsum(onehot, axis=1) - onehot
    token_position = jnp.sum(earlier * onehot, axis=2)
    column = (jnp.arange(SOURCES, dtype=jnp.int32)[:, None] * CAP + token_position).astype(jnp.int32)
    return chosen, column


def mamba_grads(mixer_input, step_sizes, decay_rates, input_proj, output_proj, skip_gain, doc_starts, ssm_grad):
    seg_len = 16
    seg_count = SPAN_ELEMENTS // seg_len
    input_vals = mixer_input.astype(jnp.float32).reshape(seg_count, seg_len, DI)
    step_vals = step_sizes.reshape(seg_count, seg_len, DI)
    grad_vals = ssm_grad.astype(jnp.float32).reshape(seg_count, seg_len, DI)
    keep_vals = (1 - doc_starts).astype(jnp.float32).reshape(seg_count, seg_len)
    in_weights = input_proj.T.reshape(seg_count, seg_len, NS)
    out_weights = output_proj.T.reshape(seg_count, seg_len, NS)
    segments = (input_vals, step_vals, keep_vals, in_weights)

    def advance(carried, sequence_element):
        input_now, step_now, keep_now, in_now = sequence_element
        decay_now = jnp.exp(step_now[None, :] * decay_rates) * keep_now
        updated = decay_now * carried + (step_now * input_now)[None, :] * in_now[:, None]
        return updated, (carried, updated, decay_now)

    def forward(carried, segment):
        ending, _ = lax.scan(advance, carried, segment)
        return ending, carried

    zero_state = jnp.zeros((NS, DI), jnp.float32)
    _, openings = lax.scan(forward, zero_state, segments)

    def backward(carry_pair, element_bundle):
        incoming, accrued = carry_pair
        segment, opening, grad_seg, out_seg = element_bundle
        _, (before, after, decays) = lax.scan(advance, opening, segment)
        input_seg, step_seg, _, in_seg = segment

        def retreat(inner, sequence_element):
            flowing, gathered = inner
            input_now, step_now, grad_now, in_now, out_now, state_before, state_after, decay_now = sequence_element
            adjoint = grad_now[None, :] * out_now[:, None] + flowing
            input_grad = skip_gain * grad_now + step_now * jnp.sum(adjoint * in_now[:, None], axis=0)
            step_grad = jnp.sum(adjoint * (decay_rates * decay_now * state_before + input_now[None, :] * in_now[:, None]), axis=0)
            in_grad = jnp.sum(adjoint * (step_now * input_now)[None, :], axis=1)
            out_grad = jnp.sum(grad_now[None, :] * state_after, axis=1)
            gathered = gathered + adjoint * step_now[None, :] * decay_now * state_before
            return (decay_now * adjoint, gathered), (input_grad, step_grad, in_grad, out_grad)

        ends, results = lax.scan(retreat, (incoming, accrued), (input_seg, step_seg, grad_seg, in_seg, out_seg, before, after, decays), reverse=True)
        return ends, results

    (_, decay_grad), (input_grad, step_grad, in_grad, out_grad) = lax.scan(backward, (zero_state, zero_state), (segments, openings, grad_vals, out_weights), reverse=True)
    skip_grad = jnp.sum(grad_vals * input_vals, axis=(0, 1))
    return (input_grad.reshape(SPAN_ELEMENTS, DI).astype(jnp.bfloat16), step_grad.reshape(SPAN_ELEMENTS, DI), in_grad.reshape(SPAN_ELEMENTS, NS).T, out_grad.reshape(SPAN_ELEMENTS, NS).T, decay_grad, skip_grad)


def moe_grads(moe_grad, expert_index_pairs, route_probs, hidden_saved, down_weight):
    chosen, column = route_slots(expert_index_pairs)
    picked = jnp.repeat(moe_grad.reshape(SOURCES, TOK_DEV, D), 2, axis=1)
    rows = jnp.zeros((EXPERTS, SLOTS, D), moe_grad.dtype).at[chosen, column].set(picked)
    scale = jnp.zeros((EXPERTS, SLOTS), jnp.bfloat16).at[chosen, column].set(route_probs.reshape(SOURCES, TOK_DEV * 2).astype(jnp.bfloat16))
    scale = lax.optimization_barrier(scale)

    def one_expert(expert_item):
        rows_now, scale_now, hidden_now, weight_now = expert_item
        factor = scale_now.astype(jnp.float32)
        direct = jnp.dot(weight_now, rows_now.T, preferred_element_type=jnp.float32)
        slot_hidden_gradient = (direct * factor[None, :]).astype(jnp.bfloat16)
        total = jnp.sum(hidden_now.astype(jnp.float32) * direct, axis=0)
        scaled = (rows_now.astype(jnp.float32) * factor[:, None]).astype(jnp.bfloat16)
        down_grad = jnp.dot(hidden_now, scaled, preferred_element_type=jnp.float32).astype(jnp.bfloat16)
        return slot_hidden_gradient, down_grad, total

    slot_hidden_gradient, down_grad, totals = lax.map(one_expert, (rows, scale, hidden_saved, down_weight))
    prob_grad = totals[chosen, column].reshape(SPAN_ELEMENTS, 2)
    return slot_hidden_gradient, down_grad, prob_grad


def reference(mixer_input, step_sizes, decay_rates, input_proj, output_proj, skip_gain, doc_starts, ssm_grad, mixer_in_weight, residual_grad, expert_index_pairs, route_probs, hidden_saved, down_weight):
    mamba = mamba_grads(mixer_input, step_sizes, decay_rates, input_proj, output_proj, skip_gain, doc_starts, ssm_grad)
    token_grad = jnp.dot(mamba[0], mixer_in_weight, preferred_element_type=jnp.float32)
    moe_grad = (token_grad + residual_grad.astype(jnp.float32)).astype(jnp.bfloat16)
    slot_hidden_gradient, down_grad, prob_grad = moe_grads(moe_grad, expert_index_pairs, route_probs, hidden_saved, down_weight)
    return (mamba[0], mamba[1], mamba[2], mamba[3], mamba[4], mamba[5], slot_hidden_gradient, down_grad, prob_grad)
```

```python
import jax
import jax.numpy as jnp
from jax import lax
from jax.experimental import pallas as pl
from jax.experimental.pallas import tpu as pltpu
from jax.sharding import PartitionSpec as P

F32 = jnp.float32
BF16 = jnp.bfloat16
MESH = pl.DeviceIdType.MESH

TOK = 128
CH = 128
NS = 16
BLK = 8
NBLK = TOK // BLK
Y, CORES, Z, X = 4, 2, 16, 4
CTX = Y * CORES
FSL = 512
CAP = 3
HALF = Z * CAP
SLOTS = CTX * HALF
NEAR = (1, 15, 2)
FAR = (4, 12, 8)


def nt(a, b):
    return lax.dot_general(a, b, (((1,), (1,)), ((), ())), preferred_element_type=F32)


def mm(a, b):
    return jnp.dot(a, b, preferred_element_type=F32)


def iota(shape, dim):
    return lax.broadcasted_iota(jnp.int32, shape, dim)


class Links:
    def __init__(self, send, recv):
        self.send, self.recv = send, recv
        self.n_send = self.n_recv = 0
        self.started = []

    def slot(self, n=1):
        first = self.n_recv
        self.n_recv += n
        assert self.n_recv <= NSEM
        return first

    def put(self, src, dst, recv_index, **device):
        copy = pltpu.make_async_remote_copy(
            src_ref=src,
            dst_ref=dst,
            send_sem=self.send.at[self.n_send],
            recv_sem=self.recv.at[recv_index],
            device_id=device,
            device_id_type=MESH,
        )
        self.n_send += 1
        assert self.n_send <= NSEM
        copy.start()
        self.started.append(copy)
        return copy

    def got(self, dst, recv_index):
        pltpu.make_async_copy(dst, dst, self.recv.at[recv_index]).wait()

    def drain(self):
        for copy in self.started:
            copy.wait_send()
        self.started = []


NSEM = 128


def body(
    x_ref, step_ref, rates_ref, inp_ref, outp_ref, skip_ref, doc_ref, g_ref, wmix_ref, resid_ref,
    idx_ref, prob_ref, hidden_ref, weight_ref,
    ssm_ref, stepg_ref, inpg_ref, outpg_ref, decg_ref, skipg_ref, slot_ref, down_ref, probg_ref,
    xf, gf, a_s, inf_s, adj_s, ap_s, bsel, ssm_f, xbuf, sbuf, wbuf, pbuf, rbuf1, abuf, rbuf2,
    gbuf, ibuf, pair_out, pair_in, sel_s, scale_s, scale_in, rows, w_s,
    iop, iop_in, iop_far, iop_near, iop_all, dsp, dsp_in, tot, tot_x, tot_c, tot_z,
    send_sems, recv_sems, local_sems, weight_sem,
):
    links = Links(send_sems, recv_sems)
    c, e, t = lax.axis_index("ctx"), lax.axis_index("exp"), lax.axis_index("tp")
    y, core = lax.div(c, 2), lax.rem(c, 2)
    r0, q0 = lax.rem(e, 4), lax.div(e, 4)
    fs = 2 * lax.rem(t + y, 4) + core

    def at_y(dy):
        return 2 * lax.rem(y + dy, 4) + core

    def at_x(dx):
        return lax.rem(t + dx, 4)

    def at_z(dz):
        return lax.rem(e + dz, Z)

    barrier = pltpu.get_barrier_semaphore()
    partners = 0
    for dc in range(CTX):
        for dx in range(X):
            if dc or dx:
                pl.semaphore_signal(
                    barrier, inc=1, device_id={"ctx": lax.rem(c + dc, CTX), "tp": at_x(dx)}, device_id_type=MESH
                )
                partners += 1
    for dz in range(1, Z):
        pl.semaphore_signal(barrier, inc=1, device_id={"exp": at_z(dz)}, device_id_type=MESH)
        partners += 1

    load_weight = pltpu.make_async_copy(weight_ref, w_s, local_sems.at[0])
    load_weight.start()
    pl.semaphore_wait(barrier, partners)

    for dy in range(4):
        if dy == 0:
            @pl.when(t == 0)
            def _():
                pltpu.make_async_copy(wmix_ref, wbuf.at[0], weight_sem.at[0]).start()

            @pl.when(t != 0)
            def _():
                pltpu.make_async_remote_copy(
                    src_ref=wmix_ref, dst_ref=wbuf.at[t], send_sem=local_sems.at[1], recv_sem=weight_sem.at[t],
                    device_id={"tp": 0}, device_id_type=MESH,
                ).start()
        else:
            copy = pltpu.make_async_remote_copy(
                src_ref=wmix_ref, dst_ref=wbuf.at[t], send_sem=send_sems.at[links.n_send],
                recv_sem=weight_sem.at[t], device_id={"ctx": at_y(dy), "tp": (4 - dy) % 4}, device_id_type=MESH,
            )
            links.n_send += 1
            copy.start()
            links.started.append(copy)

    lane8 = iota((BLK, 128), 1)
    idx = idx_ref[...].astype(F32)
    prob = prob_ref[...].astype(BF16).astype(F32)
    info = jnp.where(
        lane8 == 0, idx[:, 0:1], jnp.where(lane8 == 1, idx[:, 1:2], jnp.where(lane8 == 2, prob[:, 0:1], prob[:, 1:2]))
    )
    other_fs = 2 * lax.rem(t + y, 4) + (1 - core)
    pair_out[:, 0:FSL] = resid_ref[:, pl.ds(pl.multiple_of(other_fs * FSL, FSL), FSL)].astype(F32)
    pair_out[:, FSL:] = info
    k_pair = links.slot()
    links.put(pair_out, pair_in, k_pair, ctx=2 * y + (1 - core))

    xf[...] = x_ref[...].astype(F32)
    gf[...] = g_ref[...].astype(F32)
    g_bf = g_ref[...]
    u_bf = (step_ref[...] * xf[...]).astype(BF16)
    row, lane = iota((128, 128), 0), iota((128, 128), 1)
    b_tile = jnp.concatenate([inp_ref[...]] * BLK, axis=0)
    c_tile = jnp.concatenate([outp_ref[...]] * BLK, axis=0)
    bsel[...] = jnp.where(lax.rem(row, BLK) == lax.div(lane, NS), b_tile.T, 0.0)
    row_tok = lax.div(row, NS)

    def prepare(i, carry):
        at = pl.ds(pl.multiple_of(i * BLK, BLK), BLK)
        here = lane == row_tok + i * BLK
        decays = jnp.exp(step_ref[at, :][:, None, :] * rates_ref[...][None])
        for j in range(BLK):
            keep = (1 - doc_ref[i * BLK + j]).astype(F32)
            a_s[i * BLK + j] = decays[j] * keep
        inf_s[at] = mm(jnp.where(here, b_tile, 0.0).astype(BF16), u_bf).reshape(BLK, NS, CH)
        adj_s[at] = mm(jnp.where(here, c_tile, 0.0).astype(BF16), g_bf).reshape(BLK, NS, CH)
        return carry

    lax.fori_loop(0, NBLK, prepare, 0)

    zero = jnp.zeros((NS, CH), F32)

    def summarise(i, carry):
        state, back, damp = carry
        for j in range(BLK):
            up = i * BLK + j
            down = TOK - 1 - up
            decay = a_s[up]
            state = decay * state + inf_s[up]
            damp = damp * decay
            back = a_s[down] * (adj_s[down] + back)
        return state, back, damp

    state, back, damp = lax.fori_loop(0, NBLK, summarise, (zero, zero, zero + 1.0))
    xbuf[0, 0:NS] = damp
    xbuf[0, NS : 2 * NS] = state
    xbuf[0, 2 * NS :] = back
    k_ctx = links.slot(CTX)
    for dc in range(1, CTX):
        links.put(xbuf.at[0], xbuf.at[dc], k_ctx + dc, ctx=lax.rem(c + dc, CTX))

    links.got(pair_in, k_pair)
    mine = info
    theirs = pair_in[:, FSL:]
    first = core == 0
    ibuf[r0, q0, 0:BLK] = jnp.where(first, mine, theirs)
    ibuf[r0, q0, BLK:] = jnp.where(first, theirs, mine)
    k_ifar = links.slot(3)
    for n, dz in enumerate(FAR):
        links.put(ibuf.at[r0, q0], ibuf.at[r0, q0], k_ifar + n, exp=at_z(dz))

    for dc in range(1, CTX):
        links.got(xbuf.at[dc], k_ctx + dc)
    entering, arriving = zero, zero
    for other in range(CTX):
        from_slot = lax.rem(c - other + CTX, CTX)
        entering = jnp.where(
            other < c, xbuf[from_slot, 0:NS] * entering + xbuf[from_slot, NS : 2 * NS], entering
        )
    for other in reversed(range(CTX)):
        from_slot = lax.rem(c - other + CTX, CTX)
        arriving = jnp.where(other > c, xbuf[from_slot, 0:NS] * arriving + xbuf[from_slot, 2 * NS :], arriving)

    def scan(i, carry):
        state, back = carry
        for j in range(BLK):
            up = i * BLK + j
            down = TOK - 1 - up
            kept = a_s[up] * state
            ap_s[up] = kept
            state = kept + inf_s[up]
            adjoint = adj_s[down] + back
            adj_s[down] = adjoint
            back = a_s[down] * adjoint
        return state, back

    lax.fori_loop(0, NBLK, scan, (entering, arriving))

    for n, dz in enumerate(FAR):
        links.got(ibuf.at[r0, lax.rem(q0 + 4 - dz // 4, 4)], k_ifar + n)
    k_inear = links.slot(3)
    for n, dz in enumerate(NEAR):
        links.put(ibuf.at[r0], ibuf.at[r0], k_inear + n, exp=at_z(dz))

    rates = rates_ref[...]
    ones8 = jnp.where(iota((BLK, 128), 0) == lax.div(lane8, NS), 1.0, 0.0).astype(BF16)
    tok3, lane3 = iota((BLK, NS, 128), 0), iota((BLK, NS, 128), 2)
    skip = skip_ref[...]

    def gradients(i, carry):
        acc_in, acc_out, acc_decay = carry
        at = pl.ds(pl.multiple_of(i * BLK, BLK), BLK)
        adjoint, kept = adj_s[at], ap_s[at]
        states = (kept + inf_s[at]).reshape(128, CH).astype(BF16)
        adjoint_bf = adjoint.reshape(128, CH).astype(BF16)
        here = lane3 == tok3 + i * BLK
        acc_out += jnp.sum(jnp.where(here, nt(states, g_bf).reshape(BLK, NS, 128), 0.0), axis=0)
        acc_in += jnp.sum(jnp.where(here, nt(adjoint_bf, u_bf).reshape(BLK, NS, 128), 0.0), axis=0)
        through = mm(bsel[at, :].astype(BF16), adjoint_bf)
        product = adjoint * kept
        rated = mm(ones8, (product * rates[None]).reshape(128, CH).astype(BF16))
        step = step_ref[at, :]
        acc_decay += jnp.sum(product * step[:, None, :], axis=0)
        stepg_ref[at, :] = rated + xf[at, :] * through
        ssm_f[at, :] = skip * gf[at, :] + step * through
        return acc_in, acc_out, acc_decay

    acc_in, acc_out, acc_decay = lax.fori_loop(0, NBLK, gradients, (zero, zero, zero))

    ssm_bf = ssm_f[...].astype(BF16)
    ssm_ref[...] = ssm_bf
    sbuf[0, 0] = ssm_bf
    k_s = links.slot(2 * X)
    for dk in range(2):
        for dx in range(X):
            if dk or dx:
                links.put(
                    sbuf.at[0, 0], sbuf.at[dk, dx], k_s + dk * X + dx,
                    ctx=2 * y + lax.rem(core + dk, 2), tp=at_x(dx),
                )

    iop[0:2] = acc_in.reshape(2, 8, 128)
    iop[2:4] = acc_out.reshape(2, 8, 128)
    k_iox = links.slot(4)
    for dx in range(1, X):
        links.put(iop.at[at_x(dx)], iop_in.at[dx], k_iox + dx, tp=at_x(dx))
    dsp[0:NS] = acc_decay
    skip_part = jnp.sum(gf[...] * xf[...], axis=0, keepdims=True)
    dsp[NS:] = jnp.broadcast_to(skip_part, (BLK, CH))
    k_dsp = links.slot(CTX)
    for dc in range(1, CTX):
        links.put(dsp, dsp_in.at[dc], k_dsp + dc, ctx=lax.rem(c + dc, CTX))

    for n, dz in enumerate(NEAR):
        links.got(ibuf.at[lax.rem(r0 + 16 - dz, 4)], k_inear + n)
    infos = ibuf[...].reshape(256, 128)
    e_f = e.astype(F32)
    hit0 = jnp.where(infos[:, 0:1] == e_f, 1.0, 0.0)
    hit1 = jnp.where(infos[:, 1:2] == e_f, 1.0, 0.0)
    hit = jnp.broadcast_to(hit0 + hit1, (256, 128))
    factor = hit0 * infos[:, 2:3] + hit1 * infos[:, 3:4]
    r256, l256 = iota((256, 256), 0), iota((256, 256), 1)
    before = jnp.where((lax.div(r256, BLK) == lax.div(l256, BLK)) & (r256 > l256), 1.0, 0.0).astype(BF16)
    position = mm(before, hit.astype(BF16))
    tok_row = iota((256, 128), 0)
    tok_r, tok_q = lax.div(tok_row, 64), lax.rem(lax.div(tok_row, 16), 4)
    tok_k = lax.rem(lax.div(tok_row, BLK), 2)
    tok_slot = (tok_k * Z + tok_q * 4 + tok_r) * CAP
    slot_of = tok_slot.astype(F32) + position
    picked = jnp.where(iota((256, 128), 1).astype(F32) == slot_of, hit, 0.0)
    sel_s[...] = picked.T.astype(BF16)
    own_scale = jnp.sum(picked * factor, axis=0, keepdims=True)[:, 0 : 2 * HALF]
    zeros96 = jnp.zeros((1, 2 * HALF), F32)
    scale_s[0] = jnp.concatenate([jnp.where(y == n, own_scale, zeros96) for n in range(Y)], axis=1)
    k_scale = links.slot(4)
    for dy in range(1, 4):
        links.put(scale_s.at[0], scale_in.at[dy], k_scale + dy, ctx=at_y(dy))

    for n in range(4):
        pltpu.make_async_copy(wbuf.at[n], wbuf.at[n], weight_sem.at[n]).wait()
    for dk in range(2):
        for dx in range(X):
            if dk or dx:
                links.got(sbuf.at[dk, dx], k_s + dk * X + dx)
    mixer = wbuf[...].reshape(4 * 128, FSL)
    parts = []
    for k in range(2):
        dk = lax.rem(core + k, 2)
        lhs = jnp.concatenate([sbuf[dk, lax.rem(t - n + 4, 4)] for n in range(4)], axis=1)
        parts.append(mm(lhs, mixer).reshape(Z, BLK, FSL))
    chunks = jnp.concatenate(parts, axis=1).astype(BF16)
    for n in range(Z):
        pbuf[n % 4, n // 4] = chunks[n]

    k_r1 = links.slot(3)
    for n, dz in enumerate(NEAR):
        links.put(pbuf.at[lax.rem(r0 + dz, 4)], rbuf1.at[n], k_r1 + n, exp=at_z(dz))
    for dx in range(1, X):
        links.got(iop_in.at[dx], k_iox + dx)
    iop_far[0] = iop[t] + iop_in[1] + iop_in[2] + iop_in[3]
    k_iof = links.slot(4)
    for n, dz in enumerate(FAR):
        links.put(iop_far.at[0], iop_far.at[n + 1], k_iof + n, exp=at_z(dz))
    for n in range(3):
        links.got(rbuf1.at[n], k_r1 + n)
    summed = pbuf[r0].astype(F32)
    for n in range(3):
        summed += rbuf1[n].astype(F32)
    abuf[...] = summed.astype(BF16)
    k_r2 = links.slot(3)
    for n, dz in enumerate(FAR):
        links.put(abuf.at[lax.rem(q0 + dz // 4, 4)], rbuf2.at[n], k_r2 + n, exp=at_z(dz))
    own_resid = resid_ref[:, pl.ds(pl.multiple_of(fs * FSL, FSL), FSL)].astype(F32)
    their_resid = pair_in[:, 0:FSL]
    resid = jnp.concatenate(
        [jnp.where(first, own_resid, their_resid), jnp.where(first, their_resid, own_resid)], axis=0
    )
    for n in range(3):
        links.got(rbuf2.at[n], k_r2 + n)
    total = abuf[q0].astype(F32) + resid
    for n in range(3):
        total += rbuf2[n].astype(F32)

    gbuf[r0, q0] = total.astype(BF16)
    k_g1 = links.slot(3)
    for n, dz in enumerate(FAR):
        links.put(gbuf.at[r0, q0], gbuf.at[r0, q0], k_g1 + n, exp=at_z(dz))
    for n in range(3):
        links.got(iop_far.at[n + 1], k_iof + n)
    iop_near[0] = iop_far[0] + iop_far[1] + iop_far[2] + iop_far[3]
    for n, dz in enumerate(FAR):
        links.got(gbuf.at[r0, lax.rem(q0 + 4 - dz // 4, 4)], k_g1 + n)
    k_g2 = links.slot(3)
    for n, dz in enumerate(NEAR):
        links.put(gbuf.at[r0], gbuf.at[r0], k_g2 + n, exp=at_z(dz))
    k_ion = links.slot(4)
    for n, dz in enumerate(NEAR):
        links.put(iop_near.at[0], iop_near.at[n + 1], k_ion + n, exp=at_z(dz))
    for n, dz in enumerate(NEAR):
        links.got(gbuf.at[lax.rem(r0 + 16 - dz, 4)], k_g2 + n)

    picked_rows = mm(sel_s[...], gbuf[...].reshape(256, FSL)).astype(BF16)
    rows[core, t, y, 0] = picked_rows[0:HALF]
    rows[core, t, y, 1] = picked_rows[HALF : 2 * HALF]
    other_core = 2 * y + (1 - core)
    k_p1 = links.slot(8)
    for d in (1, 3, 2):
        links.put(rows.at[core, t, y, 0], rows.at[core, t, y, 0], k_p1 + d, tp=at_x(d))
        links.put(rows.at[core, t, y, 1], rows.at[core, t, y, 1], k_p1 + 4 + d, ctx=at_y(d))
    for d in (1, 3, 2):
        links.got(rows.at[core, at_x(4 - d), y, 0], k_p1 + d)
        links.got(rows.at[core, t, lax.rem(y + 4 - d, 4), 1], k_p1 + 4 + d)
    k_p2 = links.slot(8)
    for d in (1, 3, 2):
        links.put(rows.at[core, :, y, 0], rows.at[core, :, y, 0], k_p2 + d, ctx=at_y(d))
        links.put(rows.at[core, t, :, 1], rows.at[core, t, :, 1], k_p2 + 4 + d, tp=at_x(d))
    k_core = links.slot(8)
    links.put(rows.at[core, :, y, 0], rows.at[core, :, y, 0], k_core, ctx=other_core)
    links.put(rows.at[core, t, :, 1], rows.at[core, t, :, 1], k_core + 4, ctx=other_core)

    for n in range(3):
        links.got(iop_near.at[n + 1], k_ion + n)
    iop_out = iop_near[0] + iop_near[1] + iop_near[2] + iop_near[3]
    iop_in[0] = iop_out
    k_ioa = links.slot(4)
    for dx in range(1, X):
        links.put(iop_in.at[0], iop_all.at[t], k_ioa + dx, tp=at_x(dx))
    for dc in range(1, CTX):
        links.got(dsp_in.at[dc], k_dsp + dc)
    sums = dsp[...]
    for dc in range(1, CTX):
        sums += dsp_in[dc]
    decg_ref[...] = sums[0:NS]
    skipg_ref[...] = sums[NS : NS + 1]
    for dy in range(1, 4):
        links.got(scale_in.at[dy], k_scale + dy)
    scale = scale_s[0] + scale_in[1] + scale_in[2] + scale_in[3]

    hidden = hidden_ref[...]
    hidden_scaled = (hidden.astype(F32) * scale).astype(BF16)
    load_weight.wait()

    for d in (1, 3, 2):
        from_y, from_x = lax.rem(y + 4 - d, 4), at_x(4 - d)
        links.got(rows.at[core, :, from_y, 0], k_p2 + d)
        links.put(rows.at[core, :, from_y, 0], rows.at[core, :, from_y, 0], k_core + d, ctx=other_core)
        links.got(rows.at[core, from_x, :, 1], k_p2 + 4 + d)
        links.put(rows.at[core, from_x, :, 1], rows.at[core, from_x, :, 1], k_core + 4 + d, ctx=other_core)
    theirs_core = 1 - core
    for d in (0, 1, 3, 2):
        from_y, from_x = lax.rem(y + 4 - d, 4), at_x(4 - d)
        links.got(rows.at[theirs_core, :, from_y, 0], k_core + d)
        links.got(rows.at[theirs_core, from_x, :, 1], k_core + 4 + d)

    direct = jnp.zeros((hidden.shape[0], SLOTS), F32)
    for k in range(2):
        for f in range(4):
            at = pl.ds((2 * f + k) * FSL, FSL)
            part = jnp.concatenate([rows[k, (f - n) % 4, n].reshape(2 * HALF, FSL) for n in range(Y)], axis=0)
            direct += nt(w_s[:, at], part)
            down_ref[:, at] = mm(hidden_scaled, part).astype(BF16)
    slot_ref[...] = (direct * scale).astype(BF16)
    tot[0] = jnp.sum(hidden.astype(F32) * direct, axis=0, keepdims=True)

    k_tx = links.slot(4)
    for dx in range(1, X):
        links.put(tot.at[0], tot_x.at[dx], k_tx + dx, tp=at_x(dx))
    for dx in range(1, X):
        links.got(iop_all.at[at_x(4 - dx)], k_ioa + dx)
    iop_all[t] = iop_out
    inpg_ref[...] = iop_all[0:2].reshape(NS, 128)
    outpg_ref[...] = iop_all[2:4].reshape(NS, 128)

    idx0, idx1 = jnp.broadcast_to(info[:, 0:1], (BLK, 128)), jnp.broadcast_to(info[:, 1:2], (BLK, 128))
    rows8 = iota((BLK, 128), 0)
    pos0, pos1 = jnp.zeros((BLK, 128), F32), jnp.zeros((BLK, 128), F32)
    for i in range(BLK):
        i0, i1 = idx0[i : i + 1], idx1[i : i + 1]
        pos0 += jnp.where((rows8 > i) & ((i0 == idx0) | (i1 == idx0)), 1.0, 0.0)
        pos1 += jnp.where((rows8 > i) & ((i0 == idx1) | (i1 == idx1)), 1.0, 0.0)
    lane384 = iota((BLK, SLOTS), 1).astype(F32)
    base = ((c * Z + e) * CAP).astype(F32)

    for dx in range(1, X):
        links.got(tot_x.at[dx], k_tx + dx)
    tot_c[0] = tot[0] + tot_x[1] + tot_x[2] + tot_x[3]
    k_tc = links.slot(CTX)
    for dc in range(1, CTX):
        links.put(tot_c.at[0], tot_c.at[dc], k_tc + dc, ctx=lax.rem(c + dc, CTX))
    for dc in range(1, CTX):
        links.got(tot_c.at[dc], k_tc + dc)
    plane = tot_c[0]
    for dc in range(1, CTX):
        plane += tot_c[dc]
    tot_z[0] = plane
    k_tz = links.slot(Z)
    for dz in range(1, Z):
        links.put(tot_z.at[0], tot_z.at[dz], k_tz + dz, exp=at_z(dz))
    for dz in range(1, Z):
        links.got(tot_z.at[dz], k_tz + dz)
    val0, val1 = jnp.zeros((BLK, SLOTS), F32), jnp.zeros((BLK, SLOTS), F32)
    for dz in range(Z):
        expert = at_z(Z - dz).astype(F32)
        line = jnp.broadcast_to(tot_z[dz], (BLK, SLOTS))
        val0 = jnp.where(info[:, 0:1] == expert, line, val0)
        val1 = jnp.where(info[:, 1:2] == expert, line, val1)
    out0 = jnp.sum(jnp.where(lane384 == base + pos0[:, 0:1], val0, 0.0), axis=1, keepdims=True)
    out1 = jnp.sum(jnp.where(lane384 == base + pos1[:, 0:1], val1, 0.0), axis=1, keepdims=True)
    probg_ref[...] = jnp.where(iota((BLK, 2), 1) == 0, out0, out1)

    @pl.when(t != 0)
    def _():
        pltpu.make_async_copy(wmix_ref, wbuf.at[0], local_sems.at[1]).wait()

    links.drain()


def shards(
    mixer_input, step_sizes, decay_rates, input_proj, output_proj, skip_gain, doc_starts, ssm_grad, mixer_in_weight,
    residual_grad, expert_index_pairs, route_probs, hidden_saved, down_weight,
):
    hidden = hidden_saved[0].shape[0]
    features = down_weight.shape[2]
    vmem = pl.BlockSpec(memory_space=pltpu.VMEM)
    anywhere = pl.BlockSpec(memory_space=pl.ANY)
    smem = pl.BlockSpec(memory_space=pltpu.SMEM)
    shape = jax.ShapeDtypeStruct
    out = pl.pallas_call(
        body,
        out_shape=(
            shape((TOK, CH), BF16),
            shape((TOK, CH), F32),
            shape((NS, TOK), F32),
            shape((NS, TOK), F32),
            shape((NS, CH), F32),
            shape((1, CH), F32),
            shape((hidden, SLOTS), BF16),
            shape((hidden, features), BF16),
            shape((BLK, 2), F32),
        ),
        in_specs=[vmem, vmem, vmem, vmem, vmem, vmem, smem, vmem, anywhere, vmem, vmem, vmem, vmem, anywhere],
        out_specs=tuple([vmem] * 9),
        scratch_shapes=[
            pltpu.VMEM((TOK, CH), F32),
            pltpu.VMEM((TOK, CH), F32),
            pltpu.VMEM((TOK, NS, CH), F32),
            pltpu.VMEM((TOK, NS, CH), F32),
            pltpu.VMEM((TOK, NS, CH), F32),
            pltpu.VMEM((TOK, NS, CH), F32),
            pltpu.VMEM((128, 128), F32),
            pltpu.VMEM((TOK, CH), F32),
            pltpu.VMEM((CTX, 3 * NS, CH), F32),
            pltpu.VMEM((2, X, TOK, CH), BF16),
            pltpu.VMEM((4, 128, FSL), BF16),
            pltpu.VMEM((4, 4, 16, FSL), BF16),
            pltpu.VMEM((3, 4, 16, FSL), BF16),
            pltpu.VMEM((4, 16, FSL), BF16),
            pltpu.VMEM((3, 16, FSL), BF16),
            pltpu.VMEM((4, 4, 16, FSL), BF16),
            pltpu.VMEM((4, 4, 16, 128), F32),
            pltpu.VMEM((BLK, FSL + 128), F32),
            pltpu.VMEM((BLK, FSL + 128), F32),
            pltpu.VMEM((128, 256), BF16),
            pltpu.VMEM((1, 1, SLOTS), F32),
            pltpu.VMEM((4, 1, SLOTS), F32),
            pltpu.VMEM((2, X, Y, 2, HALF, FSL), BF16),
            pltpu.VMEM((hidden, features), BF16),
            pltpu.VMEM((4, 8, 128), F32),
            pltpu.VMEM((4, 8, 128), F32),
            pltpu.VMEM((4, 8, 128), F32),
            pltpu.VMEM((4, 8, 128), F32),
            pltpu.VMEM((4, 8, 128), F32),
            pltpu.VMEM((NS + BLK, CH), F32),
            pltpu.VMEM((CTX, NS + BLK, CH), F32),
            pltpu.VMEM((1, 1, SLOTS), F32),
            pltpu.VMEM((4, 1, SLOTS), F32),
            pltpu.VMEM((CTX, 1, SLOTS), F32),
            pltpu.VMEM((Z, 1, SLOTS), F32),
            pltpu.SemaphoreType.DMA((NSEM,)),
            pltpu.SemaphoreType.DMA((NSEM,)),
            pltpu.SemaphoreType.DMA((2,)),
            pltpu.SemaphoreType.DMA((4,)),
        ],
        compiler_params=pltpu.CompilerParams(
            collective_id=0, has_side_effects=True, vmem_limit_bytes=48 * 1024 * 1024
        ),
        name="scan_and_experts",
    )(
        mixer_input, step_sizes, decay_rates, input_proj, output_proj, skip_gain.reshape(1, CH), doc_starts, ssm_grad,
        mixer_in_weight, residual_grad, expert_index_pairs, route_probs, hidden_saved[0], down_weight[0],
    )
    ssm, stepg, inpg, outpg, decg, skipg, slot, down, probg = out
    return ssm, stepg, inpg, outpg, decg, skipg.reshape(CH), slot[None], down[None], probg


def solution(mesh):
    return jax.shard_map(
        shards,
        mesh=mesh,
        in_specs=(
            P("ctx", ("exp", "tp")),
            P("ctx", ("exp", "tp")),
            P(None, ("exp", "tp")),
            P(None, "ctx"),
            P(None, "ctx"),
            P(("exp", "tp")),
            P("ctx"),
            P("ctx", ("exp", "tp")),
            P(("exp", "tp"), "ctx"),
            P(("ctx", "exp"), None),
            P(("ctx", "exp"), None),
            P(("ctx", "exp"), None),
            P("exp", ("ctx", "tp"), None),
            P("exp", ("ctx", "tp"), None),
        ),
        out_specs=(
            P("ctx", ("exp", "tp")),
            P("ctx", ("exp", "tp")),
            P(None, "ctx"),
            P(None, "ctx"),
            P(None, ("exp", "tp")),
            P(("exp", "tp")),
            P("exp", ("ctx", "tp"), None),
            P("exp", ("ctx", "tp"), None),
            P(("ctx", "exp"), None),
        ),
        check_vma=False,
    )
```

```python
import jax
import jax.numpy as jnp
from jax import lax
from jax.experimental import pallas as pl
from jax.experimental.pallas import tpu as pltpu
from jax.sharding import PartitionSpec as P

F32 = jnp.float32
BF16 = jnp.bfloat16
MESH = pl.DeviceIdType.MESH

TOK = 128
CH = 128
NS = 16
BLK = 8
NBLK = TOK // BLK
Y, CORES, Z, X = 4, 2, 16, 4
CTX = Y * CORES
FSL = 512
CAP = 3
HALF = Z * CAP
SLOTS = CTX * HALF
FAR = (4, 12, 8)


def nt(a, b):
    return lax.dot_general(a, b, (((1,), (1,)), ((), ())), preferred_element_type=F32)


def mm(a, b):
    return jnp.dot(a, b, preferred_element_type=F32)


def iota(shape, dim):
    return lax.broadcasted_iota(jnp.int32, shape, dim)


class Links:
    def __init__(self, send, recv):
        self.send, self.recv = send, recv
        self.n_send = self.n_recv = 0
        self.started = []

    def slot(self, n=1):
        first = self.n_recv
        self.n_recv += n
        assert self.n_recv <= NSEM
        return first

    def put(self, src, dst, recv_index, **device):
        copy = pltpu.make_async_remote_copy(
            src_ref=src,
            dst_ref=dst,
            send_sem=self.send.at[self.n_send],
            recv_sem=self.recv.at[recv_index],
            device_id=device,
            device_id_type=MESH,
        )
        self.n_send += 1
        assert self.n_send <= NSEM
        copy.start()
        self.started.append(copy)
        return copy

    def got(self, dst, recv_index):
        pltpu.make_async_copy(dst, dst, self.recv.at[recv_index]).wait()

    def drain(self):
        for copy in self.started:
            copy.wait_send()
        self.started = []


NSEM = 160
VMEM_LIMIT = 60 * 1024 * 1024


def body(
    x_hbm, step_hbm, rates_hbm, inp_hbm, outp_hbm, skip_hbm, doc_hbm, g_hbm, wmix_ref, resid_hbm,
    idx_hbm, prob_hbm, hidden_hbm, weight_ref,
    ssm_ref, stepg_ref, inpg_ref, outpg_ref, decg_ref, skipg_ref, slot_ref, down_hbm, probg_ref,
    x_ref, step_ref, rates_ref, inp_ref, outp_ref, skip_ref, doc_ref, g_ref, resid_ref, idx_ref, prob_ref, hidden_ref, down_ref,
    xf, gf, a_s, inf_s, adj_s, ap_s, bsel, ssm_f, xbuf, sbuf, wbuf, pbuf, rbuf1, abuf, rbuf2,
    gbuf, ibuf, pair_out, pair_in, sel_s, scale_s, scale_in, rows, w_s,
    iop, iop_in, iop_far, iop_near, iop_all, dsp, dsp_in, tot, tot_x, tot_c, tot_z,
    send_sems, recv_sems, local_sems, weight_sem,
):
    links = Links(send_sems, recv_sems)
    c, e, t = lax.axis_index("ctx"), lax.axis_index("exp"), lax.axis_index("tp")
    y, core = lax.div(c, 2), lax.rem(c, 2)
    r0, q0 = lax.rem(e, 4), lax.div(e, 4)
    fs = 2 * lax.rem(t + y, 4) + core

    def at_y(dy):
        return 2 * lax.rem(y + dy, 4) + core

    def at_x(dx):
        return lax.rem(t + dx, 4)

    def at_z(dz):
        return lax.rem(e + dz, Z)

    barrier = pltpu.get_barrier_semaphore()
    partners = 0
    for dc in range(CTX):
        for dx in range(X):
            if dc or dx:
                pl.semaphore_signal(
                    barrier, inc=1, device_id={"ctx": lax.rem(c + dc, CTX), "tp": at_x(dx)}, device_id_type=MESH
                )
                partners += 1
    for dz in range(1, Z):
        pl.semaphore_signal(barrier, inc=1, device_id={"exp": at_z(dz)}, device_id_type=MESH)
        partners += 1

    def load(src, dst, at):
        copy = pltpu.make_async_copy(src, dst, local_sems.at[at])
        copy.start()
        return copy

    scan_loads = [
        load(src, dst, 2 + n)
        for n, (src, dst) in enumerate((
            (step_hbm, step_ref), (rates_hbm, rates_ref), (x_hbm, x_ref), (g_hbm, g_ref), (inp_hbm, inp_ref),
            (outp_hbm, outp_ref), (doc_hbm, doc_ref), (skip_hbm, skip_ref), (idx_hbm, idx_ref),
            (prob_hbm, prob_ref), (resid_hbm, resid_ref),
        ))
    ]
    late_loads = [load(hidden_hbm, hidden_ref, 13)]
    for n in range(7):
        part = pl.ds(n * 32, 32)
        late_loads.append(load(weight_ref.at[part], w_s.at[part], 14 + n))
    near = (1, 15, 2 + 12 * core)
    for copy in scan_loads:
        copy.wait()

    lane8 = iota((BLK, 128), 1)
    row8 = iota((BLK, 128), 0)
    info = jnp.zeros((BLK, 128), F32)
    for i in range(BLK):
        for k in range(2):
            info = jnp.where((row8 == i) & (lane8 == k), idx_ref[k, i].astype(F32), info)
            info = jnp.where((row8 == i) & (lane8 == 2 + k), prob_ref[k, i], info)
    info = info.astype(BF16).astype(F32)
    other_fs = 2 * lax.rem(t + y, 4) + (1 - core)
    pair_out[:, 0:FSL] = resid_ref[:, pl.ds(pl.multiple_of(other_fs * FSL, FSL), FSL)].astype(F32)
    pair_out[:, FSL:] = info
    xf[...] = x_ref[...].astype(F32)
    gf[...] = g_ref[...].astype(F32)
    g_bf = g_ref[...]
    u_bf = (step_ref[...] * xf[...]).astype(BF16)
    row, lane = iota((128, 128), 0), iota((128, 128), 1)
    b_tile = jnp.concatenate([inp_ref[...]] * BLK, axis=0)
    c_tile = jnp.concatenate([outp_ref[...]] * BLK, axis=0)
    bsel[...] = jnp.where(lax.rem(row, BLK) == lax.div(lane, NS), b_tile.T, 0.0)
    row_tok = lax.div(row, NS)

    def prepare(i, carry):
        at = pl.ds(pl.multiple_of(i * BLK, BLK), BLK)
        here = lane == row_tok + i * BLK
        decays = jnp.exp(step_ref[at, :][:, None, :] * rates_ref[...][None])
        for j in range(BLK):
            keep = (1 - doc_ref[i * BLK + j]).astype(F32)
            a_s[i * BLK + j] = decays[j] * keep
        inf_s[at] = mm(jnp.where(here, b_tile, 0.0).astype(BF16), u_bf).reshape(BLK, NS, CH)
        adj_s[at] = mm(jnp.where(here, c_tile, 0.0).astype(BF16), g_bf).reshape(BLK, NS, CH)
        return carry

    lax.fori_loop(0, NBLK, prepare, 0)

    zero = jnp.zeros((NS, CH), F32)

    def summarise(i, carry):
        state, back, damp = carry
        for j in range(BLK):
            up = i * BLK + j
            down = TOK - 1 - up
            decay = a_s[up]
            state = decay * state + inf_s[up]
            damp = damp * decay
            back = a_s[down] * (adj_s[down] + back)
        return state, back, damp

    state, back, damp = lax.fori_loop(0, NBLK, summarise, (zero, zero, zero + 1.0))
    xbuf[0, 0:NS] = damp
    xbuf[0, NS : 2 * NS] = state
    xbuf[0, 2 * NS :] = back
    pl.semaphore_wait(barrier, partners)
    k_ctx = links.slot(CTX)
    for dc in range(1, CTX):
        links.put(xbuf.at[0], xbuf.at[dc], k_ctx + dc, ctx=lax.rem(c + dc, CTX))

    k_pair = links.slot()
    links.put(pair_out, pair_in, k_pair, ctx=2 * y + (1 - core))

    for dy in range(4):
        if dy == 0:
            @pl.when(t == 0)
            def _():
                pltpu.make_async_copy(wmix_ref, wbuf.at[0], weight_sem.at[0]).start()

            @pl.when(t != 0)
            def _():
                pltpu.make_async_remote_copy(
                    src_ref=wmix_ref, dst_ref=wbuf.at[t], send_sem=local_sems.at[1], recv_sem=weight_sem.at[t],
                    device_id={"tp": 0}, device_id_type=MESH,
                ).start()
        else:
            copy = pltpu.make_async_remote_copy(
                src_ref=wmix_ref, dst_ref=wbuf.at[t], send_sem=send_sems.at[links.n_send],
                recv_sem=weight_sem.at[t], device_id={"ctx": at_y(dy), "tp": (4 - dy) % 4}, device_id_type=MESH,
            )
            links.n_send += 1
            copy.start()
            links.started.append(copy)

    links.got(pair_in, k_pair)
    mine = info
    theirs = pair_in[:, FSL:]
    first = core == 0
    ibuf[r0, q0, 0:BLK] = jnp.where(first, mine, theirs)
    ibuf[r0, q0, BLK:] = jnp.where(first, theirs, mine)
    k_ifar = links.slot(3)
    for n, dz in enumerate(FAR):
        links.put(ibuf.at[r0, q0], ibuf.at[r0, q0], k_ifar + n, exp=at_z(dz))

    for dc in range(1, CTX):
        links.got(xbuf.at[dc], k_ctx + dc)
    entering, arriving = zero, zero
    for other in range(CTX):
        from_slot = lax.rem(c - other + CTX, CTX)
        entering = jnp.where(
            other < c, xbuf[from_slot, 0:NS] * entering + xbuf[from_slot, NS : 2 * NS], entering
        )
    for other in reversed(range(CTX)):
        from_slot = lax.rem(c - other + CTX, CTX)
        arriving = jnp.where(other > c, xbuf[from_slot, 0:NS] * arriving + xbuf[from_slot, 2 * NS :], arriving)

    def scan(i, carry):
        state, back = carry
        for j in range(BLK):
            up = i * BLK + j
            down = TOK - 1 - up
            kept = a_s[up] * state
            ap_s[up] = kept
            state = kept + inf_s[up]
            adjoint = adj_s[down] + back
            adj_s[down] = adjoint
            back = a_s[down] * adjoint
        return state, back

    lax.fori_loop(0, NBLK, scan, (entering, arriving))

    for n, dz in enumerate(FAR):
        links.got(ibuf.at[r0, lax.rem(q0 + 4 - dz // 4, 4)], k_ifar + n)
    k_inear = links.slot(3)
    for n, dz in enumerate(near):
        links.put(ibuf.at[r0], ibuf.at[r0], k_inear + n, exp=at_z(dz))

    rates = rates_ref[...]
    ones8 = jnp.where(iota((BLK, 128), 0) == lax.div(lane8, NS), 1.0, 0.0).astype(BF16)
    tok3, lane3 = iota((BLK, NS, 128), 0), iota((BLK, NS, 128), 2)
    skip = skip_ref[...]

    def gradients(i, carry):
        acc_in, acc_out, acc_decay = carry
        at = pl.ds(pl.multiple_of(i * BLK, BLK), BLK)
        adjoint, kept = adj_s[at], ap_s[at]
        states = (kept + inf_s[at]).reshape(128, CH).astype(BF16)
        adjoint_bf = adjoint.reshape(128, CH).astype(BF16)
        here = lane3 == tok3 + i * BLK
        acc_out += jnp.sum(jnp.where(here, nt(states, g_bf).reshape(BLK, NS, 128), 0.0), axis=0)
        acc_in += jnp.sum(jnp.where(here, nt(adjoint_bf, u_bf).reshape(BLK, NS, 128), 0.0), axis=0)
        through = mm(bsel[at, :].astype(BF16), adjoint_bf)
        product = adjoint * kept
        rated = mm(ones8, (product * rates[None]).reshape(128, CH).astype(BF16))
        step = step_ref[at, :]
        acc_decay += jnp.sum(product * step[:, None, :], axis=0)
        stepg_ref[at, :] = rated + xf[at, :] * through
        ssm_f[at, :] = skip * gf[at, :] + step * through
        return acc_in, acc_out, acc_decay

    acc_in, acc_out, acc_decay = lax.fori_loop(0, NBLK, gradients, (zero, zero, zero))

    ssm_bf = ssm_f[...].astype(BF16)
    ssm_ref[...] = ssm_bf
    sbuf[0, 0] = ssm_bf
    other_core = 2 * y + (1 - core)
    k_s = links.slot(2 * X)
    for dx in (2, 1, 3):
        links.put(sbuf.at[0, 0], sbuf.at[0, dx], k_s + dx, tp=at_x(dx))
    links.put(sbuf.at[0, 0], sbuf.at[1, 0], k_s + X, ctx=other_core)

    iop[0:2] = acc_in.reshape(2, 8, 128)
    iop[2:4] = acc_out.reshape(2, 8, 128)
    k_iox = links.slot(4)
    for dx in range(1, X):
        links.put(iop.at[at_x(dx)], iop_in.at[dx], k_iox + dx, tp=at_x(dx))
    dsp[0:NS] = acc_decay
    skip_part = jnp.sum(gf[...] * xf[...], axis=0, keepdims=True)
    dsp[NS:] = jnp.broadcast_to(skip_part, (BLK, CH))
    k_dsp = links.slot(CTX)
    for dc in range(1, CTX):
        links.put(dsp, dsp_in.at[dc], k_dsp + dc, ctx=lax.rem(c + dc, CTX))

    for n, dz in enumerate(near):
        links.got(ibuf.at[lax.rem(r0 + 16 - dz, 4)], k_inear + n)
    infos = ibuf[...].reshape(256, 128)
    e_f = e.astype(F32)
    hit0 = jnp.where(infos[:, 0:1] == e_f, 1.0, 0.0)
    hit1 = jnp.where(infos[:, 1:2] == e_f, 1.0, 0.0)
    hit = jnp.broadcast_to(hit0 + hit1, (256, 128))
    factor = hit0 * infos[:, 2:3] + hit1 * infos[:, 3:4]
    r256, l256 = iota((256, 256), 0), iota((256, 256), 1)
    before = jnp.where((lax.div(r256, BLK) == lax.div(l256, BLK)) & (r256 > l256), 1.0, 0.0).astype(BF16)
    position = mm(before, hit.astype(BF16))
    tok_row = iota((256, 128), 0)
    tok_r, tok_q = lax.div(tok_row, 64), lax.rem(lax.div(tok_row, 16), 4)
    tok_k = lax.rem(lax.div(tok_row, BLK), 2)
    tok_slot = (tok_k * Z + tok_q * 4 + tok_r) * CAP
    slot_of = tok_slot.astype(F32) + position
    picked = jnp.where(iota((256, 128), 1).astype(F32) == slot_of, hit, 0.0)
    sel_s[...] = picked.T.astype(BF16)
    own_scale = jnp.sum(picked * factor, axis=0, keepdims=True)[:, 0 : 2 * HALF]
    zeros96 = jnp.zeros((1, 2 * HALF), F32)
    scale_s[0] = jnp.concatenate([jnp.where(y == n, own_scale, zeros96) for n in range(Y)], axis=1)
    k_scale = links.slot(4)
    for dy in range(1, 4):
        links.put(scale_s.at[0], scale_in.at[dy], k_scale + dy, ctx=at_y(dy))

    for n in range(4):
        pltpu.make_async_copy(wbuf.at[n], wbuf.at[n], weight_sem.at[n]).wait()
    for dx in (1, 3, 2):
        links.got(sbuf.at[0, dx], k_s + dx)
        links.put(sbuf.at[0, dx], sbuf.at[1, dx], k_s + X + dx, ctx=other_core)
    for dx in (0, 1, 3, 2):
        links.got(sbuf.at[1, dx], k_s + X + dx)
    mixer = wbuf[...].reshape(4 * 128, FSL)
    parts = []
    for k in range(2):
        dk = lax.rem(core + k, 2)
        lhs = jnp.concatenate([sbuf[dk, lax.rem(t - n + 4, 4)] for n in range(4)], axis=1)
        parts.append(mm(lhs, mixer).reshape(Z, BLK, FSL))
    chunks = jnp.concatenate(parts, axis=1).astype(BF16)
    for n in range(Z):
        pbuf[n % 4, n // 4] = chunks[n]

    k_r1 = links.slot(3)
    for n, dz in enumerate(near):
        links.put(pbuf.at[lax.rem(r0 + dz, 4)], rbuf1.at[n], k_r1 + n, exp=at_z(dz))
    for dx in range(1, X):
        links.got(iop_in.at[dx], k_iox + dx)
    iop_far[0] = iop[t] + iop_in[1] + iop_in[2] + iop_in[3]
    k_iof = links.slot(4)
    for n, dz in enumerate(FAR):
        links.put(iop_far.at[0], iop_far.at[n + 1], k_iof + n, exp=at_z(dz))
    for n in range(3):
        links.got(rbuf1.at[n], k_r1 + n)
    summed = pbuf[r0].astype(F32)
    for n in range(3):
        summed += rbuf1[n].astype(F32)
    abuf[...] = summed.astype(BF16)
    k_r2 = links.slot(3)
    for n, dz in enumerate(FAR):
        links.put(abuf.at[lax.rem(q0 + dz // 4, 4)], rbuf2.at[n], k_r2 + n, exp=at_z(dz))
    own_resid = resid_ref[:, pl.ds(pl.multiple_of(fs * FSL, FSL), FSL)].astype(F32)
    their_resid = pair_in[:, 0:FSL]
    resid = jnp.concatenate(
        [jnp.where(first, own_resid, their_resid), jnp.where(first, their_resid, own_resid)], axis=0
    )
    for n in range(3):
        links.got(rbuf2.at[n], k_r2 + n)
    total = abuf[q0].astype(F32) + resid
    for n in range(3):
        total += rbuf2[n].astype(F32)

    gbuf[r0, q0] = total.astype(BF16)
    k_g1 = links.slot(3)
    for n, dz in enumerate(FAR):
        links.put(gbuf.at[r0, q0], gbuf.at[r0, q0], k_g1 + n, exp=at_z(dz))
    for n in range(3):
        links.got(iop_far.at[n + 1], k_iof + n)
    iop_near[0] = iop_far[0] + iop_far[1] + iop_far[2] + iop_far[3]
    for n, dz in enumerate(FAR):
        links.got(gbuf.at[r0, lax.rem(q0 + 4 - dz // 4, 4)], k_g1 + n)
    k_g2 = links.slot(3)
    for n, dz in enumerate(near):
        links.put(gbuf.at[r0], gbuf.at[r0], k_g2 + n, exp=at_z(dz))
    k_ion = links.slot(4)
    for n, dz in enumerate(near):
        links.put(iop_near.at[0], iop_near.at[n + 1], k_ion + n, exp=at_z(dz))
    for n, dz in enumerate(near):
        links.got(gbuf.at[lax.rem(r0 + 16 - dz, 4)], k_g2 + n)

    picked_rows = mm(sel_s[...], gbuf[...].reshape(256, FSL)).astype(BF16)
    rows[core, t, y, 0] = picked_rows[0:HALF]
    rows[core, t, y, 1] = picked_rows[HALF : 2 * HALF]
    k_p1 = links.slot(8)
    for d in (2, 1, 3):
        links.put(rows.at[core, t, y, 0], rows.at[core, t, y, 0], k_p1 + d, tp=at_x(d))
        links.put(rows.at[core, t, y, 1], rows.at[core, t, y, 1], k_p1 + 4 + d, ctx=at_y(d))
    for d in (1, 3, 2):
        links.got(rows.at[core, at_x(4 - d), y, 0], k_p1 + d)
        links.got(rows.at[core, t, lax.rem(y + 4 - d, 4), 1], k_p1 + 4 + d)

    def along_y(k, from_y, h):
        return rows.at[k, pl.ds(2 * h, 2), from_y, 0]

    def along_x(k, from_x, h):
        return rows.at[k, from_x, pl.ds(2 * h, 2), 1]

    def put_y(from_y, h, slot, dy):
        links.put(along_y(core, from_y, h), along_y(core, from_y, h), slot, ctx=at_y(dy))

    def put_x(from_x, h, slot, dx):
        links.put(along_x(core, from_x, h), along_x(core, from_x, h), slot, tp=at_x(dx))

    k_p2 = links.slot(12)
    for d, h, k in ((3, 0, 0), (1, 0, 2), (1, 1, 3), (2, 1, 5), (3, 1, 1)):
        put_y(y, h, k_p2 + k, d)
        put_x(t, h, k_p2 + 6 + k, d)
    k_core = links.slot(16)

    def to_core(d, h):
        from_y, from_x = lax.rem(y + 4 - d, 4), at_x(4 - d)
        links.put(along_y(core, from_y, h), along_y(core, from_y, h), k_core + 4 * d + h, ctx=other_core)
        links.put(along_x(core, from_x, h), along_x(core, from_x, h), k_core + 4 * d + 2 + h, ctx=other_core)

    to_core(0, 0)
    to_core(0, 1)

    for n in range(3):
        links.got(iop_near.at[n + 1], k_ion + n)
    iop_out = iop_near[0] + iop_near[1] + iop_near[2] + iop_near[3]
    iop_in[0] = iop_out
    k_ioa = links.slot(4)
    for dx in range(1, X):
        links.put(iop_in.at[0], iop_all.at[t], k_ioa + dx, tp=at_x(dx))
    for dc in range(1, CTX):
        links.got(dsp_in.at[dc], k_dsp + dc)
    sums = dsp[...]
    for dc in range(1, CTX):
        sums += dsp_in[dc]
    decg_ref[...] = sums[0:NS]
    skipg_ref[...] = sums[NS : NS + 1]
    for dy in range(1, 4):
        links.got(scale_in.at[dy], k_scale + dy)
    scale = scale_s[0] + scale_in[1] + scale_in[2] + scale_in[3]

    late_loads[0].wait()
    hidden = hidden_ref[...]
    hidden_scaled = (hidden.astype(F32) * scale).astype(BF16)
    for copy in late_loads[1:]:
        copy.wait()

    def got_2(d, h, k):
        links.got(along_y(core, lax.rem(y + 4 - d, 4), h), k_p2 + k)
        links.got(along_x(core, at_x(4 - d), h), k_p2 + 6 + k)

    got_2(3, 0, 0)
    put_y(lax.rem(y + 1, 4), 0, k_p2 + 4, 3)
    put_x(at_x(1), 0, k_p2 + 10, 3)
    to_core(3, 0)
    for d, h, k in ((1, 0, 2), (1, 1, 3), (3, 1, 1), (2, 1, 5), (2, 0, 4)):
        got_2(d, h, k)
        to_core(d, h)

    direct = jnp.zeros((hidden.shape[0], SLOTS), F32)
    down_stores = []
    for turn in range(2):
        k = core if turn == 0 else 1 - core
        if turn == 1:
            for d in (0, 3, 1, 2):
                for h in range(2):
                    from_y, from_x = lax.rem(y + 4 - d, 4), at_x(4 - d)
                    links.got(along_y(k, from_y, h), k_core + 4 * d + h)
                    links.got(along_x(k, from_x, h), k_core + 4 * d + 2 + h)
        for f in range(4):
            at = pl.ds(pl.multiple_of((2 * f + k) * FSL, FSL), FSL)
            part = jnp.concatenate([rows[k, (f - n) % 4, n].reshape(2 * HALF, FSL) for n in range(Y)], axis=0)
            direct += nt(w_s[:, at], part)
            down_ref[:, at] = mm(hidden_scaled, part).astype(BF16)
            down_stores.append(load(down_ref.at[:, at], down_hbm.at[:, at], 21 + 4 * turn + f))
    slot_ref[...] = (direct * scale).astype(BF16)
    tot[0] = jnp.sum(hidden.astype(F32) * direct, axis=0, keepdims=True)

    k_tx = links.slot(4)
    for dx in range(1, X):
        links.put(tot.at[0], tot_x.at[dx], k_tx + dx, tp=at_x(dx))
    for dx in range(1, X):
        links.got(iop_all.at[at_x(4 - dx)], k_ioa + dx)
    iop_all[t] = iop_out
    inpg_ref[...] = iop_all[0:2].reshape(NS, 128)
    outpg_ref[...] = iop_all[2:4].reshape(NS, 128)

    idx0, idx1 = jnp.broadcast_to(info[:, 0:1], (BLK, 128)), jnp.broadcast_to(info[:, 1:2], (BLK, 128))
    pos0, pos1 = jnp.zeros((BLK, 128), F32), jnp.zeros((BLK, 128), F32)
    for i in range(BLK):
        i0, i1 = idx0[i : i + 1], idx1[i : i + 1]
        pos0 += jnp.where((row8 > i) & ((i0 == idx0) | (i1 == idx0)), 1.0, 0.0)
        pos1 += jnp.where((row8 > i) & ((i0 == idx1) | (i1 == idx1)), 1.0, 0.0)
    lane384 = iota((BLK, SLOTS), 1).astype(F32)
    base = ((c * Z + e) * CAP).astype(F32)

    for dx in range(1, X):
        links.got(tot_x.at[dx], k_tx + dx)
    tot_c[0] = tot[0] + tot_x[1] + tot_x[2] + tot_x[3]
    k_tc = links.slot(CTX)
    for dc in range(1, CTX):
        links.put(tot_c.at[0], tot_c.at[dc], k_tc + dc, ctx=lax.rem(c + dc, CTX))
    for dc in range(1, CTX):
        links.got(tot_c.at[dc], k_tc + dc)
    plane = tot_c[0]
    for dc in range(1, CTX):
        plane += tot_c[dc]
    tot_z[0] = plane
    k_tz = links.slot(Z)
    for dz in range(1, Z):
        links.put(tot_z.at[0], tot_z.at[dz], k_tz + dz, exp=at_z(dz))
    for dz in range(1, Z):
        links.got(tot_z.at[dz], k_tz + dz)
    val0, val1 = jnp.zeros((BLK, SLOTS), F32), jnp.zeros((BLK, SLOTS), F32)
    for dz in range(Z):
        expert = at_z(Z - dz).astype(F32)
        line = jnp.broadcast_to(tot_z[dz], (BLK, SLOTS))
        val0 = jnp.where(info[:, 0:1] == expert, line, val0)
        val1 = jnp.where(info[:, 1:2] == expert, line, val1)
    out0 = jnp.sum(jnp.where(lane384 == base + pos0[:, 0:1], val0, 0.0), axis=1, keepdims=True)
    out1 = jnp.sum(jnp.where(lane384 == base + pos1[:, 0:1], val1, 0.0), axis=1, keepdims=True)
    diagonal = row8 == lane8
    probg_ref[0:1, :] = jnp.sum(jnp.where(diagonal, out0, 0.0), axis=0, keepdims=True)[:, 0:BLK]
    probg_ref[1:2, :] = jnp.sum(jnp.where(diagonal, out1, 0.0), axis=0, keepdims=True)[:, 0:BLK]

    @pl.when(t != 0)
    def _():
        pltpu.make_async_copy(wmix_ref, wbuf.at[0], local_sems.at[1]).wait()

    for copy in down_stores:
        copy.wait()
    links.drain()


def store(*refs):
    ins, outs, held, sems = refs[:9], refs[9:18], refs[18:27], refs[27]
    steps = list(zip(ins, held, outs))
    big = steps.pop(7)
    steps += [[ref.at[pl.ds(n * 32, 32)] for ref in big] for n in range(7)]
    loads = [pltpu.make_async_copy(src, mid, sems.at[0, n]) for n, (src, mid, _) in enumerate(steps)]
    stores = [pltpu.make_async_copy(mid, dst, sems.at[1, n]) for n, (_, mid, dst) in enumerate(steps)]
    for copy in loads:
        copy.start()
    for load, save in zip(loads, stores):
        load.wait()
        save.start()
    for copy in stores:
        copy.wait()


def shards(
    mixer_input, step_sizes, decay_rates, input_proj, output_proj, skip_gain, doc_starts, ssm_grad, mixer_in_weight,
    residual_grad, expert_index_pairs, route_probs, hidden_saved, down_weight,
):
    hidden = hidden_saved[0].shape[0]
    features = down_weight.shape[2]
    vmem = pl.BlockSpec(memory_space=pltpu.VMEM)
    anywhere = pl.BlockSpec(memory_space=pl.ANY)
    hbm = pl.BlockSpec(memory_space=pltpu.HBM)
    shape = jax.ShapeDtypeStruct
    out = pl.pallas_call(
        body,
        out_shape=(
            shape((TOK, CH), BF16),
            shape((TOK, CH), F32),
            shape((NS, TOK), F32),
            shape((NS, TOK), F32),
            shape((NS, CH), F32),
            shape((1, CH), F32),
            shape((hidden, SLOTS), BF16),
            shape((hidden, features), BF16),
            shape((2, BLK), F32),
        ),
        in_specs=[hbm] * 14,
        out_specs=(vmem,) * 7 + (hbm, vmem),
        scratch_shapes=[
            pltpu.VMEM((TOK, CH), BF16),
            pltpu.VMEM((TOK, CH), F32),
            pltpu.VMEM((NS, CH), F32),
            pltpu.VMEM((NS, TOK), F32),
            pltpu.VMEM((NS, TOK), F32),
            pltpu.VMEM((1, CH), F32),
            pltpu.SMEM((TOK,), jnp.int32),
            pltpu.VMEM((TOK, CH), BF16),
            pltpu.VMEM((BLK, features), BF16),
            pltpu.SMEM((2, BLK), jnp.int32),
            pltpu.SMEM((2, BLK), F32),
            pltpu.VMEM((hidden, SLOTS), BF16),
            pltpu.VMEM((hidden, features), BF16),
            pltpu.VMEM((TOK, CH), F32),
            pltpu.VMEM((TOK, CH), F32),
            pltpu.VMEM((TOK, NS, CH), F32),
            pltpu.VMEM((TOK, NS, CH), F32),
            pltpu.VMEM((TOK, NS, CH), F32),
            pltpu.VMEM((TOK, NS, CH), F32),
            pltpu.VMEM((128, 128), F32),
            pltpu.VMEM((TOK, CH), F32),
            pltpu.VMEM((CTX, 3 * NS, CH), F32),
            pltpu.VMEM((2, X, TOK, CH), BF16),
            pltpu.VMEM((4, 128, FSL), BF16),
            pltpu.VMEM((4, 4, 16, FSL), BF16),
            pltpu.VMEM((3, 4, 16, FSL), BF16),
            pltpu.VMEM((4, 16, FSL), BF16),
            pltpu.VMEM((3, 16, FSL), BF16),
            pltpu.VMEM((4, 4, 16, FSL), BF16),
            pltpu.VMEM((4, 4, 16, 128), F32),
            pltpu.VMEM((BLK, FSL + 128), F32),
            pltpu.VMEM((BLK, FSL + 128), F32),
            pltpu.VMEM((128, 256), BF16),
            pltpu.VMEM((1, 1, SLOTS), F32),
            pltpu.VMEM((4, 1, SLOTS), F32),
            pltpu.VMEM((2, X, Y, 2, HALF, FSL), BF16),
            pltpu.VMEM((hidden, features), BF16),
            pltpu.VMEM((4, 8, 128), F32),
            pltpu.VMEM((4, 8, 128), F32),
            pltpu.VMEM((4, 8, 128), F32),
            pltpu.VMEM((4, 8, 128), F32),
            pltpu.VMEM((4, 8, 128), F32),
            pltpu.VMEM((NS + BLK, CH), F32),
            pltpu.VMEM((CTX, NS + BLK, CH), F32),
            pltpu.VMEM((1, 1, SLOTS), F32),
            pltpu.VMEM((4, 1, SLOTS), F32),
            pltpu.VMEM((CTX, 1, SLOTS), F32),
            pltpu.VMEM((Z, 1, SLOTS), F32),
            pltpu.SemaphoreType.DMA((NSEM,)),
            pltpu.SemaphoreType.DMA((NSEM,)),
            pltpu.SemaphoreType.DMA((32,)),
            pltpu.SemaphoreType.DMA((4,)),
        ],
        compiler_params=pltpu.CompilerParams(
            collective_id=0, has_side_effects=True, vmem_limit_bytes=VMEM_LIMIT
        ),
        name="scan_and_experts",
    )(
        mixer_input, step_sizes, decay_rates, input_proj, output_proj, skip_gain.reshape(1, CH), doc_starts, ssm_grad,
        mixer_in_weight, residual_grad, expert_index_pairs.T, route_probs.T, hidden_saved[0], down_weight[0],
    )
    ssm, stepg, inpg, outpg, decg, skipg, slot, down, probg = pl.pallas_call(
        store,
        out_shape=tuple(shape(array.shape, array.dtype) for array in out),
        in_specs=[anywhere] * 9,
        out_specs=tuple([hbm] * 9),
        scratch_shapes=[pltpu.VMEM(array.shape, array.dtype) for array in out] + [pltpu.SemaphoreType.DMA((2, 16))],
        compiler_params=pltpu.CompilerParams(vmem_limit_bytes=VMEM_LIMIT),
        name="store_results",
    )(*out)
    return ssm, stepg, inpg, outpg, decg, skipg.reshape(CH), slot[None], down[None], probg.T


def solution(mesh):
    return jax.shard_map(
        shards,
        mesh=mesh,
        in_specs=(
            P("ctx", ("exp", "tp")),
            P("ctx", ("exp", "tp")),
            P(None, ("exp", "tp")),
            P(None, "ctx"),
            P(None, "ctx"),
            P(("exp", "tp")),
            P("ctx"),
            P("ctx", ("exp", "tp")),
            P(("exp", "tp"), "ctx"),
            P(("ctx", "exp"), None),
            P(("ctx", "exp"), None),
            P(("ctx", "exp"), None),
            P("exp", ("ctx", "tp"), None),
            P("exp", ("ctx", "tp"), None),
        ),
        out_specs=(
            P("ctx", ("exp", "tp")),
            P("ctx", ("exp", "tp")),
            P(None, "ctx"),
            P(None, "ctx"),
            P(None, ("exp", "tp")),
            P(("exp", "tp")),
            P("exp", ("ctx", "tp"), None),
            P("exp", ("ctx", "tp"), None),
            P(("ctx", "exp"), None),
        ),
        check_vma=False,
    )
```

```python
import jax
import jax.numpy as jnp
from jax import lax
from jax.experimental import pallas as pl
from jax.experimental.pallas import tpu as pltpu
from jax.sharding import PartitionSpec as P

F32 = jnp.float32
BF16 = jnp.bfloat16
MESH = pl.DeviceIdType.MESH

TOK = 128
CH = 128
NS = 16
BLK = 8
NBLK = TOK // BLK
Y, CORES, Z, X = 4, 2, 16, 4
CTX = Y * CORES
FSL = 512
CAP = 3
HALF = Z * CAP
SLOTS = CTX * HALF
FAR = (4, 12, 8)


def nt(a, b):
    return lax.dot_general(a, b, (((1,), (1,)), ((), ())), preferred_element_type=F32)


def mm(a, b):
    return jnp.dot(a, b, preferred_element_type=F32)


def iota(shape, dim):
    return lax.broadcasted_iota(jnp.int32, shape, dim)


class Links:
    def __init__(self, send, recv):
        self.send, self.recv = send, recv
        self.n_send = self.n_recv = 0
        self.started = []

    def slot(self, n=1):
        first = self.n_recv
        self.n_recv += n
        assert self.n_recv <= NSEM
        return first

    def put(self, src, dst, recv_index, **device):
        copy = pltpu.make_async_remote_copy(
            src_ref=src,
            dst_ref=dst,
            send_sem=self.send.at[self.n_send],
            recv_sem=self.recv.at[recv_index],
            device_id=device,
            device_id_type=MESH,
        )
        self.n_send += 1
        assert self.n_send <= NSEM
        copy.start()
        self.started.append(copy)
        return copy

    def got(self, dst, recv_index):
        pltpu.make_async_copy(dst, dst, self.recv.at[recv_index]).wait()

    def drain(self):
        for copy in self.started:
            copy.wait_send()
        self.started = []


NSEM = 192
VMEM_LIMIT = 60 * 1024 * 1024


def body(
    x_hbm, step_hbm, rates_hbm, inp_hbm, outp_hbm, skip_hbm, doc_hbm, g_hbm, wmix_ref, resid_hbm,
    idx_hbm, prob_hbm, hidden_hbm, weight_ref,
    ssm_hbm, stepg_hbm, inpg_hbm, outpg_hbm, decg_hbm, skipg_hbm, slot_hbm, down_hbm, probg_hbm,
    x_ref, step_ref, rates_ref, inp_ref, outp_ref, skip_ref, doc_ref, g_ref, resid_ref, idx_ref, prob_ref, hidden_ref, down_ref,
    stepg_ref, inpg_ref, outpg_ref, decg_ref, skipg_ref, slot_ref, probg_ref,
    gs, g0, g1x, g1y, a1, b1, g2a, g2b,
    xf, gf, a_s, inf_s, adj_s, ap_s, bsel, ssm_f, xbuf, sbuf, wbuf, pbuf, rbuf1, abuf, rbuf2,
    gbuf, ibuf, pair_out, pair_in, sel_s, scale_s, scale_in, rows, w_s,
    iop, iop_in, iop_far, iop_near, iop_all, dsp, dsp_in, tot_p, tot_z,
    send_sems, recv_sems, local_sems, weight_sem,
):
    links = Links(send_sems, recv_sems)
    c, e, t = lax.axis_index("ctx"), lax.axis_index("exp"), lax.axis_index("tp")
    y, core = lax.div(c, 2), lax.rem(c, 2)
    r0, q0 = lax.rem(e, 4), lax.div(e, 4)
    fs = 2 * lax.rem(t + y, 4) + core

    def at_y(dy):
        return 2 * lax.rem(y + dy, 4) + core

    def at_x(dx):
        return lax.rem(t + dx, 4)

    def at_z(dz):
        return lax.rem(e + dz, Z)

    barrier = pltpu.get_barrier_semaphore()
    partners = 0
    for dc in range(CTX):
        for dx in range(X):
            if dc or dx:
                pl.semaphore_signal(
                    barrier, inc=1, device_id={"ctx": lax.rem(c + dc, CTX), "tp": at_x(dx)}, device_id_type=MESH
                )
                partners += 1
    for dz in range(1, Z):
        pl.semaphore_signal(barrier, inc=1, device_id={"exp": at_z(dz)}, device_id_type=MESH)
        partners += 1

    def load(src, dst, at):
        copy = pltpu.make_async_copy(src, dst, local_sems.at[at])
        copy.start()
        return copy

    scan_loads = [
        load(src, dst, 2 + n)
        for n, (src, dst) in enumerate((
            (step_hbm, step_ref), (rates_hbm, rates_ref), (x_hbm, x_ref), (g_hbm, g_ref), (inp_hbm, inp_ref),
            (outp_hbm, outp_ref), (doc_hbm, doc_ref), (skip_hbm, skip_ref), (idx_hbm, idx_ref),
            (prob_hbm, prob_ref), (resid_hbm, resid_ref),
        ))
    ]
    late_loads = [load(hidden_hbm, hidden_ref, 13)]
    for n in range(7):
        part = pl.ds(n * 32, 32)
        late_loads.append(load(weight_ref.at[part], w_s.at[part], 14 + n))
    near = (1, 15, 2 + 12 * core)
    for copy in scan_loads:
        copy.wait()

    lane8 = iota((BLK, 128), 1)
    row8 = iota((BLK, 128), 0)
    info = jnp.zeros((BLK, 128), F32)
    for i in range(BLK):
        for k in range(2):
            info = jnp.where((row8 == i) & (lane8 == k), idx_ref[k, i].astype(F32), info)
            info = jnp.where((row8 == i) & (lane8 == 2 + k), prob_ref[k, i], info)
    info = info.astype(BF16).astype(F32)
    other_fs = 2 * lax.rem(t + y, 4) + (1 - core)
    pair_out[:, 0:FSL] = resid_ref[:, pl.ds(pl.multiple_of(other_fs * FSL, FSL), FSL)].astype(F32)
    pair_out[:, FSL:] = info
    xf[...] = x_ref[...].astype(F32)
    gf[...] = g_ref[...].astype(F32)
    g_bf = g_ref[...]
    u_bf = (step_ref[...] * xf[...]).astype(BF16)
    row, lane = iota((128, 128), 0), iota((128, 128), 1)
    b_tile = jnp.concatenate([inp_ref[...]] * BLK, axis=0)
    c_tile = jnp.concatenate([outp_ref[...]] * BLK, axis=0)
    bsel[...] = jnp.where(lax.rem(row, BLK) == lax.div(lane, NS), b_tile.T, 0.0)
    row_tok = lax.div(row, NS)

    def prepare(i, carry):
        at = pl.ds(pl.multiple_of(i * BLK, BLK), BLK)
        here = lane == row_tok + i * BLK
        decays = jnp.exp(step_ref[at, :][:, None, :] * rates_ref[...][None])
        for j in range(BLK):
            keep = (1 - doc_ref[i * BLK + j]).astype(F32)
            a_s[i * BLK + j] = decays[j] * keep
        inf_s[at] = mm(jnp.where(here, b_tile, 0.0).astype(BF16), u_bf).reshape(BLK, NS, CH)
        adj_s[at] = mm(jnp.where(here, c_tile, 0.0).astype(BF16), g_bf).reshape(BLK, NS, CH)
        return carry

    lax.fori_loop(0, NBLK, prepare, 0)

    zero = jnp.zeros((NS, CH), F32)

    def summarise(i, carry):
        state, back, damp = carry
        for j in range(BLK):
            up = i * BLK + j
            down = TOK - 1 - up
            decay = a_s[up]
            state = decay * state + inf_s[up]
            damp = damp * decay
            back = a_s[down] * (adj_s[down] + back)
        return state, back, damp

    state, back, damp = lax.fori_loop(0, NBLK, summarise, (zero, zero, zero + 1.0))
    xbuf[0, 0:NS] = damp
    xbuf[0, NS : 2 * NS] = state
    xbuf[0, 2 * NS :] = back
    for copy in late_loads:
        copy.wait()
    hidden_t = hidden_ref[...].T
    for k in range(2):
        for f in range(4):
            part = mm(hidden_t, w_s[:, pl.ds((2 * f + k) * FSL, FSL)]).astype(BF16).reshape(Y, 2, HALF, FSL)
            for n in range(Y):
                gs[k, (f - n) % 4, n] = part[n]

    pl.semaphore_wait(barrier, partners)
    k_ctx = links.slot(CTX)
    for dc in range(1, CTX):
        links.put(xbuf.at[0], xbuf.at[dc], k_ctx + dc, ctx=lax.rem(c + dc, CTX))

    k_pair = links.slot()
    links.put(pair_out, pair_in, k_pair, ctx=2 * y + (1 - core))

    for dy in range(4):
        if dy == 0:
            @pl.when(t == 0)
            def _():
                pltpu.make_async_copy(wmix_ref, wbuf.at[0], weight_sem.at[0]).start()

            @pl.when(t != 0)
            def _():
                pltpu.make_async_remote_copy(
                    src_ref=wmix_ref, dst_ref=wbuf.at[t], send_sem=local_sems.at[1], recv_sem=weight_sem.at[t],
                    device_id={"tp": 0}, device_id_type=MESH,
                ).start()
        else:
            copy = pltpu.make_async_remote_copy(
                src_ref=wmix_ref, dst_ref=wbuf.at[t], send_sem=send_sems.at[links.n_send],
                recv_sem=weight_sem.at[t], device_id={"ctx": at_y(dy), "tp": (4 - dy) % 4}, device_id_type=MESH,
            )
            links.n_send += 1
            copy.start()
            links.started.append(copy)

    other_core = 2 * y + (1 - core)
    k_g0 = links.slot(8)
    for n in range(X):
        for h in range(2):
            half = pl.ds(2 * h, 2)
            links.put(gs.at[1 - core, n, half], g0.at[n, half], k_g0 + 2 * n + h, ctx=other_core)

    links.got(pair_in, k_pair)
    mine = info
    theirs = pair_in[:, FSL:]
    first = core == 0
    ibuf[r0, q0, 0:BLK] = jnp.where(first, mine, theirs)
    ibuf[r0, q0, BLK:] = jnp.where(first, theirs, mine)
    k_ifar = links.slot(3)
    for n, dz in enumerate(FAR):
        links.put(ibuf.at[r0, q0], ibuf.at[r0, q0], k_ifar + n, exp=at_z(dz))

    for dc in range(1, CTX):
        links.got(xbuf.at[dc], k_ctx + dc)
    entering, arriving = zero, zero
    for other in range(CTX):
        from_slot = lax.rem(c - other + CTX, CTX)
        entering = jnp.where(
            other < c, xbuf[from_slot, 0:NS] * entering + xbuf[from_slot, NS : 2 * NS], entering
        )
    for other in reversed(range(CTX)):
        from_slot = lax.rem(c - other + CTX, CTX)
        arriving = jnp.where(other > c, xbuf[from_slot, 0:NS] * arriving + xbuf[from_slot, 2 * NS :], arriving)

    def scan(i, carry):
        state, back = carry
        for j in range(BLK):
            up = i * BLK + j
            down = TOK - 1 - up
            kept = a_s[up] * state
            ap_s[up] = kept
            state = kept + inf_s[up]
            adjoint = adj_s[down] + back
            adj_s[down] = adjoint
            back = a_s[down] * adjoint
        return state, back

    lax.fori_loop(0, NBLK, scan, (entering, arriving))

    for n, dz in enumerate(FAR):
        links.got(ibuf.at[r0, lax.rem(q0 + 4 - dz // 4, 4)], k_ifar + n)
    k_inear = links.slot(3)
    for n, dz in enumerate(near):
        links.put(ibuf.at[r0], ibuf.at[r0], k_inear + n, exp=at_z(dz))

    rates = rates_ref[...]
    ones8 = jnp.where(iota((BLK, 128), 0) == lax.div(lane8, NS), 1.0, 0.0).astype(BF16)
    tok3, lane3 = iota((BLK, NS, 128), 0), iota((BLK, NS, 128), 2)
    skip = skip_ref[...]

    def gradients(i, carry):
        acc_in, acc_out, acc_decay = carry
        at = pl.ds(pl.multiple_of(i * BLK, BLK), BLK)
        adjoint, kept = adj_s[at], ap_s[at]
        states = (kept + inf_s[at]).reshape(128, CH).astype(BF16)
        adjoint_bf = adjoint.reshape(128, CH).astype(BF16)
        here = lane3 == tok3 + i * BLK
        acc_out += jnp.sum(jnp.where(here, nt(states, g_bf).reshape(BLK, NS, 128), 0.0), axis=0)
        acc_in += jnp.sum(jnp.where(here, nt(adjoint_bf, u_bf).reshape(BLK, NS, 128), 0.0), axis=0)
        through = mm(bsel[at, :].astype(BF16), adjoint_bf)
        product = adjoint * kept
        rated = mm(ones8, (product * rates[None]).reshape(128, CH).astype(BF16))
        step = step_ref[at, :]
        acc_decay += jnp.sum(product * step[:, None, :], axis=0)
        stepg_ref[at, :] = rated + xf[at, :] * through
        ssm_f[at, :] = skip * gf[at, :] + step * through
        return acc_in, acc_out, acc_decay

    acc_in, acc_out, acc_decay = lax.fori_loop(0, NBLK, gradients, (zero, zero, zero))

    ssm_bf = ssm_f[...].astype(BF16)
    sbuf[0, 0] = ssm_bf
    stores = [load(sbuf.at[0, 0], ssm_hbm, 29), load(stepg_ref, stepg_hbm, 30)]
    k_s = links.slot(2 * X)
    for dx in (2, 1, 3):
        links.put(sbuf.at[0, 0], sbuf.at[0, dx], k_s + dx, tp=at_x(dx))
    links.put(sbuf.at[0, 0], sbuf.at[1, 0], k_s + X, ctx=other_core)

    iop[0:2] = acc_in.reshape(2, 8, 128)
    iop[2:4] = acc_out.reshape(2, 8, 128)
    k_iox = links.slot(4)
    for dx in range(1, X):
        links.put(iop.at[at_x(dx)], iop_in.at[dx], k_iox + dx, tp=at_x(dx))
    dsp[0:NS] = acc_decay
    skip_part = jnp.sum(gf[...] * xf[...], axis=0, keepdims=True)
    dsp[NS:] = jnp.broadcast_to(skip_part, (BLK, CH))
    k_dsp = links.slot(CTX)
    for dc in range(1, CTX):
        links.put(dsp, dsp_in.at[dc], k_dsp + dc, ctx=lax.rem(c + dc, CTX))

    for n, dz in enumerate(near):
        links.got(ibuf.at[lax.rem(r0 + 16 - dz, 4)], k_inear + n)
    infos = ibuf[...].reshape(256, 128)
    e_f = e.astype(F32)
    hit0 = jnp.where(infos[:, 0:1] == e_f, 1.0, 0.0)
    hit1 = jnp.where(infos[:, 1:2] == e_f, 1.0, 0.0)
    hit = jnp.broadcast_to(hit0 + hit1, (256, 128))
    factor = hit0 * infos[:, 2:3] + hit1 * infos[:, 3:4]
    r256, l256 = iota((256, 256), 0), iota((256, 256), 1)
    before = jnp.where((lax.div(r256, BLK) == lax.div(l256, BLK)) & (r256 > l256), 1.0, 0.0).astype(BF16)
    position = mm(before, hit.astype(BF16))
    tok_row = iota((256, 128), 0)
    tok_r, tok_q = lax.div(tok_row, 64), lax.rem(lax.div(tok_row, 16), 4)
    tok_k = lax.rem(lax.div(tok_row, BLK), 2)
    tok_slot = (tok_k * Z + tok_q * 4 + tok_r) * CAP
    slot_of = tok_slot.astype(F32) + position
    picked = jnp.where(iota((256, 128), 1).astype(F32) == slot_of, hit, 0.0)
    sel_s[...] = picked.T.astype(BF16)
    own_scale = jnp.sum(picked * factor, axis=0, keepdims=True)[:, 0 : 2 * HALF]
    zeros96 = jnp.zeros((1, 2 * HALF), F32)
    scale_s[0] = jnp.concatenate([jnp.where(y == n, own_scale, zeros96) for n in range(Y)], axis=1)
    k_scale = links.slot(4)
    for dy in range(1, 4):
        links.put(scale_s.at[0], scale_in.at[dy], k_scale + dy, ctx=at_y(dy))

    for n in range(X):
        for h in range(2):
            links.got(g0.at[n, pl.ds(2 * h, 2)], k_g0 + 2 * n + h)
        gs[core, n] = (gs[core, n].astype(F32) + g0[n].astype(F32)).astype(BF16)

    for n in range(4):
        pltpu.make_async_copy(wbuf.at[n], wbuf.at[n], weight_sem.at[n]).wait()
    for dx in (1, 3, 2):
        links.got(sbuf.at[0, dx], k_s + dx)
        links.put(sbuf.at[0, dx], sbuf.at[1, dx], k_s + X + dx, ctx=other_core)
    for dx in (0, 1, 3, 2):
        links.got(sbuf.at[1, dx], k_s + X + dx)
    k_g1 = links.slot(8)
    for d in (2, 1, 3):
        links.put(gs.at[core, at_x(d), :, 0], g1x.at[d], k_g1 + d, tp=at_x(d))
        links.put(gs.at[core, :, lax.rem(y + d, 4), 1], g1y.at[d], k_g1 + 4 + d, ctx=at_y(d))
    mixer = wbuf[...].reshape(4 * 128, FSL)
    parts = []
    for k in range(2):
        dk = lax.rem(core + k, 2)
        lhs = jnp.concatenate([sbuf[dk, lax.rem(t - n + 4, 4)] for n in range(4)], axis=1)
        parts.append(mm(lhs, mixer).reshape(Z, BLK, FSL))
    chunks = jnp.concatenate(parts, axis=1).astype(BF16)
    for n in range(Z):
        pbuf[n % 4, n // 4] = chunks[n]

    k_r1 = links.slot(3)
    for n, dz in enumerate(near):
        links.put(pbuf.at[lax.rem(r0 + dz, 4)], rbuf1.at[n], k_r1 + n, exp=at_z(dz))
    for dx in range(1, X):
        links.got(iop_in.at[dx], k_iox + dx)
    iop_far[0] = iop[t] + iop_in[1] + iop_in[2] + iop_in[3]
    k_iof = links.slot(4)
    for n, dz in enumerate(FAR):
        links.put(iop_far.at[0], iop_far.at[n + 1], k_iof + n, exp=at_z(dz))
    for n in range(3):
        links.got(rbuf1.at[n], k_r1 + n)
    summed = pbuf[r0].astype(F32)
    for n in range(3):
        summed += rbuf1[n].astype(F32)
    abuf[...] = summed.astype(BF16)
    k_r2 = links.slot(3)
    for n, dz in enumerate(FAR):
        links.put(abuf.at[lax.rem(q0 + dz // 4, 4)], rbuf2.at[n], k_r2 + n, exp=at_z(dz))
    own_resid = resid_ref[:, pl.ds(pl.multiple_of(fs * FSL, FSL), FSL)].astype(F32)
    their_resid = pair_in[:, 0:FSL]
    resid = jnp.concatenate(
        [jnp.where(first, own_resid, their_resid), jnp.where(first, their_resid, own_resid)], axis=0
    )
    for n in range(3):
        links.got(rbuf2.at[n], k_r2 + n)
    total = abuf[q0].astype(F32) + resid
    for n in range(3):
        total += rbuf2[n].astype(F32)

    gbuf[r0, q0] = total.astype(BF16)
    k_a1 = links.slot(3)
    for n, dz in enumerate(FAR):
        links.put(gbuf.at[r0, q0], gbuf.at[r0, q0], k_a1 + n, exp=at_z(dz))
    for d in (1, 3, 2):
        links.got(g1x.at[d], k_g1 + d)
        links.got(g1y.at[d], k_g1 + 4 + d)
    for n in range(4):
        over_x, over_y = gs[core, t, n, 0].astype(F32), gs[core, n, y, 1].astype(F32)
        for d in range(1, 4):
            over_x += g1x[d, n].astype(F32)
            over_y += g1y[d, n].astype(F32)
        a1[n] = over_x.astype(BF16)
        b1[n] = over_y.astype(BF16)
    k_g2 = links.slot(8)
    for d in (2, 1, 3):
        links.put(a1.at[lax.rem(y + d, 4)], g2a.at[d], k_g2 + d, ctx=at_y(d))
        links.put(b1.at[at_x(d)], g2b.at[d], k_g2 + 4 + d, tp=at_x(d))
    for n in range(3):
        links.got(iop_far.at[n + 1], k_iof + n)
    iop_near[0] = iop_far[0] + iop_far[1] + iop_far[2] + iop_far[3]
    for n, dz in enumerate(FAR):
        links.got(gbuf.at[r0, lax.rem(q0 + 4 - dz // 4, 4)], k_a1 + n)
    k_a2 = links.slot(3)
    for n, dz in enumerate(near):
        links.put(gbuf.at[r0], gbuf.at[r0], k_a2 + n, exp=at_z(dz))
    k_ion = links.slot(4)
    for n, dz in enumerate(near):
        links.put(iop_near.at[0], iop_near.at[n + 1], k_ion + n, exp=at_z(dz))
    for d in (1, 3, 2):
        links.got(g2a.at[d], k_g2 + d)
        links.got(g2b.at[d], k_g2 + 4 + d)
    weight_low, weight_high = a1[y].astype(F32), b1[t].astype(F32)
    for d in range(1, 4):
        weight_low += g2a[d].astype(F32)
        weight_high += g2b[d].astype(F32)
    for n, dz in enumerate(near):
        links.got(gbuf.at[lax.rem(r0 + 16 - dz, 4)], k_a2 + n)

    picked_rows = mm(sel_s[...], gbuf[...].reshape(256, FSL)).astype(BF16)
    rows[core, t, y, 0] = picked_rows[0:HALF]
    rows[core, t, y, 1] = picked_rows[HALF : 2 * HALF]
    k_p1 = links.slot(8)
    for d in (2, 1, 3):
        links.put(rows.at[core, t, y, 0], rows.at[core, t, y, 0], k_p1 + d, tp=at_x(d))
        links.put(rows.at[core, t, y, 1], rows.at[core, t, y, 1], k_p1 + 4 + d, ctx=at_y(d))
    product = jnp.concatenate(
        [
            picked_rows[0:HALF].astype(F32) * weight_low,
            picked_rows[HALF : 2 * HALF].astype(F32) * weight_high,
            jnp.zeros((128 - 2 * HALF, FSL), F32),
        ],
        axis=0,
    )
    high = product.astype(BF16)
    low = (product - high.astype(F32)).astype(BF16)
    ones = jnp.ones((BLK, FSL), BF16)
    tot_p[0] = nt(ones, high) + nt(ones, low)
    k_tp = links.slot(2 * X)
    for dk in range(2):
        for dx in range(X):
            if dk or dx:
                links.put(
                    tot_p.at[0], tot_p.at[dk * X + dx], k_tp + dk * X + dx,
                    ctx=2 * y + lax.rem(core + dk, 2), tp=at_x(dx),
                )
    for d in (1, 3, 2):
        links.got(rows.at[core, at_x(4 - d), y, 0], k_p1 + d)
        links.got(rows.at[core, t, lax.rem(y + 4 - d, 4), 1], k_p1 + 4 + d)

    def along_y(k, from_y, h):
        return rows.at[k, pl.ds(2 * h, 2), from_y, 0]

    def along_x(k, from_x, h):
        return rows.at[k, from_x, pl.ds(2 * h, 2), 1]

    def put_y(from_y, h, slot, dy):
        links.put(along_y(core, from_y, h), along_y(core, from_y, h), slot, ctx=at_y(dy))

    def put_x(from_x, h, slot, dx):
        links.put(along_x(core, from_x, h), along_x(core, from_x, h), slot, tp=at_x(dx))

    k_p2 = links.slot(12)
    for d, h, k in ((3, 0, 0), (1, 0, 2), (1, 1, 3), (2, 1, 5), (3, 1, 1)):
        put_y(y, h, k_p2 + k, d)
        put_x(t, h, k_p2 + 6 + k, d)
    k_core = links.slot(16)

    def to_core(d, h):
        from_y, from_x = lax.rem(y + 4 - d, 4), at_x(4 - d)
        links.put(along_y(core, from_y, h), along_y(core, from_y, h), k_core + 4 * d + h, ctx=other_core)
        links.put(along_x(core, from_x, h), along_x(core, from_x, h), k_core + 4 * d + 2 + h, ctx=other_core)

    to_core(0, 0)
    to_core(0, 1)
    for n in range(1, 2 * X):
        links.got(tot_p.at[n], k_tp + n)
    slot_total = tot_p[0]
    for n in range(1, 2 * X):
        slot_total += tot_p[n]
    tot_z[0] = slot_total
    k_tz = links.slot(Z)
    for dz in range(1, Z):
        links.put(tot_z.at[0], tot_z.at[dz], k_tz + dz, exp=at_z(dz))

    for n in range(3):
        links.got(iop_near.at[n + 1], k_ion + n)
    iop_out = iop_near[0] + iop_near[1] + iop_near[2] + iop_near[3]
    iop_in[0] = iop_out
    k_ioa = links.slot(4)
    for dx in range(1, X):
        links.put(iop_in.at[0], iop_all.at[t], k_ioa + dx, tp=at_x(dx))
    for dc in range(1, CTX):
        links.got(dsp_in.at[dc], k_dsp + dc)
    sums = dsp[...]
    for dc in range(1, CTX):
        sums += dsp_in[dc]
    decg_ref[...] = sums[0:NS]
    skipg_ref[...] = sums[NS : NS + 1]
    stores += [load(decg_ref, decg_hbm, 31), load(skipg_ref, skipg_hbm, 32)]
    for dy in range(1, 4):
        links.got(scale_in.at[dy], k_scale + dy)
    scale = scale_s[0] + scale_in[1] + scale_in[2] + scale_in[3]

    hidden = hidden_ref[...]
    hidden_scaled = (hidden.astype(F32) * scale).astype(BF16)
    def got_2(d, h, k):
        links.got(along_y(core, lax.rem(y + 4 - d, 4), h), k_p2 + k)
        links.got(along_x(core, at_x(4 - d), h), k_p2 + 6 + k)

    got_2(3, 0, 0)
    put_y(lax.rem(y + 1, 4), 0, k_p2 + 4, 3)
    put_x(at_x(1), 0, k_p2 + 10, 3)
    to_core(3, 0)
    for d, h, k in ((1, 0, 2), (1, 1, 3), (3, 1, 1), (2, 1, 5), (2, 0, 4)):
        got_2(d, h, k)
        to_core(d, h)

    direct = jnp.zeros((hidden.shape[0], SLOTS), F32)
    down_stores = []
    for turn in range(2):
        k = core if turn == 0 else 1 - core
        if turn == 1:
            for d in (0, 3, 1, 2):
                for h in range(2):
                    from_y, from_x = lax.rem(y + 4 - d, 4), at_x(4 - d)
                    links.got(along_y(k, from_y, h), k_core + 4 * d + h)
                    links.got(along_x(k, from_x, h), k_core + 4 * d + 2 + h)
        for f in range(4):
            at = pl.ds(pl.multiple_of((2 * f + k) * FSL, FSL), FSL)
            part = jnp.concatenate([rows[k, (f - n) % 4, n].reshape(2 * HALF, FSL) for n in range(Y)], axis=0)
            direct += nt(w_s[:, at], part)
            down_ref[:, at] = mm(hidden_scaled, part).astype(BF16)
            down_stores.append(load(down_ref.at[:, at], down_hbm.at[:, at], 21 + 4 * turn + f))
    slot_ref[...] = (direct * scale).astype(BF16)
    stores.append(load(slot_ref, slot_hbm, 33))

    for dx in range(1, X):
        links.got(iop_all.at[at_x(4 - dx)], k_ioa + dx)
    iop_all[t] = iop_out
    inpg_ref[...] = iop_all[0:2].reshape(NS, 128)
    outpg_ref[...] = iop_all[2:4].reshape(NS, 128)
    stores += [load(inpg_ref, inpg_hbm, 34), load(outpg_ref, outpg_hbm, 35)]

    idx0, idx1 = jnp.broadcast_to(info[:, 0:1], (BLK, 128)), jnp.broadcast_to(info[:, 1:2], (BLK, 128))
    pos0, pos1 = jnp.zeros((BLK, 128), F32), jnp.zeros((BLK, 128), F32)
    for i in range(BLK):
        i0, i1 = idx0[i : i + 1], idx1[i : i + 1]
        pos0 += jnp.where((row8 > i) & ((i0 == idx0) | (i1 == idx0)), 1.0, 0.0)
        pos1 += jnp.where((row8 > i) & ((i0 == idx1) | (i1 == idx1)), 1.0, 0.0)
    own_lane = lane8.astype(F32) - ((core * Z + e) * CAP).astype(F32)
    for dz in range(1, Z):
        links.got(tot_z.at[dz], k_tz + dz)
    val0, val1 = jnp.zeros((BLK, 128), F32), jnp.zeros((BLK, 128), F32)
    for dz in range(Z):
        expert = at_z(Z - dz).astype(F32)
        val0 = jnp.where(idx0 == expert, tot_z[dz], val0)
        val1 = jnp.where(idx1 == expert, tot_z[dz], val1)
    out0 = jnp.sum(jnp.where(own_lane == pos0, val0, 0.0), axis=1, keepdims=True)
    out1 = jnp.sum(jnp.where(own_lane == pos1, val1, 0.0), axis=1, keepdims=True)
    diagonal = row8 == lane8
    probg_ref[0:1, :] = jnp.sum(jnp.where(diagonal, out0, 0.0), axis=0, keepdims=True)[:, 0:BLK]
    probg_ref[1:2, :] = jnp.sum(jnp.where(diagonal, out1, 0.0), axis=0, keepdims=True)[:, 0:BLK]
    stores.append(load(probg_ref, probg_hbm, 36))

    @pl.when(t != 0)
    def _():
        pltpu.make_async_copy(wmix_ref, wbuf.at[0], local_sems.at[1]).wait()

    for copy in stores + down_stores:
        copy.wait()
    links.drain()


def store(*refs):
    ins, outs, held, sems = refs[:9], refs[9:18], refs[18:27], refs[27]
    steps = list(zip(ins, held, outs))
    big = steps.pop(7)
    steps += [[ref.at[pl.ds(n * 32, 32)] for ref in big] for n in range(7)]
    loads = [pltpu.make_async_copy(src, mid, sems.at[0, n]) for n, (src, mid, _) in enumerate(steps)]
    stores = [pltpu.make_async_copy(mid, dst, sems.at[1, n]) for n, (_, mid, dst) in enumerate(steps)]
    for copy in loads:
        copy.start()
    for load, save in zip(loads, stores):
        load.wait()
        save.start()
    for copy in stores:
        copy.wait()


def shards(
    mixer_input, step_sizes, decay_rates, input_proj, output_proj, skip_gain, doc_starts, ssm_grad, mixer_in_weight,
    residual_grad, expert_index_pairs, route_probs, hidden_saved, down_weight,
):
    hidden = hidden_saved[0].shape[0]
    features = down_weight.shape[2]
    anywhere = pl.BlockSpec(memory_space=pl.ANY)
    hbm = pl.BlockSpec(memory_space=pltpu.HBM)
    shape = jax.ShapeDtypeStruct
    out = pl.pallas_call(
        body,
        out_shape=(
            shape((TOK, CH), BF16),
            shape((TOK, CH), F32),
            shape((NS, TOK), F32),
            shape((NS, TOK), F32),
            shape((NS, CH), F32),
            shape((1, CH), F32),
            shape((hidden, SLOTS), BF16),
            shape((hidden, features), BF16),
            shape((2, BLK), F32),
        ),
        in_specs=[hbm] * 14,
        out_specs=(hbm,) * 9,
        scratch_shapes=[
            pltpu.VMEM((TOK, CH), BF16),
            pltpu.VMEM((TOK, CH), F32),
            pltpu.VMEM((NS, CH), F32),
            pltpu.VMEM((NS, TOK), F32),
            pltpu.VMEM((NS, TOK), F32),
            pltpu.VMEM((1, CH), F32),
            pltpu.SMEM((TOK,), jnp.int32),
            pltpu.VMEM((TOK, CH), BF16),
            pltpu.VMEM((BLK, features), BF16),
            pltpu.SMEM((2, BLK), jnp.int32),
            pltpu.SMEM((2, BLK), F32),
            pltpu.VMEM((hidden, SLOTS), BF16),
            pltpu.VMEM((hidden, features), BF16),
            pltpu.VMEM((TOK, CH), F32),
            pltpu.VMEM((NS, TOK), F32),
            pltpu.VMEM((NS, TOK), F32),
            pltpu.VMEM((NS, CH), F32),
            pltpu.VMEM((1, CH), F32),
            pltpu.VMEM((hidden, SLOTS), BF16),
            pltpu.VMEM((2, BLK), F32),
            pltpu.VMEM((2, X, Y, 2, HALF, FSL), BF16),
            pltpu.VMEM((X, Y, 2, HALF, FSL), BF16),
            pltpu.VMEM((4, Y, HALF, FSL), BF16),
            pltpu.VMEM((4, X, HALF, FSL), BF16),
            pltpu.VMEM((Y, HALF, FSL), BF16),
            pltpu.VMEM((X, HALF, FSL), BF16),
            pltpu.VMEM((4, HALF, FSL), BF16),
            pltpu.VMEM((4, HALF, FSL), BF16),
            pltpu.VMEM((TOK, CH), F32),
            pltpu.VMEM((TOK, CH), F32),
            pltpu.VMEM((TOK, NS, CH), F32),
            pltpu.VMEM((TOK, NS, CH), F32),
            pltpu.VMEM((TOK, NS, CH), F32),
            pltpu.VMEM((TOK, NS, CH), F32),
            pltpu.VMEM((128, 128), F32),
            pltpu.VMEM((TOK, CH), F32),
            pltpu.VMEM((CTX, 3 * NS, CH), F32),
            pltpu.VMEM((2, X, TOK, CH), BF16),
            pltpu.VMEM((4, 128, FSL), BF16),
            pltpu.VMEM((4, 4, 16, FSL), BF16),
            pltpu.VMEM((3, 4, 16, FSL), BF16),
            pltpu.VMEM((4, 16, FSL), BF16),
            pltpu.VMEM((3, 16, FSL), BF16),
            pltpu.VMEM((4, 4, 16, FSL), BF16),
            pltpu.VMEM((4, 4, 16, 128), F32),
            pltpu.VMEM((BLK, FSL + 128), F32),
            pltpu.VMEM((BLK, FSL + 128), F32),
            pltpu.VMEM((128, 256), BF16),
            pltpu.VMEM((1, 1, SLOTS), F32),
            pltpu.VMEM((4, 1, SLOTS), F32),
            pltpu.VMEM((2, X, Y, 2, HALF, FSL), BF16),
            pltpu.VMEM((hidden, features), BF16),
            pltpu.VMEM((4, 8, 128), F32),
            pltpu.VMEM((4, 8, 128), F32),
            pltpu.VMEM((4, 8, 128), F32),
            pltpu.VMEM((4, 8, 128), F32),
            pltpu.VMEM((4, 8, 128), F32),
            pltpu.VMEM((NS + BLK, CH), F32),
            pltpu.VMEM((CTX, NS + BLK, CH), F32),
            pltpu.VMEM((2 * X, BLK, 128), F32),
            pltpu.VMEM((Z, BLK, 128), F32),
            pltpu.SemaphoreType.DMA((NSEM,)),
            pltpu.SemaphoreType.DMA((NSEM,)),
            pltpu.SemaphoreType.DMA((40,)),
            pltpu.SemaphoreType.DMA((4,)),
        ],
        compiler_params=pltpu.CompilerParams(
            collective_id=0, has_side_effects=True, vmem_limit_bytes=VMEM_LIMIT
        ),
        name="scan_and_experts",
    )(
        mixer_input, step_sizes, decay_rates, input_proj, output_proj, skip_gain.reshape(1, CH), doc_starts, ssm_grad,
        mixer_in_weight, residual_grad, expert_index_pairs.T, route_probs.T, hidden_saved[0], down_weight[0],
    )
    ssm, stepg, inpg, outpg, decg, skipg, slot, down, probg = pl.pallas_call(
        store,
        out_shape=tuple(shape(array.shape, array.dtype) for array in out),
        in_specs=[anywhere] * 9,
        out_specs=tuple([hbm] * 9),
        scratch_shapes=[pltpu.VMEM(array.shape, array.dtype) for array in out] + [pltpu.SemaphoreType.DMA((2, 16))],
        compiler_params=pltpu.CompilerParams(vmem_limit_bytes=VMEM_LIMIT),
        name="store_results",
    )(*out)
    return ssm, stepg, inpg, outpg, decg, skipg.reshape(CH), slot[None], down[None], probg.T


def solution(mesh):
    return jax.shard_map(
        shards,
        mesh=mesh,
        in_specs=(
            P("ctx", ("exp", "tp")),
            P("ctx", ("exp", "tp")),
            P(None, ("exp", "tp")),
            P(None, "ctx"),
            P(None, "ctx"),
            P(("exp", "tp")),
            P("ctx"),
            P("ctx", ("exp", "tp")),
            P(("exp", "tp"), "ctx"),
            P(("ctx", "exp"), None),
            P(("ctx", "exp"), None),
            P(("ctx", "exp"), None),
            P("exp", ("ctx", "tp"), None),
            P("exp", ("ctx", "tp"), None),
        ),
        out_specs=(
            P("ctx", ("exp", "tp")),
            P("ctx", ("exp", "tp")),
            P(None, "ctx"),
            P(None, "ctx"),
            P(None, ("exp", "tp")),
            P(("exp", "tp")),
            P("exp", ("ctx", "tp"), None),
            P("exp", ("ctx", "tp"), None),
            P(("ctx", "exp"), None),
        ),
        check_vma=False,
    )
```

```python
import jax
import jax.numpy as jnp
from jax import lax
from jax.experimental import pallas as pl
from jax.experimental.pallas import tpu as pltpu
from jax.sharding import PartitionSpec as P

F32 = jnp.float32
BF16 = jnp.bfloat16
MESH = pl.DeviceIdType.MESH

TOK = 128
CH = 128
NS = 16
BLK = 8
NBLK = TOK // BLK
Y, CORES, Z, X = 4, 2, 16, 4
CTX = Y * CORES
FSL = 512
CAP = 3
HALF = Z * CAP
SLOTS = CTX * HALF
FAR = (10, 14, 2, 6)


def nt(a, b):
    return lax.dot_general(a, b, (((1,), (1,)), ((), ())), preferred_element_type=F32)


def mm(a, b):
    return jnp.dot(a, b, preferred_element_type=F32)


def iota(shape, dim):
    return lax.broadcasted_iota(jnp.int32, shape, dim)


class Links:
    def __init__(self, send, recv):
        self.send, self.recv = send, recv
        self.n_send = self.n_recv = 0
        self.started = []

    def slot(self, n=1):
        first = self.n_recv
        self.n_recv += n
        assert self.n_recv <= NSEM
        return first

    def put(self, src, dst, recv_index, **device):
        copy = pltpu.make_async_remote_copy(
            src_ref=src,
            dst_ref=dst,
            send_sem=self.send.at[self.n_send],
            recv_sem=self.recv.at[recv_index],
            device_id=device,
            device_id_type=MESH,
        )
        self.n_send += 1
        assert self.n_send <= NSEM
        copy.start()
        self.started.append(copy)
        return copy

    def got(self, dst, recv_index):
        pltpu.make_async_copy(dst, dst, self.recv.at[recv_index]).wait()

    def drain(self):
        for copy in self.started:
            copy.wait_send()
        self.started = []


NSEM = 256
VMEM_LIMIT = 60 * 1024 * 1024


def body(
    x_hbm, step_hbm, rates_hbm, inp_hbm, outp_hbm, skip_hbm, doc_hbm, g_hbm, wmix_ref, resid_hbm,
    idx_hbm, prob_hbm, hidden_hbm, weight_ref,
    ssm_hbm, stepg_hbm, inpg_hbm, outpg_hbm, decg_hbm, skipg_hbm, slot_hbm, down_hbm, probg_hbm,
    x_ref, step_ref, rates_ref, inp_ref, outp_ref, skip_ref, doc_ref, g_ref, resid_ref, idx_ref, prob_ref, hidden_ref, down_ref,
    stepg_ref, inpg_ref, outpg_ref, decg_ref, skipg_ref, slot_ref, probg_ref,
    gs, g0, g1x, g1y, a1, b1, g2a, g2b,
    xf, gf, a_s, inf_s, adj_s, ap_s, bsel, ssm_f, xbuf, sbuf, wbuf, pbuf, rbuf1, abuf, rbuf2,
    gbuf, ibuf, gown, iown, pair_out, pair_in, sel_s, scale_s, scale_in, rows, w_s,
    iop, iop_in, iop_far, iop_near, iop_all, dsp, dsp_in, tot_p, tot_z,
    send_sems, recv_sems, local_sems, weight_sem,
):
    links = Links(send_sems, recv_sems)
    c, e, t = lax.axis_index("ctx"), lax.axis_index("exp"), lax.axis_index("tp")
    y, core = lax.div(c, 2), lax.rem(c, 2)
    fs = 2 * lax.rem(t + y + 2 * core, 4) + core

    def at_y(dy):
        return 2 * lax.rem(y + dy, 4) + core

    def at_x(dx):
        return lax.rem(t + dx, 4)

    def at_z(dz):
        return lax.rem(e + dz, Z)

    barrier = pltpu.get_barrier_semaphore()
    partners = 0
    for dc in range(CTX):
        for dx in range(X):
            if dc or dx:
                pl.semaphore_signal(
                    barrier, inc=1, device_id={"ctx": lax.rem(c + dc, CTX), "tp": at_x(dx)}, device_id_type=MESH
                )
                partners += 1
    for dz in range(1, Z):
        pl.semaphore_signal(barrier, inc=1, device_id={"exp": at_z(dz)}, device_id_type=MESH)
        partners += 1

    def load(src, dst, at):
        copy = pltpu.make_async_copy(src, dst, local_sems.at[at])
        copy.start()
        return copy

    scan_loads = [
        load(src, dst, 2 + n)
        for n, (src, dst) in enumerate((
            (step_hbm, step_ref), (rates_hbm, rates_ref), (x_hbm, x_ref), (g_hbm, g_ref), (inp_hbm, inp_ref),
            (outp_hbm, outp_ref), (doc_hbm, doc_ref), (skip_hbm, skip_ref), (idx_hbm, idx_ref),
            (prob_hbm, prob_ref), (resid_hbm, resid_ref),
        ))
    ]
    late_loads = [load(hidden_hbm, hidden_ref, 13)]
    for n in range(7):
        part = pl.ds(n * 32, 32)
        late_loads.append(load(weight_ref.at[part], w_s.at[part], 14 + n))
    near = (1, 15, 2 + 12 * core)
    for copy in scan_loads:
        copy.wait()

    lane8 = iota((BLK, 128), 1)
    row8 = iota((BLK, 128), 0)
    info = jnp.zeros((BLK, 128), F32)
    for i in range(BLK):
        for k in range(2):
            info = jnp.where((row8 == i) & (lane8 == k), idx_ref[k, i].astype(F32), info)
            info = jnp.where((row8 == i) & (lane8 == 2 + k), prob_ref[k, i], info)
    info = info.astype(BF16).astype(F32)
    other_fs = 2 * lax.rem(t + y + 2 * (1 - core), 4) + (1 - core)
    pair_out[:, 0:FSL] = resid_ref[:, pl.ds(pl.multiple_of(other_fs * FSL, FSL), FSL)].astype(F32)
    pair_out[:, FSL:] = info
    xf[...] = x_ref[...].astype(F32)
    gf[...] = g_ref[...].astype(F32)
    g_bf = g_ref[...]
    u_bf = (step_ref[...] * xf[...]).astype(BF16)
    row, lane = iota((128, 128), 0), iota((128, 128), 1)
    b_tile = jnp.concatenate([inp_ref[...]] * BLK, axis=0)
    c_tile = jnp.concatenate([outp_ref[...]] * BLK, axis=0)
    bsel[...] = jnp.where(lax.rem(row, BLK) == lax.div(lane, NS), b_tile.T, 0.0)
    row_tok = lax.div(row, NS)

    def prepare(i, carry):
        at = pl.ds(pl.multiple_of(i * BLK, BLK), BLK)
        here = lane == row_tok + i * BLK
        decays = jnp.exp(step_ref[at, :][:, None, :] * rates_ref[...][None])
        for j in range(BLK):
            keep = (1 - doc_ref[i * BLK + j]).astype(F32)
            a_s[i * BLK + j] = decays[j] * keep
        inf_s[at] = mm(jnp.where(here, b_tile, 0.0).astype(BF16), u_bf).reshape(BLK, NS, CH)
        adj_s[at] = mm(jnp.where(here, c_tile, 0.0).astype(BF16), g_bf).reshape(BLK, NS, CH)
        return carry

    lax.fori_loop(0, NBLK, prepare, 0)

    zero = jnp.zeros((NS, CH), F32)

    def summarise(i, carry):
        state, back, damp = carry
        for j in range(BLK):
            up = i * BLK + j
            down = TOK - 1 - up
            decay = a_s[up]
            state = decay * state + inf_s[up]
            damp = damp * decay
            back = a_s[down] * (adj_s[down] + back)
        return state, back, damp

    state, back, damp = lax.fori_loop(0, NBLK, summarise, (zero, zero, zero + 1.0))
    xbuf[0, 0:NS] = damp
    xbuf[0, NS : 2 * NS] = state
    xbuf[0, 2 * NS :] = back
    for copy in late_loads:
        copy.wait()
    hidden_t = hidden_ref[...].T
    for k in range(2):
        for f in range(4):
            part = mm(hidden_t, w_s[:, pl.ds((2 * f + k) * FSL, FSL)]).astype(BF16).reshape(Y, 2, HALF, FSL)
            for n in range(Y):
                gs[k, (f - n - 2 * k) % 4, n] = part[n]

    pl.semaphore_wait(barrier, partners)
    k_ctx = links.slot(CTX)
    for dc in range(1, CTX):
        links.put(xbuf.at[0], xbuf.at[dc], k_ctx + dc, ctx=lax.rem(c + dc, CTX))

    k_pair = links.slot()
    links.put(pair_out, pair_in, k_pair, ctx=2 * y + (1 - core))

    for turn in range(4):
        dy = lax.rem(t + 2 * core + turn, 4)
        target = {"ctx": at_y(dy), "tp": lax.rem(8 - dy + 2 * core, 4)}
        if turn == 0:
            @pl.when(t == 2 * core)
            def _():
                pltpu.make_async_copy(wmix_ref, wbuf.at[t], weight_sem.at[t]).start()

            @pl.when(t != 2 * core)
            def _():
                pltpu.make_async_remote_copy(
                    src_ref=wmix_ref, dst_ref=wbuf.at[t], send_sem=local_sems.at[1], recv_sem=weight_sem.at[t],
                    device_id=target, device_id_type=MESH,
                ).start()
        else:
            copy = pltpu.make_async_remote_copy(
                src_ref=wmix_ref, dst_ref=wbuf.at[t], send_sem=send_sems.at[links.n_send],
                recv_sem=weight_sem.at[t], device_id=target, device_id_type=MESH,
            )
            links.n_send += 1
            copy.start()
            links.started.append(copy)

    other_core = 2 * y + (1 - core)
    k_g0 = links.slot(8)
    for n in range(X):
        for h in range(2):
            half = pl.ds(2 * h, 2)
            links.put(gs.at[1 - core, n, half], g0.at[n, half], k_g0 + 2 * n + h, ctx=other_core)

    links.got(pair_in, k_pair)
    mine = info
    theirs = pair_in[:, FSL:]
    first = core == 0
    iown[0:BLK] = jnp.where(first, mine, theirs)
    iown[BLK:] = jnp.where(first, theirs, mine)
    k_ifar = links.slot(4)
    for n, dz in enumerate(FAR):
        links.put(iown, ibuf.at[0, n], k_ifar + n, exp=at_z(dz))

    for dc in range(1, CTX):
        links.got(xbuf.at[dc], k_ctx + dc)
    entering, arriving = zero, zero
    for other in range(CTX):
        from_slot = lax.rem(c - other + CTX, CTX)
        entering = jnp.where(
            other < c, xbuf[from_slot, 0:NS] * entering + xbuf[from_slot, NS : 2 * NS], entering
        )
    for other in reversed(range(CTX)):
        from_slot = lax.rem(c - other + CTX, CTX)
        arriving = jnp.where(other > c, xbuf[from_slot, 0:NS] * arriving + xbuf[from_slot, 2 * NS :], arriving)

    def scan(i, carry):
        state, back = carry
        for j in range(BLK):
            up = i * BLK + j
            down = TOK - 1 - up
            kept = a_s[up] * state
            ap_s[up] = kept
            state = kept + inf_s[up]
            adjoint = adj_s[down] + back
            adj_s[down] = adjoint
            back = a_s[down] * adjoint
        return state, back

    lax.fori_loop(0, NBLK, scan, (entering, arriving))

    for n in range(4):
        links.got(ibuf.at[0, n], k_ifar + n)
    k_inear = links.slot(3)
    for n, dz in enumerate(near):
        links.put(ibuf.at[0], ibuf.at[1 + n], k_inear + n, exp=at_z(dz))

    rates = rates_ref[...]
    ones8 = jnp.where(iota((BLK, 128), 0) == lax.div(lane8, NS), 1.0, 0.0).astype(BF16)
    tok3, lane3 = iota((BLK, NS, 128), 0), iota((BLK, NS, 128), 2)
    skip = skip_ref[...]

    def gradients(i, carry):
        acc_in, acc_out, acc_decay = carry
        at = pl.ds(pl.multiple_of(i * BLK, BLK), BLK)
        adjoint, kept = adj_s[at], ap_s[at]
        states = (kept + inf_s[at]).reshape(128, CH).astype(BF16)
        adjoint_bf = adjoint.reshape(128, CH).astype(BF16)
        here = lane3 == tok3 + i * BLK
        acc_out += jnp.sum(jnp.where(here, nt(states, g_bf).reshape(BLK, NS, 128), 0.0), axis=0)
        acc_in += jnp.sum(jnp.where(here, nt(adjoint_bf, u_bf).reshape(BLK, NS, 128), 0.0), axis=0)
        through = mm(bsel[at, :].astype(BF16), adjoint_bf)
        product = adjoint * kept
        rated = mm(ones8, (product * rates[None]).reshape(128, CH).astype(BF16))
        step = step_ref[at, :]
        acc_decay += jnp.sum(product * step[:, None, :], axis=0)
        stepg_ref[at, :] = rated + xf[at, :] * through
        ssm_f[at, :] = skip * gf[at, :] + step * through
        return acc_in, acc_out, acc_decay

    acc_in, acc_out, acc_decay = lax.fori_loop(0, NBLK, gradients, (zero, zero, zero))

    ssm_bf = ssm_f[...].astype(BF16)
    sbuf[0, 0] = ssm_bf
    stores = [load(sbuf.at[0, 0], ssm_hbm, 29), load(stepg_ref, stepg_hbm, 30)]
    k_s = links.slot(2 * X)
    for dx in (2, 1, 3):
        links.put(sbuf.at[0, 0], sbuf.at[0, dx], k_s + dx, tp=at_x(dx))
    links.put(sbuf.at[0, 0], sbuf.at[1, 0], k_s + X, ctx=other_core)

    iop[0:2] = acc_in.reshape(2, 8, 128)
    iop[2:4] = acc_out.reshape(2, 8, 128)
    k_iox = links.slot(4)
    for dx in range(1, X):
        links.put(iop.at[at_x(dx)], iop_in.at[dx], k_iox + dx, tp=at_x(dx))
    dsp[0:NS] = acc_decay
    skip_part = jnp.sum(gf[...] * xf[...], axis=0, keepdims=True)
    dsp[NS:] = jnp.broadcast_to(skip_part, (BLK, CH))
    k_dsp = links.slot(CTX)
    for dc in range(1, CTX):
        links.put(dsp, dsp_in.at[dc], k_dsp + dc, ctx=lax.rem(c + dc, CTX))

    for n in range(3):
        links.got(ibuf.at[1 + n], k_inear + n)
    infos = ibuf[...].reshape(256, 128)
    e_f = e.astype(F32)
    hit0 = jnp.where(infos[:, 0:1] == e_f, 1.0, 0.0)
    hit1 = jnp.where(infos[:, 1:2] == e_f, 1.0, 0.0)
    hit = jnp.broadcast_to(hit0 + hit1, (256, 128))
    factor = hit0 * infos[:, 2:3] + hit1 * infos[:, 3:4]
    r256, l256 = iota((256, 256), 0), iota((256, 256), 1)
    before = jnp.where((lax.div(r256, BLK) == lax.div(l256, BLK)) & (r256 > l256), 1.0, 0.0).astype(BF16)
    position = mm(before, hit.astype(BF16))
    tok_row = iota((256, 128), 0)
    tok_near, tok_far = lax.div(tok_row, 64), lax.rem(lax.div(tok_row, 16), 4)
    near_of = jnp.where(tok_near == 1, 1, jnp.where(tok_near == 2, 15, jnp.where(tok_near == 3, 2 + 12 * core, 0)))
    tok_block = lax.rem(e + 4 * Z - near_of - 10 - 4 * tok_far, Z)
    tok_k = lax.rem(lax.div(tok_row, BLK), 2)
    tok_slot = (tok_k * Z + tok_block) * CAP
    slot_of = tok_slot.astype(F32) + position
    picked = jnp.where(iota((256, 128), 1).astype(F32) == slot_of, hit, 0.0)
    sel_s[...] = picked.T.astype(BF16)
    own_scale = jnp.sum(picked * factor, axis=0, keepdims=True)[:, 0 : 2 * HALF]
    zeros96 = jnp.zeros((1, 2 * HALF), F32)
    scale_s[0] = jnp.concatenate([jnp.where(y == n, own_scale, zeros96) for n in range(Y)], axis=1)
    k_scale = links.slot(4)
    for dy in range(1, 4):
        links.put(scale_s.at[0], scale_in.at[dy], k_scale + dy, ctx=at_y(dy))

    for n in range(X):
        for h in range(2):
            links.got(g0.at[n, pl.ds(2 * h, 2)], k_g0 + 2 * n + h)
        gs[core, n] = (gs[core, n].astype(F32) + g0[n].astype(F32)).astype(BF16)

    for n in range(4):
        pltpu.make_async_copy(wbuf.at[n], wbuf.at[n], weight_sem.at[n]).wait()
    for dx in (1, 3, 2):
        links.got(sbuf.at[0, dx], k_s + dx)
        links.put(sbuf.at[0, dx], sbuf.at[1, dx], k_s + X + dx, ctx=other_core)
    for dx in (0, 1, 3, 2):
        links.got(sbuf.at[1, dx], k_s + X + dx)
    k_g1 = links.slot(8)
    for d in (2, 1, 3):
        links.put(gs.at[core, at_x(d), :, 0], g1x.at[d], k_g1 + d, tp=at_x(d))
        links.put(gs.at[core, :, lax.rem(y + d, 4), 1], g1y.at[d], k_g1 + 4 + d, ctx=at_y(d))
    mixer = wbuf[...].reshape(4 * 128, FSL)
    parts = []
    for k in range(2):
        dk = lax.rem(core + k, 2)
        lhs = jnp.concatenate([sbuf[dk, lax.rem(t - n + 4, 4)] for n in range(4)], axis=1)
        parts.append(mm(lhs, mixer).reshape(Z, BLK, FSL))
    chunks = jnp.concatenate(parts, axis=1).astype(BF16)
    for n in range(Z):
        ahead = lax.rem(n + Z - e, Z)
        pbuf[lax.rem(ahead, 4), lax.div(ahead, 4)] = chunks[n]

    k_r1 = links.slot(3)
    for n, dz in enumerate(near):
        links.put(pbuf.at[(3, 1, 0)[n]], rbuf1.at[n], k_r1 + n, exp=at_z(dz))
    for dx in range(1, X):
        links.got(iop_in.at[dx], k_iox + dx)
    iop_far[4] = iop[t] + iop_in[1] + iop_in[2] + iop_in[3]
    k_iof = links.slot(4)
    for n, dz in enumerate(FAR):
        links.put(iop_far.at[4], iop_far.at[n], k_iof + n, exp=at_z(dz))
    for n in range(3):
        links.got(rbuf1.at[n], k_r1 + n)
    k_r2 = links.slot(4)
    for n, dz in ((0, 10), (3, 6), (1, 14), (2, 2)):
        at = (2 + n) % 4
        summed = pbuf[2, at].astype(F32) + rbuf1[0, at].astype(F32) + rbuf1[1, at].astype(F32)
        summed += rbuf1[2, lax.rem(3 - core + n, 4)].astype(F32)
        abuf[n] = summed.astype(BF16)
        links.put(abuf.at[n], rbuf2.at[n], k_r2 + n, exp=at_z(dz))
    own_resid = resid_ref[:, pl.ds(pl.multiple_of(fs * FSL, FSL), FSL)].astype(F32)
    their_resid = pair_in[:, 0:FSL]
    resid = jnp.concatenate(
        [jnp.where(first, own_resid, their_resid), jnp.where(first, their_resid, own_resid)], axis=0
    )
    for n in range(4):
        links.got(rbuf2.at[n], k_r2 + n)
    total = resid
    for n in range(4):
        total += rbuf2[n].astype(F32)

    gown[...] = total.astype(BF16)
    k_a1 = links.slot(4)
    for n, dz in enumerate(FAR):
        links.put(gown, gbuf.at[0, n], k_a1 + n, exp=at_z(dz))
    for d in (1, 3, 2):
        links.got(g1x.at[d], k_g1 + d)
        links.got(g1y.at[d], k_g1 + 4 + d)
    for n in range(4):
        over_x, over_y = gs[core, t, n, 0].astype(F32), gs[core, n, y, 1].astype(F32)
        for d in range(1, 4):
            over_x += g1x[d, n].astype(F32)
            over_y += g1y[d, n].astype(F32)
        a1[n] = over_x.astype(BF16)
        b1[n] = over_y.astype(BF16)
    k_g2 = links.slot(8)
    for d in (2, 1, 3):
        links.put(a1.at[lax.rem(y + d, 4)], g2a.at[d], k_g2 + d, ctx=at_y(d))
        links.put(b1.at[at_x(d)], g2b.at[d], k_g2 + 4 + d, tp=at_x(d))
    for n in range(4):
        links.got(iop_far.at[n], k_iof + n)
    iop_near[0] = iop_far[0] + iop_far[1] + iop_far[2] + iop_far[3]
    for n in range(4):
        links.got(gbuf.at[0, n], k_a1 + n)
    k_a2 = links.slot(3)
    for n, dz in enumerate(near):
        links.put(gbuf.at[0], gbuf.at[1 + n], k_a2 + n, exp=at_z(dz))
    k_ion = links.slot(4)
    for n, dz in enumerate(near):
        links.put(iop_near.at[0], iop_near.at[n + 1], k_ion + n, exp=at_z(dz))
    for d in (1, 3, 2):
        links.got(g2a.at[d], k_g2 + d)
        links.got(g2b.at[d], k_g2 + 4 + d)
    weight_low, weight_high = a1[y].astype(F32), b1[t].astype(F32)
    for d in range(1, 4):
        weight_low += g2a[d].astype(F32)
        weight_high += g2b[d].astype(F32)
    for n in range(3):
        links.got(gbuf.at[1 + n], k_a2 + n)

    picked_rows = mm(sel_s[...], gbuf[...].reshape(256, FSL)).astype(BF16)
    rows[core, t, y, 0] = picked_rows[0:HALF]
    rows[core, t, y, 1] = picked_rows[HALF : 2 * HALF]
    def piece(axis, k, step, d=0):
        if axis == 0:
            return rows.at[k, at_x(step), lax.rem(y + 4 - d, 4), 0]
        return rows.at[k, at_x(4 - d), lax.rem(y + step, 4), 1]

    def pass_on(axis, step, d_from, slot, d):
        device = {"ctx": at_y(d)} if axis == 0 else {"tp": at_x(d)}
        links.put(piece(axis, core, step, d_from), piece(axis, core, step, d_from), slot, **device)

    k_p1, k_p2, k_core = links.slot(8), links.slot(32), links.slot(32)

    def slot_2(axis, step, d):
        return k_p2 + 16 * axis + 4 * step + d

    def to_core(axis, step, d):
        ref = piece(axis, core, step, d)
        links.put(ref, ref, k_core + 16 * axis + 4 * step + d, ctx=other_core)

    def got_1(d):
        for axis in range(2):
            step = 4 - d
            links.got(piece(axis, core, step), k_p1 + 4 * axis + d)
            for to in ((1, 3, 2) if d == 2 else (3, 1)):
                pass_on(axis, step, 0, slot_2(axis, step, to), to)
        for axis in range(2):
            to_core(axis, 4 - d, 0)

    def got_2(step, d, relay=False):
        for axis in range(2):
            links.got(piece(axis, core, step, d), slot_2(axis, step, d))
            if relay:
                pass_on(axis, step, 3, slot_2(axis, step, 2), 3)
        for axis in range(2):
            to_core(axis, step, d)

    for d in (2, 1, 3):
        links.put(rows.at[core, t, y, 0], rows.at[core, t, y, 0], k_p1 + d, tp=at_x(d))
        links.put(rows.at[core, t, y, 1], rows.at[core, t, y, 1], k_p1 + 4 + d, ctx=at_y(d))
    for d in (3, 1):
        for axis in range(2):
            pass_on(axis, 0, 0, slot_2(axis, 0, d), d)
    for axis in range(2):
        to_core(axis, 0, 0)
    product = jnp.concatenate(
        [
            picked_rows[0:HALF].astype(F32) * weight_low,
            picked_rows[HALF : 2 * HALF].astype(F32) * weight_high,
            jnp.zeros((128 - 2 * HALF, FSL), F32),
        ],
        axis=0,
    )
    high = product.astype(BF16)
    low = (product - high.astype(F32)).astype(BF16)
    ones = jnp.ones((BLK, FSL), BF16)
    tot_p[0] = nt(ones, high) + nt(ones, low)
    k_tp = links.slot(2 * X)
    for dk in range(2):
        for dx in range(X):
            if dk or dx:
                links.put(
                    tot_p.at[0], tot_p.at[dk * X + dx], k_tp + dk * X + dx,
                    ctx=2 * y + lax.rem(core + dk, 2), tp=at_x(dx),
                )
    got_1(1)
    got_1(3)
    got_2(0, 3, relay=True)
    got_1(2)
    for n in range(1, 2 * X):
        links.got(tot_p.at[n], k_tp + n)
    slot_total = tot_p[0]
    for n in range(1, 2 * X):
        slot_total += tot_p[n]
    tot_z[0] = slot_total
    k_tz = links.slot(Z)
    for dz in range(1, Z):
        links.put(tot_z.at[0], tot_z.at[dz], k_tz + dz, exp=at_z(dz))

    for n in range(3):
        links.got(iop_near.at[n + 1], k_ion + n)
    iop_out = iop_near[0] + iop_near[1] + iop_near[2] + iop_near[3]
    iop_in[0] = iop_out
    k_ioa = links.slot(4)
    for dx in range(1, X):
        links.put(iop_in.at[0], iop_all.at[t], k_ioa + dx, tp=at_x(dx))
    for dc in range(1, CTX):
        links.got(dsp_in.at[dc], k_dsp + dc)
    sums = dsp[...]
    for dc in range(1, CTX):
        sums += dsp_in[dc]
    decg_ref[...] = sums[0:NS]
    skipg_ref[...] = sums[NS : NS + 1]
    stores += [load(decg_ref, decg_hbm, 31), load(skipg_ref, skipg_hbm, 32)]
    for dy in range(1, 4):
        links.got(scale_in.at[dy], k_scale + dy)
    scale = scale_s[0] + scale_in[1] + scale_in[2] + scale_in[3]

    hidden = hidden_ref[...]
    hidden_scaled = (hidden.astype(F32) * scale).astype(BF16)
    got_2(0, 1)
    got_2(3, 3, relay=True)
    got_2(1, 3, relay=True)
    for step, d in ((3, 1), (1, 1), (0, 2), (2, 1), (2, 3), (3, 2), (1, 2), (2, 2)):
        got_2(step, d)

    direct = jnp.zeros((hidden.shape[0], SLOTS), F32)
    down_stores = []
    for turn in range(2):
        k = core if turn == 0 else 1 - core
        if turn == 1:
            for step in range(4):
                for d in range(4):
                    for axis in range(2):
                        links.got(piece(axis, k, step, d), k_core + 16 * axis + 4 * step + d)
        for f in range(4):
            at = pl.ds(pl.multiple_of((2 * f + k) * FSL, FSL), FSL)
            part = jnp.concatenate([rows[k, lax.rem(f - n - 2 * k + 8, 4), n].reshape(2 * HALF, FSL) for n in range(Y)], axis=0)
            direct += nt(w_s[:, at], part)
            down_ref[:, at] = mm(hidden_scaled, part).astype(BF16)
            down_stores.append(load(down_ref.at[:, at], down_hbm.at[:, at], 21 + 4 * turn + f))
    slot_ref[...] = (direct * scale).astype(BF16)
    stores.append(load(slot_ref, slot_hbm, 33))

    for dx in range(1, X):
        links.got(iop_all.at[at_x(4 - dx)], k_ioa + dx)
    iop_all[t] = iop_out
    inpg_ref[...] = iop_all[0:2].reshape(NS, 128)
    outpg_ref[...] = iop_all[2:4].reshape(NS, 128)
    stores += [load(inpg_ref, inpg_hbm, 34), load(outpg_ref, outpg_hbm, 35)]

    idx0, idx1 = jnp.broadcast_to(info[:, 0:1], (BLK, 128)), jnp.broadcast_to(info[:, 1:2], (BLK, 128))
    pos0, pos1 = jnp.zeros((BLK, 128), F32), jnp.zeros((BLK, 128), F32)
    for i in range(BLK):
        i0, i1 = idx0[i : i + 1], idx1[i : i + 1]
        pos0 += jnp.where((row8 > i) & ((i0 == idx0) | (i1 == idx0)), 1.0, 0.0)
        pos1 += jnp.where((row8 > i) & ((i0 == idx1) | (i1 == idx1)), 1.0, 0.0)
    own_lane = lane8.astype(F32) - ((core * Z + e) * CAP).astype(F32)
    for dz in range(1, Z):
        links.got(tot_z.at[dz], k_tz + dz)
    val0, val1 = jnp.zeros((BLK, 128), F32), jnp.zeros((BLK, 128), F32)
    for dz in range(Z):
        expert = at_z(Z - dz).astype(F32)
        val0 = jnp.where(idx0 == expert, tot_z[dz], val0)
        val1 = jnp.where(idx1 == expert, tot_z[dz], val1)
    out0 = jnp.sum(jnp.where(own_lane == pos0, val0, 0.0), axis=1, keepdims=True)
    out1 = jnp.sum(jnp.where(own_lane == pos1, val1, 0.0), axis=1, keepdims=True)
    diagonal = row8 == lane8
    probg_ref[0:1, :] = jnp.sum(jnp.where(diagonal, out0, 0.0), axis=0, keepdims=True)[:, 0:BLK]
    probg_ref[1:2, :] = jnp.sum(jnp.where(diagonal, out1, 0.0), axis=0, keepdims=True)[:, 0:BLK]
    stores.append(load(probg_ref, probg_hbm, 36))

    @pl.when(t != 2 * core)
    def _():
        pltpu.make_async_copy(wmix_ref, wbuf.at[0], local_sems.at[1]).wait()

    for copy in stores + down_stores:
        copy.wait()
    links.drain()


def store(*refs):
    ins, outs, held, sems = refs[:9], refs[9:18], refs[18:27], refs[27]
    steps = list(zip(ins, held, outs))
    big = steps.pop(7)
    steps += [[ref.at[pl.ds(n * 32, 32)] for ref in big] for n in range(7)]
    loads = [pltpu.make_async_copy(src, mid, sems.at[0, n]) for n, (src, mid, _) in enumerate(steps)]
    stores = [pltpu.make_async_copy(mid, dst, sems.at[1, n]) for n, (_, mid, dst) in enumerate(steps)]
    for copy in loads:
        copy.start()
    for load, save in zip(loads, stores):
        load.wait()
        save.start()
    for copy in stores:
        copy.wait()


def shards(
    mixer_input, step_sizes, decay_rates, input_proj, output_proj, skip_gain, doc_starts, ssm_grad, mixer_in_weight,
    residual_grad, expert_index_pairs, route_probs, hidden_saved, down_weight,
):
    hidden = hidden_saved[0].shape[0]
    features = down_weight.shape[2]
    anywhere = pl.BlockSpec(memory_space=pl.ANY)
    hbm = pl.BlockSpec(memory_space=pltpu.HBM)
    shape = jax.ShapeDtypeStruct
    out = pl.pallas_call(
        body,
        out_shape=(
            shape((TOK, CH), BF16),
            shape((TOK, CH), F32),
            shape((NS, TOK), F32),
            shape((NS, TOK), F32),
            shape((NS, CH), F32),
            shape((1, CH), F32),
            shape((hidden, SLOTS), BF16),
            shape((hidden, features), BF16),
            shape((2, BLK), F32),
        ),
        in_specs=[hbm] * 14,
        out_specs=(hbm,) * 9,
        scratch_shapes=[
            pltpu.VMEM((TOK, CH), BF16),
            pltpu.VMEM((TOK, CH), F32),
            pltpu.VMEM((NS, CH), F32),
            pltpu.VMEM((NS, TOK), F32),
            pltpu.VMEM((NS, TOK), F32),
            pltpu.VMEM((1, CH), F32),
            pltpu.SMEM((TOK,), jnp.int32),
            pltpu.VMEM((TOK, CH), BF16),
            pltpu.VMEM((BLK, features), BF16),
            pltpu.SMEM((2, BLK), jnp.int32),
            pltpu.SMEM((2, BLK), F32),
            pltpu.VMEM((hidden, SLOTS), BF16),
            pltpu.VMEM((hidden, features), BF16),
            pltpu.VMEM((TOK, CH), F32),
            pltpu.VMEM((NS, TOK), F32),
            pltpu.VMEM((NS, TOK), F32),
            pltpu.VMEM((NS, CH), F32),
            pltpu.VMEM((1, CH), F32),
            pltpu.VMEM((hidden, SLOTS), BF16),
            pltpu.VMEM((2, BLK), F32),
            pltpu.VMEM((2, X, Y, 2, HALF, FSL), BF16),
            pltpu.VMEM((X, Y, 2, HALF, FSL), BF16),
            pltpu.VMEM((4, Y, HALF, FSL), BF16),
            pltpu.VMEM((4, X, HALF, FSL), BF16),
            pltpu.VMEM((Y, HALF, FSL), BF16),
            pltpu.VMEM((X, HALF, FSL), BF16),
            pltpu.VMEM((4, HALF, FSL), BF16),
            pltpu.VMEM((4, HALF, FSL), BF16),
            pltpu.VMEM((TOK, CH), F32),
            pltpu.VMEM((TOK, CH), F32),
            pltpu.VMEM((TOK, NS, CH), F32),
            pltpu.VMEM((TOK, NS, CH), F32),
            pltpu.VMEM((TOK, NS, CH), F32),
            pltpu.VMEM((TOK, NS, CH), F32),
            pltpu.VMEM((128, 128), F32),
            pltpu.VMEM((TOK, CH), F32),
            pltpu.VMEM((CTX, 3 * NS, CH), F32),
            pltpu.VMEM((2, X, TOK, CH), BF16),
            pltpu.VMEM((4, 128, FSL), BF16),
            pltpu.VMEM((4, 4, 16, FSL), BF16),
            pltpu.VMEM((3, 4, 16, FSL), BF16),
            pltpu.VMEM((4, 16, FSL), BF16),
            pltpu.VMEM((4, 16, FSL), BF16),
            pltpu.VMEM((4, 4, 16, FSL), BF16),
            pltpu.VMEM((4, 4, 16, 128), F32),
            pltpu.VMEM((16, FSL), BF16),
            pltpu.VMEM((16, 128), F32),
            pltpu.VMEM((BLK, FSL + 128), F32),
            pltpu.VMEM((BLK, FSL + 128), F32),
            pltpu.VMEM((128, 256), BF16),
            pltpu.VMEM((1, 1, SLOTS), F32),
            pltpu.VMEM((4, 1, SLOTS), F32),
            pltpu.VMEM((2, X, Y, 2, HALF, FSL), BF16),
            pltpu.VMEM((hidden, features), BF16),
            pltpu.VMEM((4, 8, 128), F32),
            pltpu.VMEM((4, 8, 128), F32),
            pltpu.VMEM((5, 8, 128), F32),
            pltpu.VMEM((4, 8, 128), F32),
            pltpu.VMEM((4, 8, 128), F32),
            pltpu.VMEM((NS + BLK, CH), F32),
            pltpu.VMEM((CTX, NS + BLK, CH), F32),
            pltpu.VMEM((2 * X, BLK, 128), F32),
            pltpu.VMEM((Z, BLK, 128), F32),
            pltpu.SemaphoreType.DMA((NSEM,)),
            pltpu.SemaphoreType.DMA((NSEM,)),
            pltpu.SemaphoreType.DMA((40,)),
            pltpu.SemaphoreType.DMA((4,)),
        ],
        compiler_params=pltpu.CompilerParams(
            collective_id=0, has_side_effects=True, vmem_limit_bytes=VMEM_LIMIT
        ),
        name="scan_and_experts",
    )(
        mixer_input, step_sizes, decay_rates, input_proj, output_proj, skip_gain.reshape(1, CH), doc_starts, ssm_grad,
        mixer_in_weight, residual_grad, expert_index_pairs.T, route_probs.T, hidden_saved[0], down_weight[0],
    )
    ssm, stepg, inpg, outpg, decg, skipg, slot, down, probg = pl.pallas_call(
        store,
        out_shape=tuple(shape(array.shape, array.dtype) for array in out),
        in_specs=[anywhere] * 9,
        out_specs=tuple([hbm] * 9),
        scratch_shapes=[pltpu.VMEM(array.shape, array.dtype) for array in out] + [pltpu.SemaphoreType.DMA((2, 16))],
        compiler_params=pltpu.CompilerParams(vmem_limit_bytes=VMEM_LIMIT),
        name="store_results",
    )(*out)
    return ssm, stepg, inpg, outpg, decg, skipg.reshape(CH), slot[None], down[None], probg.T


def solution(mesh):
    return jax.shard_map(
        shards,
        mesh=mesh,
        in_specs=(
            P("ctx", ("exp", "tp")),
            P("ctx", ("exp", "tp")),
            P(None, ("exp", "tp")),
            P(None, "ctx"),
            P(None, "ctx"),
            P(("exp", "tp")),
            P("ctx"),
            P("ctx", ("exp", "tp")),
            P(("exp", "tp"), "ctx"),
            P(("ctx", "exp"), None),
            P(("ctx", "exp"), None),
            P(("ctx", "exp"), None),
            P("exp", ("ctx", "tp"), None),
            P("exp", ("ctx", "tp"), None),
        ),
        out_specs=(
            P("ctx", ("exp", "tp")),
            P("ctx", ("exp", "tp")),
            P(None, "ctx"),
            P(None, "ctx"),
            P(None, ("exp", "tp")),
            P(("exp", "tp")),
            P("exp", ("ctx", "tp"), None),
            P("exp", ("ctx", "tp"), None),
            P(("ctx", "exp"), None),
        ),
        check_vma=False,
    )
```

```python
import jax
import jax.numpy as jnp
from jax import lax
from jax.experimental import pallas as pl
from jax.experimental.pallas import tpu as pltpu
from jax.sharding import PartitionSpec as P

F32 = jnp.float32
BF16 = jnp.bfloat16
MESH = pl.DeviceIdType.MESH

TOK = 128
CH = 128
NS = 16
BLK = 8
NBLK = TOK // BLK
Y, CORES, Z, X = 4, 2, 16, 4
CTX = Y * CORES
FSL = 512
CAP = 3
HALF = Z * CAP
SLOTS = CTX * HALF
FAR = (10, 14, 2, 6)


def nt(a, b):
    return lax.dot_general(a, b, (((1,), (1,)), ((), ())), preferred_element_type=F32)


def mm(a, b):
    return jnp.dot(a, b, preferred_element_type=F32)


def iota(shape, dim):
    return lax.broadcasted_iota(jnp.int32, shape, dim)


class Links:
    def __init__(self, send, recv):
        self.send, self.recv = send, recv
        self.n_send = self.n_recv = 0
        self.started = []

    def slot(self, n=1):
        first = self.n_recv
        self.n_recv += n
        assert self.n_recv <= NSEM
        return first

    def put(self, src, dst, recv_index, **device):
        copy = pltpu.make_async_remote_copy(
            src_ref=src,
            dst_ref=dst,
            send_sem=self.send.at[self.n_send],
            recv_sem=self.recv.at[recv_index],
            device_id=device,
            device_id_type=MESH,
        )
        self.n_send += 1
        assert self.n_send <= NSEM
        copy.start()
        self.started.append(copy)
        return copy

    def got(self, dst, recv_index):
        pltpu.make_async_copy(dst, dst, self.recv.at[recv_index]).wait()

    def drain(self):
        for copy in self.started:
            copy.wait_send()
        self.started = []


NSEM = 256
VMEM_LIMIT = 60 * 1024 * 1024


def body(
    x_hbm, step_hbm, rates_hbm, inp_hbm, outp_hbm, skip_hbm, doc_hbm, g_hbm, wmix_ref, resid_hbm,
    idx_hbm, prob_hbm, hidden_hbm, weight_ref,
    ssm_hbm, stepg_hbm, inpg_hbm, outpg_hbm, decg_hbm, skipg_hbm, slot_hbm, down_hbm, probg_hbm,
    x_ref, step_ref, rates_ref, inp_ref, outp_ref, skip_ref, doc_ref, g_ref, resid_ref, idx_ref, prob_ref, hidden_ref, down_ref,
    stepg_ref, inpg_ref, outpg_ref, decg_ref, skipg_ref, slot_ref, probg_ref,
    gs, g0, g1x, g1y, a1, b1, g2a, g2b,
    xf, gf, a_s, inf_s, adj_s, ap_s, bsel, ssm_f, xbuf, sbuf, wbuf, pbuf, rbuf1, abuf, rbuf2,
    gbuf, ibuf, gown, iown, pair_out, pair_in, sel_s, scale_s, scale_in, rows, w_s,
    iop, iop_in, iop_far, iop_near, iop_all, dsp, dsp_in, tot_p, tot_z,
    send_sems, recv_sems, local_sems, weight_sem,
):
    links = Links(send_sems, recv_sems)
    c, e, t = lax.axis_index("ctx"), lax.axis_index("exp"), lax.axis_index("tp")
    y, core = lax.div(c, 2), lax.rem(c, 2)
    fs = 2 * lax.rem(t + y + 2 * core, 4) + core

    def at_y(dy):
        return 2 * lax.rem(y + dy, 4) + core

    def at_x(dx):
        return lax.rem(t + dx, 4)

    def at_z(dz):
        return lax.rem(e + dz, Z)

    def load(src, dst, at):
        copy = pltpu.make_async_copy(src, dst, local_sems.at[at])
        copy.start()
        return copy

    scan_loads = [
        load(src, dst, 2 + n)
        for n, (src, dst) in enumerate((
            (step_hbm, step_ref), (rates_hbm, rates_ref), (x_hbm, x_ref), (g_hbm, g_ref), (inp_hbm, inp_ref),
            (outp_hbm, outp_ref), (doc_hbm, doc_ref), (skip_hbm, skip_ref), (idx_hbm, idx_ref),
            (prob_hbm, prob_ref), (resid_hbm, resid_ref),
        ))
    ]
    late_loads = [load(hidden_hbm, hidden_ref, 13)]
    for n in range(7):
        part = pl.ds(n * 32, 32)
        late_loads.append(load(weight_ref.at[part], w_s.at[part], 14 + n))

    barrier = pltpu.get_barrier_semaphore()
    partners = 0
    for dc in range(CTX):
        for dx in range(X):
            if dc or dx:
                pl.semaphore_signal(
                    barrier, inc=1, device_id={"ctx": lax.rem(c + dc, CTX), "tp": at_x(dx)}, device_id_type=MESH
                )
                partners += 1
    for dz in range(1, Z):
        pl.semaphore_signal(barrier, inc=1, device_id={"exp": at_z(dz)}, device_id_type=MESH)
        partners += 1

    near = (1, 15, 2 + 12 * core)
    for copy in scan_loads:
        copy.wait()

    lane8 = iota((BLK, 128), 1)
    row8 = iota((BLK, 128), 0)
    info = jnp.zeros((BLK, 128), F32)
    for i in range(BLK):
        for k in range(2):
            info = jnp.where((row8 == i) & (lane8 == k), idx_ref[k, i].astype(F32), info)
            info = jnp.where((row8 == i) & (lane8 == 2 + k), prob_ref[k, i], info)
    info = info.astype(BF16).astype(F32)
    other_fs = 2 * lax.rem(t + y + 2 * (1 - core), 4) + (1 - core)
    pair_out[:, 0:FSL] = resid_ref[:, pl.ds(pl.multiple_of(other_fs * FSL, FSL), FSL)].astype(F32)
    pair_out[:, FSL:] = info
    xf[...] = x_ref[...].astype(F32)
    gf[...] = g_ref[...].astype(F32)
    g_bf = g_ref[...]
    u_bf = (step_ref[...] * xf[...]).astype(BF16)
    row, lane = iota((128, 128), 0), iota((128, 128), 1)
    b_tile = jnp.concatenate([inp_ref[...]] * BLK, axis=0)
    c_tile = jnp.concatenate([outp_ref[...]] * BLK, axis=0)
    bsel[...] = jnp.where(lax.rem(row, BLK) == lax.div(lane, NS), b_tile.T, 0.0)
    row_tok = lax.div(row, NS)

    def prepare(i, carry):
        at = pl.ds(pl.multiple_of(i * BLK, BLK), BLK)
        here = lane == row_tok + i * BLK
        decays = jnp.exp(step_ref[at, :][:, None, :] * rates_ref[...][None])
        for j in range(BLK):
            keep = (1 - doc_ref[i * BLK + j]).astype(F32)
            a_s[i * BLK + j] = decays[j] * keep
        inf_s[at] = mm(jnp.where(here, b_tile, 0.0).astype(BF16), u_bf).reshape(BLK, NS, CH)
        adj_s[at] = mm(jnp.where(here, c_tile, 0.0).astype(BF16), g_bf).reshape(BLK, NS, CH)
        return carry

    lax.fori_loop(0, NBLK, prepare, 0)

    zero = jnp.zeros((NS, CH), F32)

    def summarise(i, carry):
        state, back, damp = carry
        for j in range(BLK):
            up = i * BLK + j
            down = TOK - 1 - up
            decay = a_s[up]
            state = decay * state + inf_s[up]
            damp = damp * decay
            back = a_s[down] * (adj_s[down] + back)
        return state, back, damp

    state, back, damp = lax.fori_loop(0, NBLK, summarise, (zero, zero, zero + 1.0))
    xbuf[0, 0:NS] = damp
    xbuf[0, NS : 2 * NS] = state
    xbuf[0, 2 * NS :] = back
    pl.semaphore_wait(barrier, partners)
    k_ctx = links.slot(CTX)
    for dc in range(1, CTX):
        links.put(xbuf.at[0], xbuf.at[dc], k_ctx + dc, ctx=lax.rem(c + dc, CTX))

    k_pair = links.slot()
    links.put(pair_out, pair_in, k_pair, ctx=2 * y + (1 - core))

    for copy in late_loads:
        copy.wait()
    hidden_t = hidden_ref[...].T
    for k in range(2):
        for f in range(4):
            part = mm(hidden_t, w_s[:, pl.ds((2 * f + k) * FSL, FSL)]).astype(BF16).reshape(Y, 2, HALF, FSL)
            for n in range(Y):
                gs[k, (f - n - 2 * k) % 4, n] = part[n]

    other_core = 2 * y + (1 - core)
    k_g0 = links.slot(8)
    for n in range(X):
        for h in range(2):
            half = pl.ds(2 * h, 2)
            links.put(gs.at[1 - core, n, half], g0.at[n, half], k_g0 + 2 * n + h, ctx=other_core)

    links.got(pair_in, k_pair)
    mine = info
    theirs = pair_in[:, FSL:]
    first = core == 0
    iown[0:BLK] = jnp.where(first, mine, theirs)
    iown[BLK:] = jnp.where(first, theirs, mine)
    k_ifar = links.slot(4)
    for n, dz in enumerate(FAR):
        links.put(iown, ibuf.at[0, n], k_ifar + n, exp=at_z(dz))

    for dc in range(1, CTX):
        links.got(xbuf.at[dc], k_ctx + dc)
    for turn in range(4):
        dy = lax.rem(t + 2 * core + turn, 4)
        target = {"ctx": at_y(dy), "tp": lax.rem(8 - dy + 2 * core, 4)}
        if turn == 0:
            @pl.when(t == 2 * core)
            def _():
                pltpu.make_async_copy(wmix_ref, wbuf.at[t], weight_sem.at[t]).start()

            @pl.when(t != 2 * core)
            def _():
                pltpu.make_async_remote_copy(
                    src_ref=wmix_ref, dst_ref=wbuf.at[t], send_sem=local_sems.at[1], recv_sem=weight_sem.at[t],
                    device_id=target, device_id_type=MESH,
                ).start()
        else:
            copy = pltpu.make_async_remote_copy(
                src_ref=wmix_ref, dst_ref=wbuf.at[t], send_sem=send_sems.at[links.n_send],
                recv_sem=weight_sem.at[t], device_id=target, device_id_type=MESH,
            )
            links.n_send += 1
            copy.start()
            links.started.append(copy)

    entering, arriving = zero, zero
    for other in range(CTX):
        from_slot = lax.rem(c - other + CTX, CTX)
        entering = jnp.where(
            other < c, xbuf[from_slot, 0:NS] * entering + xbuf[from_slot, NS : 2 * NS], entering
        )
    for other in reversed(range(CTX)):
        from_slot = lax.rem(c - other + CTX, CTX)
        arriving = jnp.where(other > c, xbuf[from_slot, 0:NS] * arriving + xbuf[from_slot, 2 * NS :], arriving)

    def scan(i, carry):
        state, back = carry
        for j in range(BLK):
            up = i * BLK + j
            down = TOK - 1 - up
            kept = a_s[up] * state
            ap_s[up] = kept
            state = kept + inf_s[up]
            adjoint = adj_s[down] + back
            adj_s[down] = adjoint
            back = a_s[down] * adjoint
        return state, back

    lax.fori_loop(0, NBLK, scan, (entering, arriving))

    for n in range(4):
        links.got(ibuf.at[0, n], k_ifar + n)
    k_inear = links.slot(3)
    for n, dz in enumerate(near):
        links.put(ibuf.at[0], ibuf.at[1 + n], k_inear + n, exp=at_z(dz))

    rates = rates_ref[...]
    ones8 = jnp.where(iota((BLK, 128), 0) == lax.div(lane8, NS), 1.0, 0.0).astype(BF16)
    tok3, lane3 = iota((BLK, NS, 128), 0), iota((BLK, NS, 128), 2)
    skip = skip_ref[...]

    def gradients(i, carry):
        acc_in, acc_out, acc_decay = carry
        at = pl.ds(pl.multiple_of(i * BLK, BLK), BLK)
        adjoint, kept = adj_s[at], ap_s[at]
        states = (kept + inf_s[at]).reshape(128, CH).astype(BF16)
        adjoint_bf = adjoint.reshape(128, CH).astype(BF16)
        here = lane3 == tok3 + i * BLK
        acc_out += jnp.sum(jnp.where(here, nt(states, g_bf).reshape(BLK, NS, 128), 0.0), axis=0)
        acc_in += jnp.sum(jnp.where(here, nt(adjoint_bf, u_bf).reshape(BLK, NS, 128), 0.0), axis=0)
        through = mm(bsel[at, :].astype(BF16), adjoint_bf)
        product = adjoint * kept
        rated = mm(ones8, (product * rates[None]).reshape(128, CH).astype(BF16))
        step = step_ref[at, :]
        acc_decay += jnp.sum(product * step[:, None, :], axis=0)
        stepg_ref[at, :] = rated + xf[at, :] * through
        ssm_f[at, :] = skip * gf[at, :] + step * through
        return acc_in, acc_out, acc_decay

    acc_in, acc_out, acc_decay = lax.fori_loop(0, NBLK, gradients, (zero, zero, zero))

    ssm_bf = ssm_f[...].astype(BF16)
    sbuf[0, 0] = ssm_bf
    stores = [load(sbuf.at[0, 0], ssm_hbm, 29), load(stepg_ref, stepg_hbm, 30)]
    k_s = links.slot(2 * X)
    for dx in (2, 1, 3):
        links.put(sbuf.at[0, 0], sbuf.at[0, dx], k_s + dx, tp=at_x(dx))
    links.put(sbuf.at[0, 0], sbuf.at[1, 0], k_s + X, ctx=other_core)

    iop[0:2] = acc_in.reshape(2, 8, 128)
    iop[2:4] = acc_out.reshape(2, 8, 128)
    k_iox = links.slot(4)
    for dx in range(1, X):
        links.put(iop.at[at_x(dx)], iop_in.at[dx], k_iox + dx, tp=at_x(dx))
    dsp[0:NS] = acc_decay
    skip_part = jnp.sum(gf[...] * xf[...], axis=0, keepdims=True)
    dsp[NS:] = jnp.broadcast_to(skip_part, (BLK, CH))
    k_dsp = links.slot(CTX)
    for dc in range(1, CTX):
        links.put(dsp, dsp_in.at[dc], k_dsp + dc, ctx=lax.rem(c + dc, CTX))

    for n in range(3):
        links.got(ibuf.at[1 + n], k_inear + n)
    infos = ibuf[...].reshape(256, 128)
    e_f = e.astype(F32)
    hit0 = jnp.where(infos[:, 0:1] == e_f, 1.0, 0.0)
    hit1 = jnp.where(infos[:, 1:2] == e_f, 1.0, 0.0)
    hit = jnp.broadcast_to(hit0 + hit1, (256, 128))
    factor = hit0 * infos[:, 2:3] + hit1 * infos[:, 3:4]
    r256, l256 = iota((256, 256), 0), iota((256, 256), 1)
    before = jnp.where((lax.div(r256, BLK) == lax.div(l256, BLK)) & (r256 > l256), 1.0, 0.0).astype(BF16)
    position = mm(before, hit.astype(BF16))
    tok_row = iota((256, 128), 0)
    tok_near, tok_far = lax.div(tok_row, 64), lax.rem(lax.div(tok_row, 16), 4)
    near_of = jnp.where(tok_near == 1, 1, jnp.where(tok_near == 2, 15, jnp.where(tok_near == 3, 2 + 12 * core, 0)))
    tok_block = lax.rem(e + 4 * Z - near_of - 10 - 4 * tok_far, Z)
    tok_k = lax.rem(lax.div(tok_row, BLK), 2)
    tok_slot = (tok_k * Z + tok_block) * CAP
    slot_of = tok_slot.astype(F32) + position
    picked = jnp.where(iota((256, 128), 1).astype(F32) == slot_of, hit, 0.0)
    sel_s[...] = picked.T.astype(BF16)
    own_scale = jnp.sum(picked * factor, axis=0, keepdims=True)[:, 0 : 2 * HALF]
    zeros96 = jnp.zeros((1, 2 * HALF), F32)
    scale_s[0] = jnp.concatenate([jnp.where(y == n, own_scale, zeros96) for n in range(Y)], axis=1)
    k_scale = links.slot(4)
    for dy in range(1, 4):
        links.put(scale_s.at[0], scale_in.at[dy], k_scale + dy, ctx=at_y(dy))

    for n in range(X):
        for h in range(2):
            links.got(g0.at[n, pl.ds(2 * h, 2)], k_g0 + 2 * n + h)
        gs[core, n] = (gs[core, n].astype(F32) + g0[n].astype(F32)).astype(BF16)

    for n in range(4):
        pltpu.make_async_copy(wbuf.at[n], wbuf.at[n], weight_sem.at[n]).wait()
    for dx in (1, 3, 2):
        links.got(sbuf.at[0, dx], k_s + dx)
        links.put(sbuf.at[0, dx], sbuf.at[1, dx], k_s + X + dx, ctx=other_core)
    for dx in (0, 1, 3, 2):
        links.got(sbuf.at[1, dx], k_s + X + dx)
    k_g1 = links.slot(8)
    for d in (2, 1, 3):
        links.put(gs.at[core, at_x(d), :, 0], g1x.at[d], k_g1 + d, tp=at_x(d))
        links.put(gs.at[core, :, lax.rem(y + d, 4), 1], g1y.at[d], k_g1 + 4 + d, ctx=at_y(d))
    mixer = wbuf[...].reshape(4 * 128, FSL)
    parts = []
    for k in range(2):
        dk = lax.rem(core + k, 2)
        lhs = jnp.concatenate([sbuf[dk, lax.rem(t - n + 4, 4)] for n in range(4)], axis=1)
        parts.append(mm(lhs, mixer).reshape(Z, BLK, FSL))
    chunks = jnp.concatenate(parts, axis=1).astype(BF16)
    for n in range(Z):
        ahead = lax.rem(n + Z - e, Z)
        pbuf[lax.rem(ahead, 4), lax.div(ahead, 4)] = chunks[n]

    k_r1 = links.slot(3)
    for n, dz in enumerate(near):
        links.put(pbuf.at[(3, 1, 0)[n]], rbuf1.at[n], k_r1 + n, exp=at_z(dz))
    for dx in range(1, X):
        links.got(iop_in.at[dx], k_iox + dx)
    iop_far[4] = iop[t] + iop_in[1] + iop_in[2] + iop_in[3]
    k_iof = links.slot(4)
    for n, dz in enumerate(FAR):
        links.put(iop_far.at[4], iop_far.at[n], k_iof + n, exp=at_z(dz))
    for n in range(3):
        links.got(rbuf1.at[n], k_r1 + n)
    k_r2 = links.slot(4)
    for n, dz in ((0, 10), (3, 6), (1, 14), (2, 2)):
        at = (2 + n) % 4
        summed = pbuf[2, at].astype(F32) + rbuf1[0, at].astype(F32) + rbuf1[1, at].astype(F32)
        summed += rbuf1[2, lax.rem(3 - core + n, 4)].astype(F32)
        abuf[n] = summed.astype(BF16)
        links.put(abuf.at[n], rbuf2.at[n], k_r2 + n, exp=at_z(dz))
    own_resid = resid_ref[:, pl.ds(pl.multiple_of(fs * FSL, FSL), FSL)].astype(F32)
    their_resid = pair_in[:, 0:FSL]
    resid = jnp.concatenate(
        [jnp.where(first, own_resid, their_resid), jnp.where(first, their_resid, own_resid)], axis=0
    )
    for n in range(4):
        links.got(rbuf2.at[n], k_r2 + n)
    total = resid
    for n in range(4):
        total += rbuf2[n].astype(F32)

    gown[...] = total.astype(BF16)
    k_a1 = links.slot(4)
    for n, dz in enumerate(FAR):
        links.put(gown, gbuf.at[0, n], k_a1 + n, exp=at_z(dz))
    for d in (1, 3, 2):
        links.got(g1x.at[d], k_g1 + d)
        links.got(g1y.at[d], k_g1 + 4 + d)
    for n in range(4):
        over_x, over_y = gs[core, t, n, 0].astype(F32), gs[core, n, y, 1].astype(F32)
        for d in range(1, 4):
            over_x += g1x[d, n].astype(F32)
            over_y += g1y[d, n].astype(F32)
        a1[n] = over_x.astype(BF16)
        b1[n] = over_y.astype(BF16)
    k_g2 = links.slot(8)
    for d in (2, 1, 3):
        links.put(a1.at[lax.rem(y + d, 4)], g2a.at[d], k_g2 + d, ctx=at_y(d))
        links.put(b1.at[at_x(d)], g2b.at[d], k_g2 + 4 + d, tp=at_x(d))
    for n in range(4):
        links.got(iop_far.at[n], k_iof + n)
    iop_near[0] = iop_far[0] + iop_far[1] + iop_far[2] + iop_far[3]
    for n in range(4):
        links.got(gbuf.at[0, n], k_a1 + n)
    k_a2 = links.slot(3)
    for n, dz in enumerate(near):
        links.put(gbuf.at[0], gbuf.at[1 + n], k_a2 + n, exp=at_z(dz))
    k_ion = links.slot(4)
    for n, dz in enumerate(near):
        links.put(iop_near.at[0], iop_near.at[n + 1], k_ion + n, exp=at_z(dz))
    for d in (1, 3, 2):
        links.got(g2a.at[d], k_g2 + d)
        links.got(g2b.at[d], k_g2 + 4 + d)
    weight_low, weight_high = a1[y].astype(F32), b1[t].astype(F32)
    for d in range(1, 4):
        weight_low += g2a[d].astype(F32)
        weight_high += g2b[d].astype(F32)
    for n in range(3):
        links.got(gbuf.at[1 + n], k_a2 + n)

    picked_rows = mm(sel_s[...], gbuf[...].reshape(256, FSL)).astype(BF16)
    rows[core, t, y, 0] = picked_rows[0:HALF]
    rows[core, t, y, 1] = picked_rows[HALF : 2 * HALF]
    def piece(axis, k, step, d=0):
        if axis == 0:
            return rows.at[k, at_x(step), lax.rem(y + 4 - d, 4), 0]
        return rows.at[k, at_x(4 - d), lax.rem(y + step, 4), 1]

    def pass_on(axis, step, d_from, slot, d):
        device = {"ctx": at_y(d)} if axis == 0 else {"tp": at_x(d)}
        links.put(piece(axis, core, step, d_from), piece(axis, core, step, d_from), slot, **device)

    k_p1, k_p2, k_core = links.slot(8), links.slot(32), links.slot(32)

    def slot_2(axis, step, d):
        return k_p2 + 16 * axis + 4 * step + d

    def to_core(axis, step, d):
        ref = piece(axis, core, step, d)
        links.put(ref, ref, k_core + 16 * axis + 4 * step + d, ctx=other_core)

    def got_1(d):
        for axis in range(2):
            step = 4 - d
            links.got(piece(axis, core, step), k_p1 + 4 * axis + d)
            for to in ((1, 3, 2) if d == 2 else (3, 1)):
                pass_on(axis, step, 0, slot_2(axis, step, to), to)
        for axis in range(2):
            to_core(axis, 4 - d, 0)

    def got_2(step, d, relay=False):
        for axis in range(2):
            links.got(piece(axis, core, step, d), slot_2(axis, step, d))
            if relay:
                pass_on(axis, step, 3, slot_2(axis, step, 2), 3)
        for axis in range(2):
            to_core(axis, step, d)

    for d in (2, 1, 3):
        links.put(rows.at[core, t, y, 0], rows.at[core, t, y, 0], k_p1 + d, tp=at_x(d))
        links.put(rows.at[core, t, y, 1], rows.at[core, t, y, 1], k_p1 + 4 + d, ctx=at_y(d))
    for d in (3, 1):
        for axis in range(2):
            pass_on(axis, 0, 0, slot_2(axis, 0, d), d)
    for axis in range(2):
        to_core(axis, 0, 0)
    product = jnp.concatenate(
        [
            picked_rows[0:HALF].astype(F32) * weight_low,
            picked_rows[HALF : 2 * HALF].astype(F32) * weight_high,
            jnp.zeros((128 - 2 * HALF, FSL), F32),
        ],
        axis=0,
    )
    high = product.astype(BF16)
    low = (product - high.astype(F32)).astype(BF16)
    ones = jnp.ones((BLK, FSL), BF16)
    tot_p[0] = nt(ones, high) + nt(ones, low)
    k_tp = links.slot(2 * X)
    for dk in range(2):
        for dx in range(X):
            if dk or dx:
                links.put(
                    tot_p.at[0], tot_p.at[dk * X + dx], k_tp + dk * X + dx,
                    ctx=2 * y + lax.rem(core + dk, 2), tp=at_x(dx),
                )
    got_1(1)
    got_1(3)
    got_2(0, 3, relay=True)
    got_1(2)
    for n in range(1, 2 * X):
        links.got(tot_p.at[n], k_tp + n)
    slot_total = tot_p[0]
    for n in range(1, 2 * X):
        slot_total += tot_p[n]
    tot_z[0] = slot_total
    k_tz = links.slot(Z)
    for dz in range(1, Z):
        links.put(tot_z.at[0], tot_z.at[dz], k_tz + dz, exp=at_z(dz))

    for n in range(3):
        links.got(iop_near.at[n + 1], k_ion + n)
    iop_out = iop_near[0] + iop_near[1] + iop_near[2] + iop_near[3]
    iop_in[0] = iop_out
    k_ioa = links.slot(4)
    for dx in range(1, X):
        links.put(iop_in.at[0], iop_all.at[t], k_ioa + dx, tp=at_x(dx))
    for dc in range(1, CTX):
        links.got(dsp_in.at[dc], k_dsp + dc)
    sums = dsp[...]
    for dc in range(1, CTX):
        sums += dsp_in[dc]
    decg_ref[...] = sums[0:NS]
    skipg_ref[...] = sums[NS : NS + 1]
    stores += [load(decg_ref, decg_hbm, 31), load(skipg_ref, skipg_hbm, 32)]
    for dy in range(1, 4):
        links.got(scale_in.at[dy], k_scale + dy)
    scale = scale_s[0] + scale_in[1] + scale_in[2] + scale_in[3]

    hidden = hidden_ref[...]
    hidden_scaled = (hidden.astype(F32) * scale).astype(BF16)
    got_2(0, 1)
    got_2(3, 3, relay=True)
    got_2(1, 3, relay=True)
    for step, d in ((3, 1), (1, 1), (0, 2), (2, 1), (2, 3), (3, 2), (1, 2), (2, 2)):
        got_2(step, d)

    direct = jnp.zeros((hidden.shape[0], SLOTS), F32)
    down_stores = []
    for turn in range(2):
        k = core if turn == 0 else 1 - core
        if turn == 1:
            for step in range(4):
                for d in range(4):
                    for axis in range(2):
                        links.got(piece(axis, k, step, d), k_core + 16 * axis + 4 * step + d)
        for f in range(4):
            at = pl.ds(pl.multiple_of((2 * f + k) * FSL, FSL), FSL)
            part = jnp.concatenate([rows[k, lax.rem(f - n - 2 * k + 8, 4), n].reshape(2 * HALF, FSL) for n in range(Y)], axis=0)
            direct += nt(w_s[:, at], part)
            down_ref[:, at] = mm(hidden_scaled, part).astype(BF16)
            down_stores.append(load(down_ref.at[:, at], down_hbm.at[:, at], 21 + 4 * turn + f))
    slot_ref[...] = (direct * scale).astype(BF16)
    stores.append(load(slot_ref, slot_hbm, 33))

    for dx in range(1, X):
        links.got(iop_all.at[at_x(4 - dx)], k_ioa + dx)
    iop_all[t] = iop_out
    inpg_ref[...] = iop_all[0:2].reshape(NS, 128)
    outpg_ref[...] = iop_all[2:4].reshape(NS, 128)
    stores += [load(inpg_ref, inpg_hbm, 34), load(outpg_ref, outpg_hbm, 35)]

    idx0, idx1 = jnp.broadcast_to(info[:, 0:1], (BLK, 128)), jnp.broadcast_to(info[:, 1:2], (BLK, 128))
    pos0, pos1 = jnp.zeros((BLK, 128), F32), jnp.zeros((BLK, 128), F32)
    for i in range(BLK):
        i0, i1 = idx0[i : i + 1], idx1[i : i + 1]
        pos0 += jnp.where((row8 > i) & ((i0 == idx0) | (i1 == idx0)), 1.0, 0.0)
        pos1 += jnp.where((row8 > i) & ((i0 == idx1) | (i1 == idx1)), 1.0, 0.0)
    own_lane = lane8.astype(F32) - ((core * Z + e) * CAP).astype(F32)
    for dz in range(1, Z):
        links.got(tot_z.at[dz], k_tz + dz)
    val0, val1 = jnp.zeros((BLK, 128), F32), jnp.zeros((BLK, 128), F32)
    for dz in range(Z):
        expert = at_z(Z - dz).astype(F32)
        val0 = jnp.where(idx0 == expert, tot_z[dz], val0)
        val1 = jnp.where(idx1 == expert, tot_z[dz], val1)
    out0 = jnp.sum(jnp.where(own_lane == pos0, val0, 0.0), axis=1, keepdims=True)
    out1 = jnp.sum(jnp.where(own_lane == pos1, val1, 0.0), axis=1, keepdims=True)
    diagonal = row8 == lane8
    probg_ref[0:1, :] = jnp.sum(jnp.where(diagonal, out0, 0.0), axis=0, keepdims=True)[:, 0:BLK]
    probg_ref[1:2, :] = jnp.sum(jnp.where(diagonal, out1, 0.0), axis=0, keepdims=True)[:, 0:BLK]
    stores.append(load(probg_ref, probg_hbm, 36))

    @pl.when(t != 2 * core)
    def _():
        pltpu.make_async_copy(wmix_ref, wbuf.at[0], local_sems.at[1]).wait()

    for copy in stores + down_stores:
        copy.wait()
    links.drain()


def store(*refs):
    ins, outs, held, sems = refs[:9], refs[9:18], refs[18:27], refs[27]
    steps = list(zip(ins, held, outs))
    big = steps.pop(7)
    steps += [[ref.at[pl.ds(n * 32, 32)] for ref in big] for n in range(7)]
    loads = [pltpu.make_async_copy(src, mid, sems.at[0, n]) for n, (src, mid, _) in enumerate(steps)]
    stores = [pltpu.make_async_copy(mid, dst, sems.at[1, n]) for n, (_, mid, dst) in enumerate(steps)]
    for copy in loads:
        copy.start()
    for load, save in zip(loads, stores):
        load.wait()
        save.start()
    for copy in stores:
        copy.wait()


def shards(
    mixer_input, step_sizes, decay_rates, input_proj, output_proj, skip_gain, doc_starts, ssm_grad, mixer_in_weight,
    residual_grad, expert_index_pairs, route_probs, hidden_saved, down_weight,
):
    hidden = hidden_saved[0].shape[0]
    features = down_weight.shape[2]
    anywhere = pl.BlockSpec(memory_space=pl.ANY)
    hbm = pl.BlockSpec(memory_space=pltpu.HBM)
    shape = jax.ShapeDtypeStruct
    out = pl.pallas_call(
        body,
        out_shape=(
            shape((TOK, CH), BF16),
            shape((TOK, CH), F32),
            shape((NS, TOK), F32),
            shape((NS, TOK), F32),
            shape((NS, CH), F32),
            shape((1, CH), F32),
            shape((hidden, SLOTS), BF16),
            shape((hidden, features), BF16),
            shape((2, BLK), F32),
        ),
        in_specs=[hbm] * 14,
        out_specs=(hbm,) * 9,
        scratch_shapes=[
            pltpu.VMEM((TOK, CH), BF16),
            pltpu.VMEM((TOK, CH), F32),
            pltpu.VMEM((NS, CH), F32),
            pltpu.VMEM((NS, TOK), F32),
            pltpu.VMEM((NS, TOK), F32),
            pltpu.VMEM((1, CH), F32),
            pltpu.SMEM((TOK,), jnp.int32),
            pltpu.VMEM((TOK, CH), BF16),
            pltpu.VMEM((BLK, features), BF16),
            pltpu.SMEM((2, BLK), jnp.int32),
            pltpu.SMEM((2, BLK), F32),
            pltpu.VMEM((hidden, SLOTS), BF16),
            pltpu.VMEM((hidden, features), BF16),
            pltpu.VMEM((TOK, CH), F32),
            pltpu.VMEM((NS, TOK), F32),
            pltpu.VMEM((NS, TOK), F32),
            pltpu.VMEM((NS, CH), F32),
            pltpu.VMEM((1, CH), F32),
            pltpu.VMEM((hidden, SLOTS), BF16),
            pltpu.VMEM((2, BLK), F32),
            pltpu.VMEM((2, X, Y, 2, HALF, FSL), BF16),
            pltpu.VMEM((X, Y, 2, HALF, FSL), BF16),
            pltpu.VMEM((4, Y, HALF, FSL), BF16),
            pltpu.VMEM((4, X, HALF, FSL), BF16),
            pltpu.VMEM((Y, HALF, FSL), BF16),
            pltpu.VMEM((X, HALF, FSL), BF16),
            pltpu.VMEM((4, HALF, FSL), BF16),
            pltpu.VMEM((4, HALF, FSL), BF16),
            pltpu.VMEM((TOK, CH), F32),
            pltpu.VMEM((TOK, CH), F32),
            pltpu.VMEM((TOK, NS, CH), F32),
            pltpu.VMEM((TOK, NS, CH), F32),
            pltpu.VMEM((TOK, NS, CH), F32),
            pltpu.VMEM((TOK, NS, CH), F32),
            pltpu.VMEM((128, 128), F32),
            pltpu.VMEM((TOK, CH), F32),
            pltpu.VMEM((CTX, 3 * NS, CH), F32),
            pltpu.VMEM((2, X, TOK, CH), BF16),
            pltpu.VMEM((4, 128, FSL), BF16),
            pltpu.VMEM((4, 4, 16, FSL), BF16),
            pltpu.VMEM((3, 4, 16, FSL), BF16),
            pltpu.VMEM((4, 16, FSL), BF16),
            pltpu.VMEM((4, 16, FSL), BF16),
            pltpu.VMEM((4, 4, 16, FSL), BF16),
            pltpu.VMEM((4, 4, 16, 128), F32),
            pltpu.VMEM((16, FSL), BF16),
            pltpu.VMEM((16, 128), F32),
            pltpu.VMEM((BLK, FSL + 128), F32),
            pltpu.VMEM((BLK, FSL + 128), F32),
            pltpu.VMEM((128, 256), BF16),
            pltpu.VMEM((1, 1, SLOTS), F32),
            pltpu.VMEM((4, 1, SLOTS), F32),
            pltpu.VMEM((2, X, Y, 2, HALF, FSL), BF16),
            pltpu.VMEM((hidden, features), BF16),
            pltpu.VMEM((4, 8, 128), F32),
            pltpu.VMEM((4, 8, 128), F32),
            pltpu.VMEM((5, 8, 128), F32),
            pltpu.VMEM((4, 8, 128), F32),
            pltpu.VMEM((4, 8, 128), F32),
            pltpu.VMEM((NS + BLK, CH), F32),
            pltpu.VMEM((CTX, NS + BLK, CH), F32),
            pltpu.VMEM((2 * X, BLK, 128), F32),
            pltpu.VMEM((Z, BLK, 128), F32),
            pltpu.SemaphoreType.DMA((NSEM,)),
            pltpu.SemaphoreType.DMA((NSEM,)),
            pltpu.SemaphoreType.DMA((40,)),
            pltpu.SemaphoreType.DMA((4,)),
        ],
        compiler_params=pltpu.CompilerParams(
            collective_id=0, has_side_effects=True, vmem_limit_bytes=VMEM_LIMIT
        ),
        name="scan_and_experts",
    )(
        mixer_input, step_sizes, decay_rates, input_proj, output_proj, skip_gain.reshape(1, CH), doc_starts, ssm_grad,
        mixer_in_weight, residual_grad, expert_index_pairs.T, route_probs.T, hidden_saved[0], down_weight[0],
    )
    ssm, stepg, inpg, outpg, decg, skipg, slot, down, probg = pl.pallas_call(
        store,
        out_shape=tuple(shape(array.shape, array.dtype) for array in out),
        in_specs=[anywhere] * 9,
        out_specs=tuple([hbm] * 9),
        scratch_shapes=[pltpu.VMEM(array.shape, array.dtype) for array in out] + [pltpu.SemaphoreType.DMA((2, 16))],
        compiler_params=pltpu.CompilerParams(vmem_limit_bytes=VMEM_LIMIT),
        name="store_results",
    )(*out)
    return ssm, stepg, inpg, outpg, decg, skipg.reshape(CH), slot[None], down[None], probg.T


def solution(mesh):
    return jax.shard_map(
        shards,
        mesh=mesh,
        in_specs=(
            P("ctx", ("exp", "tp")),
            P("ctx", ("exp", "tp")),
            P(None, ("exp", "tp")),
            P(None, "ctx"),
            P(None, "ctx"),
            P(("exp", "tp")),
            P("ctx"),
            P("ctx", ("exp", "tp")),
            P(("exp", "tp"), "ctx"),
            P(("ctx", "exp"), None),
            P(("ctx", "exp"), None),
            P(("ctx", "exp"), None),
            P("exp", ("ctx", "tp"), None),
            P("exp", ("ctx", "tp"), None),
        ),
        out_specs=(
            P("ctx", ("exp", "tp")),
            P("ctx", ("exp", "tp")),
            P(None, "ctx"),
            P(None, "ctx"),
            P(None, ("exp", "tp")),
            P(("exp", "tp")),
            P("exp", ("ctx", "tp"), None),
            P("exp", ("ctx", "tp"), None),
            P(("ctx", "exp"), None),
        ),
        check_vma=False,
    )
```

```python
import jax
import jax.numpy as jnp
from jax import lax
from jax.experimental import pallas as pl
from jax.experimental.pallas import tpu as pltpu
from jax.sharding import PartitionSpec as P

F32 = jnp.float32
BF16 = jnp.bfloat16
MESH = pl.DeviceIdType.MESH

TOK = 128
CH = 128
NS = 16
BLK = 8
NBLK = TOK // BLK
Y, CORES, Z, X = 4, 2, 16, 4
CTX = Y * CORES
FSL = 512
CAP = 3
HALF = Z * CAP
SLOTS = CTX * HALF
FAR = (10, 14, 2, 6)


def nt(a, b):
    return lax.dot_general(a, b, (((1,), (1,)), ((), ())), preferred_element_type=F32)


def mm(a, b):
    return jnp.dot(a, b, preferred_element_type=F32)


def iota(shape, dim):
    return lax.broadcasted_iota(jnp.int32, shape, dim)


class Links:
    def __init__(self, send, recv):
        self.send, self.recv = send, recv
        self.n_send = self.n_recv = 0
        self.started = []

    def slot(self, n=1):
        first = self.n_recv
        self.n_recv += n
        assert self.n_recv <= NSEM
        return first

    def put(self, src, dst, recv_index, **device):
        copy = pltpu.make_async_remote_copy(
            src_ref=src,
            dst_ref=dst,
            send_sem=self.send.at[self.n_send],
            recv_sem=self.recv.at[recv_index],
            device_id=device,
            device_id_type=MESH,
        )
        self.n_send += 1
        assert self.n_send <= NSEM
        copy.start()
        self.started.append(copy)
        return copy

    def got(self, dst, recv_index):
        pltpu.make_async_copy(dst, dst, self.recv.at[recv_index]).wait()

    def drain(self):
        for copy in self.started:
            copy.wait_send()
        self.started = []


NSEM = 256
VMEM_LIMIT = 60 * 1024 * 1024


def body(
    x_hbm, step_hbm, rates_hbm, inp_hbm, outp_hbm, skip_hbm, doc_hbm, g_hbm, wmix_ref, resid_hbm,
    idx_hbm, prob_hbm, hidden_hbm, weight_ref,
    ssm_hbm, stepg_hbm, inpg_hbm, outpg_hbm, decg_hbm, skipg_hbm, slot_hbm, down_hbm, probg_hbm,
    x_ref, step_ref, rates_ref, inp_ref, outp_ref, skip_ref, doc_ref, g_ref, resid_ref, idx_ref, prob_ref, hidden_ref, down_ref,
    stepg_ref, inpg_ref, outpg_ref, decg_ref, skipg_ref, slot_ref, probg_ref,
    gs, g0, g1x, g1y, a1, b1, g2a, g2b,
    xf, gf, a_s, inf_s, adj_s, ap_s, bsel, ssm_f, xbuf, sbuf, wbuf, pbuf, rbuf1, abuf, rbuf2,
    gbuf, ibuf, gown, iown, pair_out, pair_in, sel_s, scale_s, scale_in, rows, w_s,
    iop, iop_in, iop_far, iop_near, iop_all, dsp, dsp_in, tot_p, tot_z,
    send_sems, recv_sems, local_sems, weight_sem,
):
    links = Links(send_sems, recv_sems)
    c, e, t = lax.axis_index("ctx"), lax.axis_index("exp"), lax.axis_index("tp")
    y, core = lax.div(c, 2), lax.rem(c, 2)
    fs = 2 * lax.rem(t + y + 2 * core, 4) + core

    def at_y(dy):
        return 2 * lax.rem(y + dy, 4) + core

    def at_x(dx):
        return lax.rem(t + dx, 4)

    def at_z(dz):
        return lax.rem(e + dz, Z)

    def load(src, dst, at):
        copy = pltpu.make_async_copy(src, dst, local_sems.at[at])
        copy.start()
        return copy

    scan_loads = [
        load(src, dst, 2 + n)
        for n, (src, dst) in enumerate((
            (step_hbm, step_ref), (rates_hbm, rates_ref), (x_hbm, x_ref), (g_hbm, g_ref), (inp_hbm, inp_ref),
            (outp_hbm, outp_ref), (doc_hbm, doc_ref), (skip_hbm, skip_ref), (idx_hbm, idx_ref),
            (prob_hbm, prob_ref), (resid_hbm, resid_ref),
        ))
    ]
    late_loads = [load(hidden_hbm, hidden_ref, 13)]
    for n in range(7):
        part = pl.ds(n * 32, 32)
        late_loads.append(load(weight_ref.at[part], w_s.at[part], 14 + n))

    barrier = pltpu.get_barrier_semaphore()
    partners = 0
    for dc in range(CTX):
        for dx in range(X):
            if dc or dx:
                pl.semaphore_signal(
                    barrier, inc=1, device_id={"ctx": lax.rem(c + dc, CTX), "tp": at_x(dx)}, device_id_type=MESH
                )
                partners += 1
    for dz in range(1, Z):
        pl.semaphore_signal(barrier, inc=1, device_id={"exp": at_z(dz)}, device_id_type=MESH)
        partners += 1

    near = (1, 15, 2 + 12 * core)
    for copy in scan_loads:
        copy.wait()

    lane8 = iota((BLK, 128), 1)
    row8 = iota((BLK, 128), 0)
    info = jnp.zeros((BLK, 128), F32)
    for i in range(BLK):
        for k in range(2):
            info = jnp.where((row8 == i) & (lane8 == k), idx_ref[k, i].astype(F32), info)
            info = jnp.where((row8 == i) & (lane8 == 2 + k), prob_ref[k, i], info)
    info = info.astype(BF16).astype(F32)
    other_fs = 2 * lax.rem(t + y + 2 * (1 - core), 4) + (1 - core)
    pair_out[:, 0:FSL] = resid_ref[:, pl.ds(pl.multiple_of(other_fs * FSL, FSL), FSL)].astype(F32)
    pair_out[:, FSL:] = info
    xf[...] = x_ref[...].astype(F32)
    gf[...] = g_ref[...].astype(F32)
    g_bf = g_ref[...]
    u_bf = (step_ref[...] * xf[...]).astype(BF16)
    row, lane = iota((128, 128), 0), iota((128, 128), 1)
    b_tile = jnp.concatenate([inp_ref[...]] * BLK, axis=0)
    c_tile = jnp.concatenate([outp_ref[...]] * BLK, axis=0)
    bsel[...] = jnp.where(lax.rem(row, BLK) == lax.div(lane, NS), b_tile.T, 0.0)
    row_tok = lax.div(row, NS)

    def prepare(i, carry):
        at = pl.ds(pl.multiple_of(i * BLK, BLK), BLK)
        here = lane == row_tok + i * BLK
        decays = jnp.exp(step_ref[at, :][:, None, :] * rates_ref[...][None])
        for j in range(BLK):
            keep = (1 - doc_ref[i * BLK + j]).astype(F32)
            a_s[i * BLK + j] = decays[j] * keep
        inf_s[at] = mm(jnp.where(here, b_tile, 0.0).astype(BF16), u_bf).reshape(BLK, NS, CH)
        adj_s[at] = mm(jnp.where(here, c_tile, 0.0).astype(BF16), g_bf).reshape(BLK, NS, CH)
        return carry

    lax.fori_loop(0, NBLK, prepare, 0)

    zero = jnp.zeros((NS, CH), F32)

    def summarise(i, carry):
        state, back, damp = carry
        for j in range(BLK):
            up = i * BLK + j
            down = TOK - 1 - up
            decay = a_s[up]
            state = decay * state + inf_s[up]
            damp = damp * decay
            back = a_s[down] * (adj_s[down] + back)
        return state, back, damp

    state, back, damp = lax.fori_loop(0, NBLK, summarise, (zero, zero, zero + 1.0))
    xbuf[0, 0:NS] = damp
    xbuf[0, NS : 2 * NS] = state
    xbuf[0, 2 * NS :] = back
    pl.semaphore_wait(barrier, partners)
    k_ctx = links.slot(CTX)
    for dc in range(1, CTX):
        links.put(xbuf.at[0], xbuf.at[dc], k_ctx + dc, ctx=lax.rem(c + dc, CTX))

    k_pair = links.slot()
    links.put(pair_out, pair_in, k_pair, ctx=2 * y + (1 - core))

    for copy in late_loads:
        copy.wait()
    hidden_t = hidden_ref[...].T
    for k in range(2):
        for f in range(4):
            part = mm(hidden_t, w_s[:, pl.ds((2 * f + k) * FSL, FSL)]).astype(BF16).reshape(Y, 2, HALF, FSL)
            for n in range(Y):
                gs[k, (f - n - 2 * k) % 4, n] = part[n]

    other_core = 2 * y + (1 - core)
    k_g0 = links.slot(8)
    for n in range(X):
        for h in range(2):
            half = pl.ds(2 * h, 2)
            links.put(gs.at[1 - core, n, half], g0.at[n, half], k_g0 + 2 * n + h, ctx=other_core)

    links.got(pair_in, k_pair)
    mine = info
    theirs = pair_in[:, FSL:]
    first = core == 0
    iown[0:BLK] = jnp.where(first, mine, theirs)
    iown[BLK:] = jnp.where(first, theirs, mine)
    k_ifar = links.slot(4)
    for n, dz in enumerate(FAR):
        links.put(iown, ibuf.at[0, n], k_ifar + n, exp=at_z(dz))

    for dc in range(1, CTX):
        links.got(xbuf.at[dc], k_ctx + dc)
    for turn in range(4):
        dy = lax.rem(t + 2 * core + turn, 4)
        target = {"ctx": at_y(dy), "tp": lax.rem(8 - dy + 2 * core, 4)}
        if turn == 0:
            @pl.when(t == 2 * core)
            def _():
                pltpu.make_async_copy(wmix_ref, wbuf.at[t], weight_sem.at[t]).start()

            @pl.when(t != 2 * core)
            def _():
                pltpu.make_async_remote_copy(
                    src_ref=wmix_ref, dst_ref=wbuf.at[t], send_sem=local_sems.at[1], recv_sem=weight_sem.at[t],
                    device_id=target, device_id_type=MESH,
                ).start()
        else:
            copy = pltpu.make_async_remote_copy(
                src_ref=wmix_ref, dst_ref=wbuf.at[t], send_sem=send_sems.at[links.n_send],
                recv_sem=weight_sem.at[t], device_id=target, device_id_type=MESH,
            )
            links.n_send += 1
            copy.start()
            links.started.append(copy)

    entering, arriving = zero, zero
    for other in range(CTX):
        from_slot = lax.rem(c - other + CTX, CTX)
        entering = jnp.where(
            other < c, xbuf[from_slot, 0:NS] * entering + xbuf[from_slot, NS : 2 * NS], entering
        )
    for other in reversed(range(CTX)):
        from_slot = lax.rem(c - other + CTX, CTX)
        arriving = jnp.where(other > c, xbuf[from_slot, 0:NS] * arriving + xbuf[from_slot, 2 * NS :], arriving)

    def scan(i, carry):
        state, back = carry
        for j in range(BLK):
            up = i * BLK + j
            down = TOK - 1 - up
            kept = a_s[up] * state
            ap_s[up] = kept
            state = kept + inf_s[up]
            adjoint = adj_s[down] + back
            adj_s[down] = adjoint
            back = a_s[down] * adjoint
        return state, back

    lax.fori_loop(0, NBLK, scan, (entering, arriving))

    for n in range(4):
        links.got(ibuf.at[0, n], k_ifar + n)
    k_inear = links.slot(3)
    for n, dz in enumerate(near):
        links.put(ibuf.at[0], ibuf.at[1 + n], k_inear + n, exp=at_z(dz))

    rates = rates_ref[...]
    ones8 = jnp.where(iota((BLK, 128), 0) == lax.div(lane8, NS), 1.0, 0.0).astype(BF16)
    tok3, lane3 = iota((BLK, NS, 128), 0), iota((BLK, NS, 128), 2)
    skip = skip_ref[...]

    def gradients(i, carry):
        acc_in, acc_out, acc_decay = carry
        at = pl.ds(pl.multiple_of(i * BLK, BLK), BLK)
        adjoint, kept = adj_s[at], ap_s[at]
        states = (kept + inf_s[at]).reshape(128, CH).astype(BF16)
        adjoint_bf = adjoint.reshape(128, CH).astype(BF16)
        here = lane3 == tok3 + i * BLK
        acc_out += jnp.sum(jnp.where(here, nt(states, g_bf).reshape(BLK, NS, 128), 0.0), axis=0)
        acc_in += jnp.sum(jnp.where(here, nt(adjoint_bf, u_bf).reshape(BLK, NS, 128), 0.0), axis=0)
        through = mm(bsel[at, :].astype(BF16), adjoint_bf)
        product = adjoint * kept
        rated = mm(ones8, (product * rates[None]).reshape(128, CH).astype(BF16))
        step = step_ref[at, :]
        acc_decay += jnp.sum(product * step[:, None, :], axis=0)
        stepg_ref[at, :] = rated + xf[at, :] * through
        ssm_f[at, :] = skip * gf[at, :] + step * through
        return acc_in, acc_out, acc_decay

    acc_in, acc_out, acc_decay = lax.fori_loop(0, NBLK, gradients, (zero, zero, zero))

    ssm_bf = ssm_f[...].astype(BF16)
    sbuf[0, 0] = ssm_bf
    stores = [load(sbuf.at[0, 0], ssm_hbm, 29), load(stepg_ref, stepg_hbm, 30)]
    k_s = links.slot(2 * X)
    for dx in (2, 1, 3):
        links.put(sbuf.at[0, 0], sbuf.at[0, dx], k_s + dx, tp=at_x(dx))
    links.put(sbuf.at[0, 0], sbuf.at[1, 0], k_s + X, ctx=other_core)

    iop[0:2] = acc_in.reshape(2, 8, 128)
    iop[2:4] = acc_out.reshape(2, 8, 128)
    k_iox = links.slot(4)
    for dx in range(1, X):
        links.put(iop.at[at_x(dx)], iop_in.at[dx], k_iox + dx, tp=at_x(dx))
    dsp[0:NS] = acc_decay
    skip_part = jnp.sum(gf[...] * xf[...], axis=0, keepdims=True)
    dsp[NS:] = jnp.broadcast_to(skip_part, (BLK, CH))
    k_dsp = links.slot(CTX)
    for dc in range(1, CTX):
        links.put(dsp, dsp_in.at[dc], k_dsp + dc, ctx=lax.rem(c + dc, CTX))

    for n in range(3):
        links.got(ibuf.at[1 + n], k_inear + n)
    infos = ibuf[...].reshape(256, 128)
    e_f = e.astype(F32)
    hit0 = jnp.where(infos[:, 0:1] == e_f, 1.0, 0.0)
    hit1 = jnp.where(infos[:, 1:2] == e_f, 1.0, 0.0)
    hit = jnp.broadcast_to(hit0 + hit1, (256, 128))
    factor = hit0 * infos[:, 2:3] + hit1 * infos[:, 3:4]
    r256, l256 = iota((256, 256), 0), iota((256, 256), 1)
    before = jnp.where((lax.div(r256, BLK) == lax.div(l256, BLK)) & (r256 > l256), 1.0, 0.0).astype(BF16)
    position = mm(before, hit.astype(BF16))
    tok_row = iota((256, 128), 0)
    tok_near, tok_far = lax.div(tok_row, 64), lax.rem(lax.div(tok_row, 16), 4)
    near_of = jnp.where(tok_near == 1, 1, jnp.where(tok_near == 2, 15, jnp.where(tok_near == 3, 2 + 12 * core, 0)))
    tok_block = lax.rem(e + 4 * Z - near_of - 10 - 4 * tok_far, Z)
    tok_k = lax.rem(lax.div(tok_row, BLK), 2)
    tok_slot = (tok_k * Z + tok_block) * CAP
    slot_of = tok_slot.astype(F32) + position
    picked = jnp.where(iota((256, 128), 1).astype(F32) == slot_of, hit, 0.0)
    sel_s[...] = picked.T.astype(BF16)
    own_scale = jnp.sum(picked * factor, axis=0, keepdims=True)[:, 0 : 2 * HALF]
    zeros96 = jnp.zeros((1, 2 * HALF), F32)
    scale_s[0] = jnp.concatenate([jnp.where(y == n, own_scale, zeros96) for n in range(Y)], axis=1)
    k_scale = links.slot(4)
    for dy in range(1, 4):
        links.put(scale_s.at[0], scale_in.at[dy], k_scale + dy, ctx=at_y(dy))

    for n in range(X):
        for h in range(2):
            links.got(g0.at[n, pl.ds(2 * h, 2)], k_g0 + 2 * n + h)
        gs[core, n] = (gs[core, n].astype(F32) + g0[n].astype(F32)).astype(BF16)

    for n in range(4):
        pltpu.make_async_copy(wbuf.at[n], wbuf.at[n], weight_sem.at[n]).wait()
    for dx in (1, 3, 2):
        links.got(sbuf.at[0, dx], k_s + dx)
        links.put(sbuf.at[0, dx], sbuf.at[1, dx], k_s + X + dx, ctx=other_core)
    for dx in (0, 1, 3, 2):
        links.got(sbuf.at[1, dx], k_s + X + dx)
    k_g1 = links.slot(8)
    for d in (2, 1, 3):
        links.put(gs.at[core, at_x(d), :, 0], g1x.at[d], k_g1 + d, tp=at_x(d))
        links.put(gs.at[core, :, lax.rem(y + d, 4), 1], g1y.at[d], k_g1 + 4 + d, ctx=at_y(d))
    mixer = wbuf[...].reshape(4 * 128, FSL)
    parts = []
    for k in range(2):
        dk = lax.rem(core + k, 2)
        lhs = jnp.concatenate([sbuf[dk, lax.rem(t - n + 4, 4)] for n in range(4)], axis=1)
        parts.append(mm(lhs, mixer).reshape(Z, BLK, FSL))
    chunks = jnp.concatenate(parts, axis=1).astype(BF16)
    for n in range(Z):
        ahead = lax.rem(n + Z - e, Z)
        pbuf[lax.rem(ahead, 4), lax.div(ahead, 4)] = chunks[n]

    k_r1 = links.slot(3)
    for n, dz in enumerate(near):
        links.put(pbuf.at[(3, 1, 0)[n]], rbuf1.at[n], k_r1 + n, exp=at_z(dz))
    for dx in range(1, X):
        links.got(iop_in.at[dx], k_iox + dx)
    iop_far[4] = iop[t] + iop_in[1] + iop_in[2] + iop_in[3]
    k_iof = links.slot(4)
    for n, dz in enumerate(FAR):
        links.put(iop_far.at[4], iop_far.at[n], k_iof + n, exp=at_z(dz))
    for n in range(3):
        links.got(rbuf1.at[n], k_r1 + n)
    k_r2 = links.slot(4)
    for n, dz in ((0, 10), (3, 6), (1, 14), (2, 2)):
        at = (2 + n) % 4
        summed = pbuf[2, at].astype(F32) + rbuf1[0, at].astype(F32) + rbuf1[1, at].astype(F32)
        summed += rbuf1[2, lax.rem(3 - core + n, 4)].astype(F32)
        abuf[n] = summed.astype(BF16)
        links.put(abuf.at[n], rbuf2.at[n], k_r2 + n, exp=at_z(dz))
    own_resid = resid_ref[:, pl.ds(pl.multiple_of(fs * FSL, FSL), FSL)].astype(F32)
    their_resid = pair_in[:, 0:FSL]
    resid = jnp.concatenate(
        [jnp.where(first, own_resid, their_resid), jnp.where(first, their_resid, own_resid)], axis=0
    )
    for n in range(4):
        links.got(rbuf2.at[n], k_r2 + n)
    total = resid
    for n in range(4):
        total += rbuf2[n].astype(F32)

    gown[...] = total.astype(BF16)
    k_a1 = links.slot(4)
    for n, dz in enumerate(FAR):
        links.put(gown, gbuf.at[0, n], k_a1 + n, exp=at_z(dz))
    for d in (1, 3, 2):
        links.got(g1x.at[d], k_g1 + d)
        links.got(g1y.at[d], k_g1 + 4 + d)
    for n in range(4):
        over_x, over_y = gs[core, t, n, 0].astype(F32), gs[core, n, y, 1].astype(F32)
        for d in range(1, 4):
            over_x += g1x[d, n].astype(F32)
            over_y += g1y[d, n].astype(F32)
        a1[n] = over_x.astype(BF16)
        b1[n] = over_y.astype(BF16)
    k_g2 = links.slot(8)
    for d in (2, 1, 3):
        links.put(a1.at[lax.rem(y + d, 4)], g2a.at[d], k_g2 + d, ctx=at_y(d))
        links.put(b1.at[at_x(d)], g2b.at[d], k_g2 + 4 + d, tp=at_x(d))
    for n in range(4):
        links.got(iop_far.at[n], k_iof + n)
    iop_near[0] = iop_far[0] + iop_far[1] + iop_far[2] + iop_far[3]
    for n in range(4):
        links.got(gbuf.at[0, n], k_a1 + n)
    k_a2 = links.slot(3)
    for n, dz in enumerate(near):
        links.put(gbuf.at[0], gbuf.at[1 + n], k_a2 + n, exp=at_z(dz))
    k_ion = links.slot(4)
    for n, dz in enumerate(near):
        links.put(iop_near.at[0], iop_near.at[n + 1], k_ion + n, exp=at_z(dz))
    for d in (1, 3, 2):
        links.got(g2a.at[d], k_g2 + d)
        links.got(g2b.at[d], k_g2 + 4 + d)
    weight_low, weight_high = a1[y].astype(F32), b1[t].astype(F32)
    for d in range(1, 4):
        weight_low += g2a[d].astype(F32)
        weight_high += g2b[d].astype(F32)
    for n in range(3):
        links.got(gbuf.at[1 + n], k_a2 + n)

    picked_rows = mm(sel_s[...], gbuf[...].reshape(256, FSL)).astype(BF16)
    rows[core, t, y, 0] = picked_rows[0:HALF]
    rows[core, t, y, 1] = picked_rows[HALF : 2 * HALF]
    def piece(axis, k, step, d=0):
        if axis == 0:
            return rows.at[k, at_x(step), lax.rem(y + 4 - d, 4), 0]
        return rows.at[k, at_x(4 - d), lax.rem(y + step, 4), 1]

    def pass_on(axis, step, d_from, slot, d):
        device = {"ctx": at_y(d)} if axis == 0 else {"tp": at_x(d)}
        links.put(piece(axis, core, step, d_from), piece(axis, core, step, d_from), slot, **device)

    k_p1, k_p2, k_core = links.slot(8), links.slot(32), links.slot(32)

    def slot_2(axis, step, d):
        return k_p2 + 16 * axis + 4 * step + d

    def to_core(axis, step, d):
        ref = piece(axis, core, step, d)
        links.put(ref, ref, k_core + 16 * axis + 4 * step + d, ctx=other_core)

    def got_1(d):
        for axis in range(2):
            step = 4 - d
            links.got(piece(axis, core, step), k_p1 + 4 * axis + d)
            for to in ((1, 3, 2) if d == 2 else (3, 1)):
                pass_on(axis, step, 0, slot_2(axis, step, to), to)
        for axis in range(2):
            to_core(axis, 4 - d, 0)

    def got_2(step, d, relay=False):
        for axis in range(2):
            links.got(piece(axis, core, step, d), slot_2(axis, step, d))
            if relay:
                pass_on(axis, step, 3, slot_2(axis, step, 2), 3)
        for axis in range(2):
            to_core(axis, step, d)

    for d in (2, 1, 3):
        links.put(rows.at[core, t, y, 0], rows.at[core, t, y, 0], k_p1 + d, tp=at_x(d))
        links.put(rows.at[core, t, y, 1], rows.at[core, t, y, 1], k_p1 + 4 + d, ctx=at_y(d))
    for d in (3, 1):
        for axis in range(2):
            pass_on(axis, 0, 0, slot_2(axis, 0, d), d)
    for axis in range(2):
        to_core(axis, 0, 0)
    got_1(1)
    got_1(3)
    product = jnp.concatenate(
        [
            picked_rows[0:HALF].astype(F32) * weight_low,
            picked_rows[HALF : 2 * HALF].astype(F32) * weight_high,
            jnp.zeros((128 - 2 * HALF, FSL), F32),
        ],
        axis=0,
    )
    high = product.astype(BF16)
    low = (product - high.astype(F32)).astype(BF16)
    ones = jnp.ones((BLK, FSL), BF16)
    tot_p[0] = nt(ones, high) + nt(ones, low)
    k_tp = links.slot(2 * X)
    for dk in range(2):
        for dx in range(X):
            if dk or dx:
                links.put(
                    tot_p.at[0], tot_p.at[dk * X + dx], k_tp + dk * X + dx,
                    ctx=2 * y + lax.rem(core + dk, 2), tp=at_x(dx),
                )
    got_2(0, 3, relay=True)
    got_1(2)
    for n in range(1, 2 * X):
        links.got(tot_p.at[n], k_tp + n)
    slot_total = tot_p[0]
    for n in range(1, 2 * X):
        slot_total += tot_p[n]
    tot_z[0] = slot_total
    k_tz = links.slot(Z)
    for dz in range(1, Z):
        links.put(tot_z.at[0], tot_z.at[dz], k_tz + dz, exp=at_z(dz))

    for n in range(3):
        links.got(iop_near.at[n + 1], k_ion + n)
    iop_out = iop_near[0] + iop_near[1] + iop_near[2] + iop_near[3]
    iop_in[0] = iop_out
    k_ioa = links.slot(4)
    for dx in range(1, X):
        links.put(iop_in.at[0], iop_all.at[t], k_ioa + dx, tp=at_x(dx))
    for dc in range(1, CTX):
        links.got(dsp_in.at[dc], k_dsp + dc)
    sums = dsp[...]
    for dc in range(1, CTX):
        sums += dsp_in[dc]
    decg_ref[...] = sums[0:NS]
    skipg_ref[...] = sums[NS : NS + 1]
    stores += [load(decg_ref, decg_hbm, 31), load(skipg_ref, skipg_hbm, 32)]
    for dy in range(1, 4):
        links.got(scale_in.at[dy], k_scale + dy)
    scale = scale_s[0] + scale_in[1] + scale_in[2] + scale_in[3]

    hidden = hidden_ref[...]
    hidden_scaled = (hidden.astype(F32) * scale).astype(BF16)
    got_2(0, 1)
    got_2(3, 3, relay=True)
    got_2(1, 3, relay=True)
    for step, d in ((3, 1), (1, 1), (0, 2), (2, 1), (2, 3), (3, 2), (1, 2), (2, 2)):
        got_2(step, d)

    direct = jnp.zeros((hidden.shape[0], SLOTS), F32)
    down_stores = []
    for turn in range(2):
        k = core if turn == 0 else 1 - core
        if turn == 1:
            for step in range(4):
                for d in range(4):
                    for axis in range(2):
                        links.got(piece(axis, k, step, d), k_core + 16 * axis + 4 * step + d)
        for f in range(4):
            at = pl.ds(pl.multiple_of((2 * f + k) * FSL, FSL), FSL)
            part = jnp.concatenate([rows[k, lax.rem(f - n - 2 * k + 8, 4), n].reshape(2 * HALF, FSL) for n in range(Y)], axis=0)
            direct += nt(w_s[:, at], part)
            down_ref[:, at] = mm(hidden_scaled, part).astype(BF16)
            down_stores.append(load(down_ref.at[:, at], down_hbm.at[:, at], 21 + 4 * turn + f))
    slot_ref[...] = (direct * scale).astype(BF16)
    stores.append(load(slot_ref, slot_hbm, 33))

    for dx in range(1, X):
        links.got(iop_all.at[at_x(4 - dx)], k_ioa + dx)
    iop_all[t] = iop_out
    inpg_ref[...] = iop_all[0:2].reshape(NS, 128)
    outpg_ref[...] = iop_all[2:4].reshape(NS, 128)
    stores += [load(inpg_ref, inpg_hbm, 34), load(outpg_ref, outpg_hbm, 35)]

    idx0, idx1 = jnp.broadcast_to(info[:, 0:1], (BLK, 128)), jnp.broadcast_to(info[:, 1:2], (BLK, 128))
    pos0, pos1 = jnp.zeros((BLK, 128), F32), jnp.zeros((BLK, 128), F32)
    for i in range(BLK):
        i0, i1 = idx0[i : i + 1], idx1[i : i + 1]
        pos0 += jnp.where((row8 > i) & ((i0 == idx0) | (i1 == idx0)), 1.0, 0.0)
        pos1 += jnp.where((row8 > i) & ((i0 == idx1) | (i1 == idx1)), 1.0, 0.0)
    own_lane = lane8.astype(F32) - ((core * Z + e) * CAP).astype(F32)
    for dz in range(1, Z):
        links.got(tot_z.at[dz], k_tz + dz)
    val0, val1 = jnp.zeros((BLK, 128), F32), jnp.zeros((BLK, 128), F32)
    for dz in range(Z):
        expert = at_z(Z - dz).astype(F32)
        val0 = jnp.where(idx0 == expert, tot_z[dz], val0)
        val1 = jnp.where(idx1 == expert, tot_z[dz], val1)
    out0 = jnp.sum(jnp.where(own_lane == pos0, val0, 0.0), axis=1, keepdims=True)
    out1 = jnp.sum(jnp.where(own_lane == pos1, val1, 0.0), axis=1, keepdims=True)
    diagonal = row8 == lane8
    probg_ref[0:1, :] = jnp.sum(jnp.where(diagonal, out0, 0.0), axis=0, keepdims=True)[:, 0:BLK]
    probg_ref[1:2, :] = jnp.sum(jnp.where(diagonal, out1, 0.0), axis=0, keepdims=True)[:, 0:BLK]
    stores.append(load(probg_ref, probg_hbm, 36))

    @pl.when(t != 2 * core)
    def _():
        pltpu.make_async_copy(wmix_ref, wbuf.at[0], local_sems.at[1]).wait()

    for copy in stores + down_stores:
        copy.wait()
    links.drain()


def store(*refs):
    ins, outs, held, sems = refs[:9], refs[9:18], refs[18:27], refs[27]
    steps = list(zip(ins, held, outs))
    big = steps.pop(7)
    steps += [[ref.at[pl.ds(n * 32, 32)] for ref in big] for n in range(7)]
    loads = [pltpu.make_async_copy(src, mid, sems.at[0, n]) for n, (src, mid, _) in enumerate(steps)]
    stores = [pltpu.make_async_copy(mid, dst, sems.at[1, n]) for n, (_, mid, dst) in enumerate(steps)]
    for copy in loads:
        copy.start()
    for load, save in zip(loads, stores):
        load.wait()
        save.start()
    for copy in stores:
        copy.wait()


def shards(
    mixer_input, step_sizes, decay_rates, input_proj, output_proj, skip_gain, doc_starts, ssm_grad, mixer_in_weight,
    residual_grad, expert_index_pairs, route_probs, hidden_saved, down_weight,
):
    hidden = hidden_saved[0].shape[0]
    features = down_weight.shape[2]
    anywhere = pl.BlockSpec(memory_space=pl.ANY)
    hbm = pl.BlockSpec(memory_space=pltpu.HBM)
    shape = jax.ShapeDtypeStruct
    out = pl.pallas_call(
        body,
        out_shape=(
            shape((TOK, CH), BF16),
            shape((TOK, CH), F32),
            shape((NS, TOK), F32),
            shape((NS, TOK), F32),
            shape((NS, CH), F32),
            shape((1, CH), F32),
            shape((hidden, SLOTS), BF16),
            shape((hidden, features), BF16),
            shape((2, BLK), F32),
        ),
        in_specs=[hbm] * 14,
        out_specs=(hbm,) * 9,
        scratch_shapes=[
            pltpu.VMEM((TOK, CH), BF16),
            pltpu.VMEM((TOK, CH), F32),
            pltpu.VMEM((NS, CH), F32),
            pltpu.VMEM((NS, TOK), F32),
            pltpu.VMEM((NS, TOK), F32),
            pltpu.VMEM((1, CH), F32),
            pltpu.SMEM((TOK,), jnp.int32),
            pltpu.VMEM((TOK, CH), BF16),
            pltpu.VMEM((BLK, features), BF16),
            pltpu.SMEM((2, BLK), jnp.int32),
            pltpu.SMEM((2, BLK), F32),
            pltpu.VMEM((hidden, SLOTS), BF16),
            pltpu.VMEM((hidden, features), BF16),
            pltpu.VMEM((TOK, CH), F32),
            pltpu.VMEM((NS, TOK), F32),
            pltpu.VMEM((NS, TOK), F32),
            pltpu.VMEM((NS, CH), F32),
            pltpu.VMEM((1, CH), F32),
            pltpu.VMEM((hidden, SLOTS), BF16),
            pltpu.VMEM((2, BLK), F32),
            pltpu.VMEM((2, X, Y, 2, HALF, FSL), BF16),
            pltpu.VMEM((X, Y, 2, HALF, FSL), BF16),
            pltpu.VMEM((4, Y, HALF, FSL), BF16),
            pltpu.VMEM((4, X, HALF, FSL), BF16),
            pltpu.VMEM((Y, HALF, FSL), BF16),
            pltpu.VMEM((X, HALF, FSL), BF16),
            pltpu.VMEM((4, HALF, FSL), BF16),
            pltpu.VMEM((4, HALF, FSL), BF16),
            pltpu.VMEM((TOK, CH), F32),
            pltpu.VMEM((TOK, CH), F32),
            pltpu.VMEM((TOK, NS, CH), F32),
            pltpu.VMEM((TOK, NS, CH), F32),
            pltpu.VMEM((TOK, NS, CH), F32),
            pltpu.VMEM((TOK, NS, CH), F32),
            pltpu.VMEM((128, 128), F32),
            pltpu.VMEM((TOK, CH), F32),
            pltpu.VMEM((CTX, 3 * NS, CH), F32),
            pltpu.VMEM((2, X, TOK, CH), BF16),
            pltpu.VMEM((4, 128, FSL), BF16),
            pltpu.VMEM((4, 4, 16, FSL), BF16),
            pltpu.VMEM((3, 4, 16, FSL), BF16),
            pltpu.VMEM((4, 16, FSL), BF16),
            pltpu.VMEM((4, 16, FSL), BF16),
            pltpu.VMEM((4, 4, 16, FSL), BF16),
            pltpu.VMEM((4, 4, 16, 128), F32),
            pltpu.VMEM((16, FSL), BF16),
            pltpu.VMEM((16, 128), F32),
            pltpu.VMEM((BLK, FSL + 128), F32),
            pltpu.VMEM((BLK, FSL + 128), F32),
            pltpu.VMEM((128, 256), BF16),
            pltpu.VMEM((1, 1, SLOTS), F32),
            pltpu.VMEM((4, 1, SLOTS), F32),
            pltpu.VMEM((2, X, Y, 2, HALF, FSL), BF16),
            pltpu.VMEM((hidden, features), BF16),
            pltpu.VMEM((4, 8, 128), F32),
            pltpu.VMEM((4, 8, 128), F32),
            pltpu.VMEM((5, 8, 128), F32),
            pltpu.VMEM((4, 8, 128), F32),
            pltpu.VMEM((4, 8, 128), F32),
            pltpu.VMEM((NS + BLK, CH), F32),
            pltpu.VMEM((CTX, NS + BLK, CH), F32),
            pltpu.VMEM((2 * X, BLK, 128), F32),
            pltpu.VMEM((Z, BLK, 128), F32),
            pltpu.SemaphoreType.DMA((NSEM,)),
            pltpu.SemaphoreType.DMA((NSEM,)),
            pltpu.SemaphoreType.DMA((40,)),
            pltpu.SemaphoreType.DMA((4,)),
        ],
        compiler_params=pltpu.CompilerParams(
            collective_id=0, has_side_effects=True, vmem_limit_bytes=VMEM_LIMIT
        ),
        name="scan_and_experts",
    )(
        mixer_input, step_sizes, decay_rates, input_proj, output_proj, skip_gain.reshape(1, CH), doc_starts, ssm_grad,
        mixer_in_weight, residual_grad, expert_index_pairs.T, route_probs.T, hidden_saved[0], down_weight[0],
    )
    ssm, stepg, inpg, outpg, decg, skipg, slot, down, probg = pl.pallas_call(
        store,
        out_shape=tuple(shape(array.shape, array.dtype) for array in out),
        in_specs=[anywhere] * 9,
        out_specs=tuple([hbm] * 9),
        scratch_shapes=[pltpu.VMEM(array.shape, array.dtype) for array in out] + [pltpu.SemaphoreType.DMA((2, 16))],
        compiler_params=pltpu.CompilerParams(vmem_limit_bytes=VMEM_LIMIT),
        name="store_results",
    )(*out)
    return ssm, stepg, inpg, outpg, decg, skipg.reshape(CH), slot[None], down[None], probg.T


def solution(mesh):
    return jax.shard_map(
        shards,
        mesh=mesh,
        in_specs=(
            P("ctx", ("exp", "tp")),
            P("ctx", ("exp", "tp")),
            P(None, ("exp", "tp")),
            P(None, "ctx"),
            P(None, "ctx"),
            P(("exp", "tp")),
            P("ctx"),
            P("ctx", ("exp", "tp")),
            P(("exp", "tp"), "ctx"),
            P(("ctx", "exp"), None),
            P(("ctx", "exp"), None),
            P(("ctx", "exp"), None),
            P("exp", ("ctx", "tp"), None),
            P("exp", ("ctx", "tp"), None),
        ),
        out_specs=(
            P("ctx", ("exp", "tp")),
            P("ctx", ("exp", "tp")),
            P(None, "ctx"),
            P(None, "ctx"),
            P(None, ("exp", "tp")),
            P(("exp", "tp")),
            P("exp", ("ctx", "tp"), None),
            P("exp", ("ctx", "tp"), None),
            P(("ctx", "exp"), None),
        ),
        check_vma=False,
    )
```
